32 devices in a mesh: bl: 8 (over y, x, core), dir: 4 (over z).
Axes of the slice: x: 2, y: 2, z: 4, core: 2. Of those that a mesh axis runs over, the one named last changes fastest.
Arguments:
- visibilities: float32 [8, 16, 2048], P(None, 'dir', 'bl'), may hold values from -24 to 24
- coherencies: bfloat16 [32, 8, 16, 2048], P('dir', None, None, 'bl'), may hold values from -6 to 6
- gain_offsets: float32 [32, 8, 512], P(None, None, 'bl'), may hold values from -1.5 to 1.5
- stations: int32 [2, 2048], P(None, 'bl'), may hold values from 0 to 511, as said below
- solve_order: int32 [32], replicated, may hold values from 0 to 31, each once
- counts: int32 [32], replicated, may hold values from 1 to 2
- damping: int32 [32], replicated, may hold values from 1 to 8
Outputs:
- gains: float32 [32, 8, 512], P(None, None, 'bl')
- residual: float32 [8, 16, 2048], P(None, 'dir', 'bl')
The draws below stay inside these ranges and needn't reach their ends.
Inputs may be any that keep to these rules, and one draw needn't show every extreme that they name: Each baseline names two different stations. `solve_order`: each direction appears once.
All inputs are finite; a program needn't handle non-finite values.
Results may differ from the reference program's by a relative error of at most 0.0003.
Values may be sent and summed in bfloat16 or wider, within the bound.
No kernel may reach another device: no remote copies, remote signals or barrier semaphores. Data moves between devices by JAX's collectives and lax.ppermute only.
A program may use at most 64 MiB of HBM per device.

```python
import jax
import jax.numpy as jnp
from jax import lax

STATION_TOTAL = 512
DIRECTION_COUNT = 32
FREQUENCY_COUNT = 16
LM_ITERS = 2
SOLVED = 4
BASELINE_TOTAL = 2048


def draw_stations(key, part):
    leading_random_key = jax.random.fold_in(key, 11)
    trailing_random_key = jax.random.fold_in(key, 12)
    leading_endpoint = jax.random.randint(leading_random_key, (BASELINE_TOTAL,), 0, STATION_TOTAL)
    gain_shifts = jax.random.randint(trailing_random_key, (BASELINE_TOTAL,), 1, STATION_TOTAL)
    return jnp.stack([leading_endpoint, (leading_endpoint + gain_shifts) % STATION_TOTAL]).astype(jnp.int32)


def draw_counts(key, part):
    chosen = jax.random.randint(jax.random.fold_in(key, 21), (DIRECTION_COUNT,), 1, LM_ITERS + 1)
    position = jax.random.randint(jax.random.fold_in(key, 22), (), 0, DIRECTION_COUNT)
    return jnp.where(jnp.arange(DIRECTION_COUNT) == position, LM_ITERS, chosen).astype(jnp.int32)


def touch_ends(values, own_key, least, high):
    spot = [jax.random.randint(jax.random.fold_in(own_key, axis), (), 0, length) for axis, length in enumerate(values.shape)]
    main_axis = values.shape.index(max(values.shape))
    neighbour = spot[:main_axis] + [(spot[main_axis] + 1) % values.shape[main_axis]] + spot[main_axis + 1:]
    return values.at[tuple(spot)].set(least).at[tuple(neighbour)].set(high)


def block_scale(rng, dims, cuts, least, top_value):
    def one(axis_at, shards_of):
        heights = jax.random.uniform(jax.random.fold_in(jax.random.fold_in(rng, 6), axis_at), (shards_of,), jnp.float32, least / len(cuts), top_value / len(cuts))
        return jnp.repeat(jnp.exp(heights), dims[axis_at] // shards_of).reshape((-1,) + (1,) * (len(dims) - axis_at - 1))

    loudness = one(*cuts[0])
    for cut in cuts[1:]:
        loudness = loudness * one(*cut)
    return loudness


def bell_draw(stream_key, dims, deviation, limit, cuts=(), dtype=jnp.bfloat16):
    array = deviation * jax.random.normal(stream_key, dims, jnp.float32)
    if cuts:
        array = array * block_scale(stream_key, dims, cuts, -0.22, 0.18)
    return jnp.clip(array, -limit, limit).astype(dtype)


def setup_inputs(seed: int = 0) -> dict:
    keys = jax.random.split(jax.random.key(seed), 8)
    return {
        "visibilities": bell_draw(keys[0], (8, FREQUENCY_COUNT, BASELINE_TOTAL), 4.0, 24.0, ((1, 4), (2, 8)), jnp.float32),
        "coherencies": bell_draw(keys[1], (DIRECTION_COUNT, 8, FREQUENCY_COUNT, BASELINE_TOTAL), 1.0, 6.0, ((0, 4), (3, 8))),
        "gain_offsets": bell_draw(keys[2], (DIRECTION_COUNT, 8, STATION_TOTAL), 0.3, 1.5, ((2, 8),), jnp.float32),
        "stations": draw_stations(jax.random.fold_in(keys[7], 71), 0),
        "solve_order": jax.random.permutation(keys[4], DIRECTION_COUNT).astype(jnp.int32),
        "counts": draw_counts(jax.random.fold_in(keys[7], 71), 0),
        "damping": touch_ends(jax.random.randint(keys[6], (DIRECTION_COUNT,), 1, 9), jax.random.fold_in(keys[6], 1), 1, 8).astype(jnp.int32),
    }


def matrix_entry(mat, i, j):
    return mat[4 * i + 2 * j], mat[4 * i + 2 * j + 1]


def matmul_two(left, right):
    pieces = []
    for i in (0, 1):
        for j in (0, 1):
            left_r0, left_i0 = matrix_entry(left, i, 0)
            left_r1, left_i1 = matrix_entry(left, i, 1)
            right_r0, right_i0 = matrix_entry(right, 0, j)
            right_r1, right_i1 = matrix_entry(right, 1, j)
            pieces.append(left_r0 * right_r0 - left_i0 * right_i0 + left_r1 * right_r1 - left_i1 * right_i1)
            pieces.append(left_r0 * right_i0 + left_i0 * right_r0 + left_r1 * right_i1 + left_i1 * right_r1)
    return jnp.stack(pieces)


def adjoint(mat):
    return jnp.stack([mat[0], -mat[1], mat[4], -mat[5], mat[2], -mat[3], mat[6], -mat[7]])


def apply_gains(gain_p, coher_now, gain_q):
    return matmul_two(matmul_two(gain_p, coher_now), adjoint(gain_q))


def gram_parts(gram):
    return jnp.stack([gram[0], gram[6], gram[2], gram[3]])


def station_terms(gain_p, gain_q, coher_now, target):
    z_rows = matmul_two(coher_now, adjoint(gain_q))
    y_rows = matmul_two(adjoint(coher_now), adjoint(gain_p))
    leading_endpoint = jnp.concatenate([matmul_two(target, adjoint(z_rows)), gram_parts(matmul_two(z_rows, adjoint(z_rows)))], 0)
    second = jnp.concatenate([matmul_two(adjoint(target), adjoint(y_rows)), gram_parts(matmul_two(y_rows, adjoint(y_rows)))], 0)
    return jnp.sum(leading_endpoint, axis=1), jnp.sum(second, axis=1)


def to_stations(leading_endpoint, second, stations, count):
    totals = jax.ops.segment_sum(leading_endpoint.T, stations[0], count) + jax.ops.segment_sum(second.T, stations[1], count)
    return totals.T


def solve_station(gathered_sums, gain_now, damp_value):
    numerator = gathered_sums[:8] + damp_value * gain_now
    diag_a = gathered_sums[8] + damp_value
    diag_d = gathered_sums[9] + damp_value
    cross_r = gathered_sums[10]
    cross_i = gathered_sums[11]
    determinant = diag_a * diag_d - cross_r * cross_r - cross_i * cross_i
    zeros_row = jnp.zeros_like(determinant)
    inverse = jnp.stack([diag_d, zeros_row, -cross_r, -cross_i, -cross_r, cross_i, diag_a, zeros_row]) / determinant
    return matmul_two(numerator, inverse)


def reference(visibilities, coherencies, gain_offsets, stations, solve_order, counts, damping):
    identity = jnp.zeros((8,), jnp.float32).at[0].set(1.0).at[6].set(1.0)
    start = gain_offsets + identity[None, :, None]
    damping_factor = BASELINE_TOTAL * FREQUENCY_COUNT / STATION_TOTAL

    def direction_model(gain_now, coher_now):
        gain_p = jnp.take(gain_now, stations[0], axis=1)[:, None, :]
        gain_q = jnp.take(gain_now, stations[1], axis=1)[:, None, :]
        return apply_gains(gain_p, coher_now, gain_q)

    def add_model(which, acc):
        return acc + direction_model(start[which], coherencies[which].astype(jnp.float32))

    first_model = lax.fori_loop(0, DIRECTION_COUNT, add_model, jnp.zeros(visibilities.shape, jnp.float32))
    first_residual = visibilities - first_model

    def sweep(step_index, state):
        gain_table, residual = state
        which = solve_order[step_index]
        coher_now = coherencies[which].astype(jnp.float32)
        damp_value = damping[which].astype(jnp.float32) * damping_factor
        gain_start = gain_table[which]
        target = residual + direction_model(gain_start, coher_now)

        def iterate(round_index, gain_now):
            gain_p = jnp.take(gain_now, stations[0], axis=1)[:, None, :]
            gain_q = jnp.take(gain_now, stations[1], axis=1)[:, None, :]
            leading_endpoint, second = station_terms(gain_p, gain_q, coher_now, target)
            gathered_sums = to_stations(leading_endpoint, second, stations, STATION_TOTAL)
            updated = solve_station(gathered_sums, gain_now, damp_value)
            return jnp.where(round_index < counts[which], updated, gain_now)

        gain_final = lax.fori_loop(0, LM_ITERS, iterate, gain_start)
        residual = target - direction_model(gain_final, coher_now)
        return gain_table.at[which].set(gain_final), residual

    gains, residual = lax.fori_loop(0, SOLVED, sweep, (start, first_residual))
    return gains, residual
```

```python
import functools

import jax
import jax.numpy as jnp
from jax import lax
from jax.experimental import pallas as pl
from jax.experimental.pallas import tpu as pltpu
from jax.sharding import PartitionSpec as P

LM_ITERS = 2
SOLVED = 4
F32 = jnp.float32
BF16 = jnp.bfloat16
VMEM_BYTES = 48 * 1024 * 1024
PAIRS = [(m, i) for i in range(SOLVED) for m in range(i)]
GRAM = [(u, v) for u in range(4) for v in range(u, 4)]
M_ROWS = 32
K_ROWS = 16
KX_ROWS = SOLVED * K_ROWS + len(PAIRS) * M_ROWS + 8
ALL_ROWS = SOLVED * M_ROWS + KX_ROWS
STATION_ROW = ALL_ROWS - 8


def mul(x, y):
    return (x[0] * y[0] - x[1] * y[1], x[0] * y[1] + x[1] * y[0])


def add(x, y):
    return (x[0] + y[0], x[1] + y[1])


def sub(x, y):
    return (x[0] - y[0], x[1] - y[1])


def conj(x):
    return (x[0], -x[1])


def total(terms):
    return functools.reduce(add, terms)


def mul_conj(x, y):
    return (x[0] * y[0] + x[1] * y[1], x[1] * y[0] - x[0] * y[1])


def matmul(left, right):
    return [add(mul(left[2 * i], right[j]), mul(left[2 * i + 1], right[2 + j])) for i in (0, 1) for j in (0, 1)]


def matmul_adj(left, right):
    return [
        add(mul_conj(left[2 * i], right[2 * j]), mul_conj(left[2 * i + 1], right[2 * j + 1]))
        for i in (0, 1)
        for j in (0, 1)
    ]


def apply_gains(gain_p, coher, gain_q):
    return matmul_adj(matmul(gain_p, coher), gain_q)


def as_matrix(parts):
    return [(parts[2 * e], parts[2 * e + 1]) for e in range(4)]


def split_rows(values):
    high = values.astype(BF16)
    low = (values - high.astype(F32)).astype(BF16)
    return jnp.concatenate([high, low], axis=0)


def one_hot(stations_p, stations_q, count):
    both = jnp.concatenate([stations_p, stations_q], axis=1)
    rows = lax.broadcasted_iota(jnp.int32, (count, both.shape[1]), 0)
    return jnp.where(rows == both, 1.0, 0.0).astype(BF16)


def pick(one_hots, values):
    count = values.shape[0]
    out = jnp.dot(split_rows(values), one_hots, preferred_element_type=F32)
    return out[:count] + out[count:]


def prep_kernel(place_ref, offs_ref, out_ref, *, owned, per):
    width = offs_ref.shape[2]
    part_rows = out_ref.shape[0]
    comp = lax.broadcasted_iota(jnp.int32, (8, width), 0)
    ident = jnp.where((comp == 0) | (comp == 6), 1.0, 0.0)
    blocks = [offs_ref[place_ref[d]] + ident for d in range(owned + SOLVED)]
    while len(blocks) * 8 < part_rows * per:
        blocks.append(jnp.zeros((8, width), F32))
    each = part_rows // 8
    columns = [jnp.concatenate(blocks[q * each : (q + 1) * each], axis=0) for q in range(per)]
    out_ref[...] = jnp.concatenate(columns, axis=1)


def model_kernel(
    base_ref, flag_ref, blocks_ref, stations_ref, coher_ref, solved_ref, vis_ref, part_ref, m_ref, kx_ref, start_ref, table, ends,
    *, width
):
    owned = coher_ref.shape[0]
    baselines = coher_ref.shape[3]
    groups, part_rows, lanes = blocks_ref.shape
    per = lanes // width
    count = groups * width
    lane_of = lax.broadcasted_iota(jnp.int32, (part_rows, lanes), 1) // width
    for tile in range(count // lanes):
        for q in range(per):
            tile_rows = jnp.zeros((part_rows, lanes), F32)
            for u in range(per):
                block = blocks_ref[per * tile + u]
                shift = ((u - q) * width) % lanes
                if shift:
                    block = pltpu.roll(block, shift, 1)
                tile_rows = jnp.where(lane_of == u, block, tile_rows)
            table[q * part_rows : (q + 1) * part_rows, tile * lanes : (tile + 1) * lanes] = tile_rows
    start_ref[...] = table[owned * 8 : (owned + SOLVED) * 8, :]
    local = stations_ref[...] ^ base_ref[0]
    ends[...] = pick(one_hot(local[0:1], local[1:2], count), table[...])
    for half in range(baselines // 128):
        kx_ref[half, KX_ROWS - 8 : KX_ROWS, :] = jnp.zeros((8, 128), F32)
        kx_ref[half, KX_ROWS - 8 : KX_ROWS - 6, :] = stations_ref[:, half * 128 : half * 128 + 128].astype(F32)

    def summed(values):
        return jnp.sum(values, axis=0, keepdims=True)

    for half in range(baselines // 128):
        at = pl.ds(half * 128, 128)
        at_q = pl.ds(baselines + half * 128, 128)

        def gain(row, where):
            block = ends[pl.ds(pl.multiple_of(row, 8), 8), where]
            return as_matrix([block[c : c + 1] for c in range(8)])

        def add_model(d, acc):
            coher = as_matrix([coher_ref[d, c, :, at].astype(F32) for c in range(8)])
            model = apply_gains(gain(d * 8, at), coher, gain(d * 8, at_q))
            return [sub(x, y) for x, y in zip(acc, model)]

        acc = as_matrix([vis_ref[c, :, at] for c in range(8)])
        acc = lax.fori_loop(0, owned, add_model, acc)
        for e in range(4):
            part_ref[2 * e, :, at] = acc[e][0]
            part_ref[2 * e + 1, :, at] = acc[e][1]
        for i in range(SOLVED):
            coher = as_matrix([solved_ref[i, c, :, at].astype(F32) for c in range(8)])
            row = (owned + i) * 8
            model = apply_gains(gain(row, at), coher, gain(row, at_q))
            flag = flag_ref[i]
            target = [
                (part_ref[2 * e, :, at] + flag * model[e][0], part_ref[2 * e + 1, :, at] + flag * model[e][1])
                for e in range(4)
            ]
            for u in range(4):
                for v in range(4):
                    value = mul_conj(target[u], coher[v])
                    out = i * M_ROWS + (u * 4 + v) * 2
                    m_ref[half, out : out + 1, :] = summed(value[0])
                    m_ref[half, out + 1 : out + 2, :] = summed(value[1])
            out = i * K_ROWS
            for u, v in GRAM:
                value = mul_conj(coher[u], coher[v])
                kx_ref[half, out : out + 1, :] = summed(value[0])
                out += 1
                if u != v:
                    kx_ref[half, out : out + 1, :] = summed(value[1])
                    out += 1
            for m in range(i):
                other = as_matrix([solved_ref[m, c, :, at].astype(F32) for c in range(8)])
                out = SOLVED * K_ROWS + PAIRS.index((m, i)) * M_ROWS
                for u in range(4):
                    for v in range(4):
                        value = mul_conj(other[u], coher[v])
                        kx_ref[half, out : out + 1, :] = summed(value[0])
                        kx_ref[half, out + 1 : out + 2, :] = summed(value[1])
                        out += 2


def sweep_kernel(
    base_ref, which_ref, rounds_ref, damp_ref, sums_ref, start_ref, offs_ref, first_ref, own_ref, gains_ref, out_ref,
    hots, ends, values, state, m_now, k_now, moved,
    *, groups
):
    count = start_ref.shape[1]
    baselines = first_ref.shape[2]
    width = offs_ref.shape[2]
    stride = ALL_ROWS
    tiles = baselines // 128
    chunks = groups * tiles

    comp = lax.broadcasted_iota(jnp.int32, (8, width), 0)
    gains_ref[...] = offs_ref[...] + jnp.where((comp == 0) | (comp == 6), 1.0, 0.0)[None]
    values[...] = jnp.zeros(values.shape, F32)
    for g in range(groups):
        starts = [(g * tiles + t) * stride + STATION_ROW for t in range(tiles)]
        rows = jnp.concatenate([sums_ref[at : at + 8, :] for at in starts], axis=1).astype(jnp.int32) ^ base_ref[0]
        hots[g] = one_hot(rows[0:1], rows[1:2], count)

    def rows_at(row):
        return sums_ref[pl.ds(row, chunks, stride=stride), :]

    def fetch(gain_now, slot):
        split = split_rows(gain_now)
        for g in range(groups):
            out = jnp.dot(split, hots[g], preferred_element_type=F32)
            out = out[:8] + out[8:]
            for end in (0, 1):
                for t in range(tiles):
                    chunk, column = (g * tiles + t) * 8, (end * tiles + t) * 128
                    ends[slot, end, chunk : chunk + 8, :] = out[:, column : column + 128]

    def gain_at(slot):
        return [as_matrix([ends[slot, end, pl.ds(c, chunks, stride=8), :] for c in range(8)]) for end in (0, 1)]

    def load_m():
        return [[(m_now[(u * 4 + v) * 2], m_now[(u * 4 + v) * 2 + 1]) for v in range(4)] for u in range(4)]

    def load_k():
        row = 0
        gram = {}
        for u, v in GRAM:
            if u == v:
                gram[u, v] = (k_now[row], None)
                row += 1
            else:
                gram[u, v] = (k_now[row], k_now[row + 1])
                gram[v, u] = conj(gram[u, v])
                row += 2
        return gram

    def prepare(i):
        for row in range(K_ROWS):
            k_now[row] = rows_at(SOLVED * M_ROWS + i * K_ROWS + row)
        for out in range(4):
            for w in range(4):
                row = (out * 4 + w) * 2
                value = (rows_at(i * M_ROWS + row), rows_at(i * M_ROWS + row + 1))
                for m in range(i):
                    base = SOLVED * M_ROWS + SOLVED * K_ROWS + PAIRS.index((m, i)) * M_ROWS
                    for uv in range(4):
                        delta = (moved[m, (out * 4 + uv) * 2], moved[m, (out * 4 + uv) * 2 + 1])
                        at = base + (uv * 4 + w) * 2
                        value = add(value, mul(delta, (rows_at(at), rows_at(at + 1))))
                m_now[row] = value[0]
                m_now[row + 1] = value[1]

    def hermitian(gain):
        a = gain[0][0] ** 2 + gain[0][1] ** 2 + gain[2][0] ** 2 + gain[2][1] ** 2
        d = gain[1][0] ** 2 + gain[1][1] ** 2 + gain[3][0] ** 2 + gain[3][1] ** 2
        cross = add(mul_conj(gain[1], gain[0]), mul_conj(gain[3], gain[2]))
        return a, d, cross

    def normal_terms(slot):
        gain_p, gain_q = gain_at(slot)
        m = load_m()
        k = load_k()
        for end, gain, other in ((0, gain_q, False), (1, gain_p, True)):
            row = 0
            for r in (0, 1):
                for c in (0, 1):
                    if other:
                        terms = [mul_conj(gain[2 * a + b], m[2 * a + r][2 * b + c]) for a in (0, 1) for b in (0, 1)]
                    else:
                        terms = [mul(gain[2 * a + b], m[2 * r + a][2 * c + b]) for a in (0, 1) for b in (0, 1)]
                    value = total(terms)
                    values[end, pl.ds(row, chunks, stride=16), :] = value[0]
                    values[end, pl.ds(row + 1, chunks, stride=16), :] = value[1]
                    row += 2
            a, d, cross = hermitian(gain)
            for r, c in ((0, 0), (1, 1), (0, 1)):
                if other:
                    kk = [[k[2 * x + r, 2 * y + c] for y in (0, 1)] for x in (0, 1)]
                    kk = [[(z[0], None if z[1] is None else -z[1]) for z in line] for line in kk]
                else:
                    kk = [[k[2 * r + x, 2 * c + y] for y in (0, 1)] for x in (0, 1)]
                real = a * kk[0][0][0] + d * kk[1][1][0]
                real += cross[0] * (kk[0][1][0] + kk[1][0][0])
                minus = None
                if kk[0][1][1] is not None:
                    minus = kk[1][0][1] - kk[0][1][1]
                    real += cross[1] * minus
                values[end, pl.ds(row, chunks, stride=16), :] = real
                row += 1
                if r != c:
                    imag = cross[1] * (kk[0][1][0] - kk[1][0][0])
                    if kk[0][0][1] is not None:
                        imag += a * kk[0][0][1]
                    if kk[1][1][1] is not None:
                        imag += d * kk[1][1][1]
                    if kk[0][1][1] is not None:
                        imag += cross[0] * kk[0][1][1]
                    if kk[1][0][1] is not None:
                        imag += cross[0] * kk[1][0][1]
                    values[end, pl.ds(row, chunks, stride=16), :] = imag
                    row += 1

    def station_sums():
        acc = jnp.zeros((32, count), F32)
        for g in range(groups):
            starts = [(end, (g * tiles + t) * 16) for end in (0, 1) for t in range(tiles)]
            split = split_rows(jnp.concatenate([values[end, at : at + 16, :] for end, at in starts], axis=1))
            acc += lax.dot_general(split, hots[g], (((1,), (1,)), ((), ())), preferred_element_type=F32)
        return acc[:16] + acc[16:]

    def solve(sums, gain_now, damp):
        numer = sums[:8] + damp * gain_now
        numer = as_matrix([numer[c : c + 1] for c in range(8)])
        diag_a = sums[8:9] + damp
        diag_d = sums[9:10] + damp
        cross_r = sums[10:11]
        cross_i = sums[11:12]
        scale = 1.0 / (diag_a * diag_d - cross_r * cross_r - cross_i * cross_i)
        rows = []
        for r in (0, 1):
            x, y = numer[2 * r], numer[2 * r + 1]
            low = mul(y, (cross_r, -cross_i))
            high = mul(x, (cross_r, cross_i))
            rows += [x[0] * diag_d - low[0], x[1] * diag_d - low[1]]
            rows += [y[0] * diag_a - high[0], y[1] * diag_a - high[1]]
        return jnp.concatenate([value * scale for value in rows], axis=0)

    out_ref[...] = first_ref[...]
    for i in range(SOLVED):
        begin = start_ref[i * 8 : i * 8 + 8, :]
        damp = damp_ref[i]
        state[...] = begin
        fetch(begin, 0)
        prepare(i)

        def round_body(r, slot):
            normal_terms(slot)
            updated = solve(station_sums(), state[...], damp)
            state[...] = updated
            fetch(updated, 1)
            return jnp.int32(1)

        lax.fori_loop(0, rounds_ref[i], round_body, jnp.int32(0))
        gains_ref[which_ref[i]] = state[:, :width]

        for tile in range(tiles):
            at = pl.ds(tile * 128, 128)
            coher = as_matrix([own_ref[i, c, :, at].astype(F32) for c in range(8)])
            own = [
                [as_matrix([ends[slot, end, tile * 8 + c : tile * 8 + c + 1, :] for c in range(8)]) for end in (0, 1)]
                for slot in (0, 1)
            ]
            before = apply_gains(own[0][0], coher, own[0][1])
            after = apply_gains(own[1][0], coher, own[1][1])
            for e in range(4):
                change = sub(before[e], after[e])
                out_ref[2 * e, :, at] += change[0]
                out_ref[2 * e + 1, :, at] += change[1]
        if i + 1 == SOLVED:
            break
        p0, q0 = gain_at(0)
        p1, q1 = gain_at(1)
        for a in (0, 1):
            for b in (0, 1):
                for u in (0, 1):
                    for v in (0, 1):
                        delta = sub(mul_conj(p0[2 * a + u], q0[2 * b + v]), mul_conj(p1[2 * a + u], q1[2 * b + v]))
                        row = ((2 * a + b) * 4 + 2 * u + v) * 2
                        moved[i, row] = delta[0]
                        moved[i, row + 1] = delta[1]


def vmem():
    return pl.BlockSpec(memory_space=pltpu.VMEM)


def smem():
    return pl.BlockSpec(memory_space=pltpu.SMEM)


def exchange(block, axis, mask):
    return lax.ppermute(block, axis, [(i, i ^ mask) for i in range(lax.axis_size(axis))])


def butterfly_sum(value, axis):
    mask = 1
    while mask < lax.axis_size(axis):
        value = value + exchange(value, axis, mask)
        mask *= 2
    return value


def gather_blocks(block, axis):
    parts = block[None]
    size = lax.axis_size(axis)
    masks = [1 << s for s in range(size.bit_length() - 1)]
    for mask in masks[1:]:
        parts = jnp.concatenate([parts, exchange(parts, axis, mask)], axis=0)
    parts = jnp.stack([parts, exchange(parts, axis, masks[0])], axis=1)
    return parts.reshape((size,) + block.shape)


def on_device(visibilities, coherencies, gain_offsets, stations, solve_order, counts, damping):
    groups = lax.axis_size("bl")
    lane, own = lax.axis_index("dir"), lax.axis_index("bl")
    owned, _, channel_count, baselines = coherencies.shape
    channels = visibilities.shape[1]
    width = gain_offsets.shape[2]
    count = groups * width
    solved = solve_order[:SOLVED]
    rounds = jnp.minimum(counts[solved], LM_ITERS)
    damp = damping[solved].astype(F32) * (baselines * groups * channel_count / count)
    mine = (solved // owned) == lane
    base = (own * width).astype(jnp.int32)[None]

    per = 128 // width
    part_rows = -(-(owned + SOLVED) // per) * 8
    places = jnp.concatenate([lane * owned + jnp.arange(owned, dtype=jnp.int32), solved])
    params = pltpu.CompilerParams(vmem_limit_bytes=VMEM_BYTES)
    packed = pl.pallas_call(
        functools.partial(prep_kernel, owned=owned, per=per),
        out_shape=jax.ShapeDtypeStruct((part_rows, 128), F32),
        in_specs=[smem(), vmem()],
        out_specs=vmem(),
        compiler_params=params,
        name="pack_gains",
    )(places, gain_offsets)
    blocks = gather_blocks(packed, "bl")

    chosen = jnp.stack(
        [
            jnp.where(mine[i], lax.dynamic_index_in_dim(coherencies, solved[i] % owned, 0, keepdims=False), 0)
            for i in range(SOLVED)
        ]
    ).astype(BF16)
    shared = butterfly_sum(chosen, "dir")
    own_channels = lax.dynamic_slice_in_dim(shared, lane * channels, channels, 2)
    vis = lax.dynamic_update_slice_in_dim(
        jnp.zeros((8, channel_count, baselines), F32), visibilities, lane * channels, 1
    )

    part, m_part, kx, start = pl.pallas_call(
        functools.partial(model_kernel, width=width),
        out_shape=(
            jax.ShapeDtypeStruct((8, channel_count, baselines), F32),
            jax.ShapeDtypeStruct((baselines // 128, SOLVED * M_ROWS, 128), F32),
            jax.ShapeDtypeStruct((baselines // 128, KX_ROWS, 128), F32),
            jax.ShapeDtypeStruct((SOLVED * 8, count), F32),
        ),
        in_specs=[smem()] * 2 + [vmem()] * 5,
        out_specs=(vmem(),) * 4,
        scratch_shapes=[pltpu.VMEM((part_rows * per, count), F32), pltpu.VMEM((part_rows * per, 2 * baselines), F32)],
        compiler_params=params,
        name="first_model",
    )(base, mine.astype(F32), blocks, stations, coherencies, shared, vis)

    first = lax.psum_scatter(part, "dir", scatter_dimension=1, tiled=True)
    sums = jnp.concatenate([butterfly_sum(m_part, "dir"), kx], axis=1)
    everything = gather_blocks(sums, "bl").reshape(-1, 128)

    gains, residual = pl.pallas_call(
        functools.partial(sweep_kernel, groups=groups),
        out_shape=(
            jax.ShapeDtypeStruct(gain_offsets.shape, F32),
            jax.ShapeDtypeStruct(visibilities.shape, F32),
        ),
        in_specs=[smem()] * 4 + [vmem()] * 5,
        out_specs=(vmem(), vmem()),
        scratch_shapes=[
            pltpu.VMEM((groups, count, 2 * baselines), BF16),
            pltpu.VMEM((2, 2, groups * baselines // 16, 128), F32),
            pltpu.VMEM((2, groups * baselines // 8, 128), F32),
            pltpu.VMEM((8, count), F32),
            pltpu.VMEM((M_ROWS, groups * baselines // 128, 128), F32),
            pltpu.VMEM((K_ROWS, groups * baselines // 128, 128), F32),
            pltpu.VMEM((SOLVED - 1, M_ROWS, groups * baselines // 128, 128), F32),
        ],
        compiler_params=params,
        name="sweep",
    )(base, solved, rounds, damp, everything, start, gain_offsets, first, own_channels)
    return gains, residual


def solution(mesh):
    return jax.shard_map(
        on_device,
        mesh=mesh,
        in_specs=(
            P(None, "dir", "bl"),
            P("dir", None, None, "bl"),
            P(None, None, "bl"),
            P(None, "bl"),
            P(),
            P(),
            P(),
        ),
        out_specs=(P(None, None, "bl"), P(None, "dir", "bl")),
        check_vma=False,
    )
```

```python
import functools

import jax
import jax.numpy as jnp
from jax import lax
from jax.experimental import pallas as pl
from jax.experimental.pallas import tpu as pltpu
from jax.sharding import PartitionSpec as P

LM_ITERS = 2
SOLVED = 4
F32 = jnp.float32
BF16 = jnp.bfloat16
VMEM_BYTES = 48 * 1024 * 1024
PAIRS = [(m, i) for i in range(SOLVED) for m in range(i)]
GRAM = [(u, v) for u in range(4) for v in range(u, 4)]
M_ROWS = 32
K_ROWS = 16
X_START = SOLVED * K_ROWS
STATION_ROW = X_START + len(PAIRS) * M_ROWS
KX_ROWS = STATION_ROW + 8


def mul(x, y):
    return (x[0] * y[0] - x[1] * y[1], x[0] * y[1] + x[1] * y[0])


def add(x, y):
    return (x[0] + y[0], x[1] + y[1])


def sub(x, y):
    return (x[0] - y[0], x[1] - y[1])


def conj(x):
    return (x[0], -x[1])


def total(terms):
    return functools.reduce(add, terms)


def mul_conj(x, y):
    return (x[0] * y[0] + x[1] * y[1], x[1] * y[0] - x[0] * y[1])


def matmul(left, right):
    return [add(mul(left[2 * i], right[j]), mul(left[2 * i + 1], right[2 + j])) for i in (0, 1) for j in (0, 1)]


def matmul_adj(left, right):
    return [
        add(mul_conj(left[2 * i], right[2 * j]), mul_conj(left[2 * i + 1], right[2 * j + 1]))
        for i in (0, 1)
        for j in (0, 1)
    ]


def apply_gains(gain_p, coher, gain_q):
    return matmul_adj(matmul(gain_p, coher), gain_q)


def as_matrix(parts):
    return [(parts[2 * e], parts[2 * e + 1]) for e in range(4)]


def split_rows(values):
    high = values.astype(BF16)
    low = (values - high.astype(F32)).astype(BF16)
    return jnp.concatenate([high, low], axis=0)


def one_hot(stations_p, stations_q, count):
    both = jnp.concatenate([stations_p, stations_q], axis=1)
    rows = lax.broadcasted_iota(jnp.int32, (count, both.shape[1]), 0)
    return jnp.where(rows == both, 1.0, 0.0).astype(BF16)


def pick(one_hots, values):
    count = values.shape[0]
    out = jnp.dot(split_rows(values), one_hots, preferred_element_type=F32)
    return out[:count] + out[count:]


def prep_kernel(place_ref, offs_ref, out_ref, *, owned, per):
    width = offs_ref.shape[2]
    part_rows = out_ref.shape[0]
    comp = lax.broadcasted_iota(jnp.int32, (8, width), 0)
    ident = jnp.where((comp == 0) | (comp == 6), 1.0, 0.0)
    blocks = [offs_ref[place_ref[d]] + ident for d in range(owned + SOLVED)]
    while len(blocks) * 8 < part_rows * per:
        blocks.append(jnp.zeros((8, width), F32))
    each = part_rows // 8
    columns = [jnp.concatenate(blocks[q * each : (q + 1) * each], axis=0) for q in range(per)]
    out_ref[...] = jnp.concatenate(columns, axis=1)


def select_kernel(places_ref, mine_ref, *refs):
    out_ref = refs[-1]
    for i in range(SOLVED):
        out_ref[i] = jnp.where(mine_ref[i] == 1, refs[i][0], jnp.zeros_like(refs[i][0]))


def model_kernel(base_ref, blocks_ref, stations_ref, coher_ref, vis_ref, part_ref, start_ref, begin_ref, table, ends, *, width):
    owned = coher_ref.shape[0]
    baselines = coher_ref.shape[3]
    groups, part_rows, lanes = blocks_ref.shape
    per = lanes // width
    count = groups * width
    lane_of = lax.broadcasted_iota(jnp.int32, (part_rows, lanes), 1) // width
    for tile in range(count // lanes):
        for q in range(per):
            tile_rows = jnp.zeros((part_rows, lanes), F32)
            for u in range(per):
                block = blocks_ref[per * tile + u]
                shift = ((u - q) * width) % lanes
                if shift:
                    block = pltpu.roll(block, shift, 1)
                tile_rows = jnp.where(lane_of == u, block, tile_rows)
            table[q * part_rows : (q + 1) * part_rows, tile * lanes : (tile + 1) * lanes] = tile_rows
    start_ref[...] = table[owned * 8 : (owned + SOLVED) * 8, :]
    local = stations_ref[...] ^ base_ref[0]
    ends[...] = pick(one_hot(local[0:1], local[1:2], count), table[...])
    begin_ref[...] = ends[owned * 8 : (owned + SOLVED) * 8, :]

    for half in range(baselines // 128):
        at = pl.ds(half * 128, 128)
        at_q = pl.ds(baselines + half * 128, 128)

        def gain(row, where):
            block = ends[pl.ds(pl.multiple_of(row, 8), 8), where]
            return as_matrix([block[c : c + 1] for c in range(8)])

        def add_model(d, acc):
            coher = as_matrix([coher_ref[d, c, :, at].astype(F32) for c in range(8)])
            model = apply_gains(gain(d * 8, at), coher, gain(d * 8, at_q))
            return [sub(x, y) for x, y in zip(acc, model)]

        acc = as_matrix([vis_ref[c, :, at] for c in range(8)])
        acc = lax.fori_loop(0, owned, add_model, acc)
        for e in range(4):
            part_ref[2 * e, :, at] = acc[e][0]
            part_ref[2 * e + 1, :, at] = acc[e][1]


def summed(values):
    return jnp.sum(values, axis=0, keepdims=True)


def target_kernel(mine_ref, part_ref, solved_ref, begin_ref, m_ref):
    baselines = part_ref.shape[2]
    for half in range(baselines // 128):
        at = pl.ds(half * 128, 128)
        for i in range(SOLVED):
            coher = as_matrix([solved_ref[i, c, :, at].astype(F32) for c in range(8)])
            gain_p, gain_q = [
                as_matrix([begin_ref[i * 8 + c : i * 8 + c + 1, pl.ds(end * baselines + half * 128, 128)] for c in range(8)])
                for end in (0, 1)
            ]
            model = apply_gains(gain_p, coher, gain_q)
            flag = mine_ref[i].astype(F32)
            target = [
                (part_ref[2 * e, :, at] + flag * model[e][0], part_ref[2 * e + 1, :, at] + flag * model[e][1])
                for e in range(4)
            ]
            out = i * M_ROWS
            for u in range(4):
                for v in range(4):
                    value = mul_conj(target[u], coher[v])
                    m_ref[half, out : out + 1, :] = summed(value[0])
                    m_ref[half, out + 1 : out + 2, :] = summed(value[1])
                    out += 2


def product_kernel(lane_ref, stations_ref, solved_ref, kx_ref, own_ref):
    baselines = solved_ref.shape[3]
    channels = own_ref.shape[2]
    for half in range(baselines // 128):
        at = pl.ds(half * 128, 128)
        kx_ref[half, STATION_ROW:KX_ROWS, :] = jnp.zeros((KX_ROWS - STATION_ROW, 128), F32)
        kx_ref[half, STATION_ROW : STATION_ROW + 2, :] = stations_ref[:, at].astype(F32)
        for i in range(SOLVED):
            parts = [solved_ref[i, c, :, at].astype(F32) for c in range(8)]
            for c in range(8):
                mine = parts[c][:channels]
                for lane in range(1, parts[c].shape[0] // channels):
                    mine = jnp.where(lane_ref[0] == lane, parts[c][lane * channels : (lane + 1) * channels], mine)
                own_ref[i, c, :, at] = mine
            coher = as_matrix(parts)
            out = i * K_ROWS
            for u, v in GRAM:
                value = mul_conj(coher[u], coher[v])
                kx_ref[half, out : out + 1, :] = summed(value[0])
                out += 1
                if u != v:
                    kx_ref[half, out : out + 1, :] = summed(value[1])
                    out += 1
            for m in range(i):
                other = as_matrix([solved_ref[m, c, :, at].astype(F32) for c in range(8)])
                out = X_START + PAIRS.index((m, i)) * M_ROWS
                for u in range(4):
                    for v in range(4):
                        value = mul_conj(other[u], coher[v])
                        kx_ref[half, out : out + 1, :] = summed(value[0])
                        kx_ref[half, out + 1 : out + 2, :] = summed(value[1])
                        out += 2


def sweep_kernel(
    base_ref, order_ref, counts_ref, damping_ref, m0_ref, m1_ref, kx0_ref, kx1_ref, start_ref, offs_ref, first_ref,
    own_ref, gains_ref, out_ref, hots, ends, values, state, m_now, k_now, moved,
    *, groups, factor
):
    count = start_ref.shape[1]
    baselines = first_ref.shape[2]
    width = offs_ref.shape[2]
    tiles = baselines // 128
    chunks = groups * tiles

    comp = lax.broadcasted_iota(jnp.int32, (8, width), 0)
    gains_ref[...] = offs_ref[...] + jnp.where((comp == 0) | (comp == 6), 1.0, 0.0)[None]
    values[...] = jnp.zeros(values.shape, F32)
    for g in range(groups):
        kx_ref, first = (kx0_ref, 0) if g < groups // 2 else (kx1_ref, groups // 2)
        starts = [((g - first) * tiles + t) * KX_ROWS + STATION_ROW for t in range(tiles)]
        rows = jnp.concatenate([kx_ref[at : at + 8, :] for at in starts], axis=1).astype(jnp.int32) ^ base_ref[0]
        hots[g] = one_hot(rows[0:1], rows[1:2], count)

    def m_at(row):
        return jnp.concatenate([ref[pl.ds(row, chunks // 2, stride=SOLVED * M_ROWS), :] for ref in (m0_ref, m1_ref)], axis=0)

    def kx_at(row):
        return jnp.concatenate([ref[pl.ds(row, chunks // 2, stride=KX_ROWS), :] for ref in (kx0_ref, kx1_ref)], axis=0)

    def fetch(gain_now, slot):
        split = split_rows(gain_now)
        for g in range(groups):
            out = jnp.dot(split, hots[g], preferred_element_type=F32)
            out = out[:8] + out[8:]
            for end in (0, 1):
                for t in range(tiles):
                    chunk, column = (g * tiles + t) * 8, (end * tiles + t) * 128
                    ends[slot, end, chunk : chunk + 8, :] = out[:, column : column + 128]

    def gain_at(slot):
        return [as_matrix([ends[slot, end, pl.ds(c, chunks, stride=8), :] for c in range(8)]) for end in (0, 1)]

    def load_m():
        return [[(m_now[(u * 4 + v) * 2], m_now[(u * 4 + v) * 2 + 1]) for v in range(4)] for u in range(4)]

    def load_k():
        row = 0
        gram = {}
        for u, v in GRAM:
            if u == v:
                gram[u, v] = (k_now[row], None)
                row += 1
            else:
                gram[u, v] = (k_now[row], k_now[row + 1])
                gram[v, u] = conj(gram[u, v])
                row += 2
        return gram

    def prepare(i):
        for row in range(K_ROWS):
            k_now[row] = kx_at(i * K_ROWS + row)
        for out in range(4):
            for w in range(4):
                row = (out * 4 + w) * 2
                value = (m_at(i * M_ROWS + row), m_at(i * M_ROWS + row + 1))
                for m in range(i):
                    base = X_START + PAIRS.index((m, i)) * M_ROWS
                    for uv in range(4):
                        delta = (moved[m, (out * 4 + uv) * 2], moved[m, (out * 4 + uv) * 2 + 1])
                        at = base + (uv * 4 + w) * 2
                        value = add(value, mul(delta, (kx_at(at), kx_at(at + 1))))
                m_now[row] = value[0]
                m_now[row + 1] = value[1]

    def hermitian(gain):
        a = gain[0][0] ** 2 + gain[0][1] ** 2 + gain[2][0] ** 2 + gain[2][1] ** 2
        d = gain[1][0] ** 2 + gain[1][1] ** 2 + gain[3][0] ** 2 + gain[3][1] ** 2
        cross = add(mul_conj(gain[1], gain[0]), mul_conj(gain[3], gain[2]))
        return a, d, cross

    def normal_terms(slot):
        gain_p, gain_q = gain_at(slot)
        m = load_m()
        k = load_k()
        for end, gain, other in ((0, gain_q, False), (1, gain_p, True)):
            row = 0
            for r in (0, 1):
                for c in (0, 1):
                    if other:
                        terms = [mul_conj(gain[2 * a + b], m[2 * a + r][2 * b + c]) for a in (0, 1) for b in (0, 1)]
                    else:
                        terms = [mul(gain[2 * a + b], m[2 * r + a][2 * c + b]) for a in (0, 1) for b in (0, 1)]
                    value = total(terms)
                    values[end, pl.ds(row, chunks, stride=16), :] = value[0]
                    values[end, pl.ds(row + 1, chunks, stride=16), :] = value[1]
                    row += 2
            a, d, cross = hermitian(gain)
            for r, c in ((0, 0), (1, 1), (0, 1)):
                if other:
                    kk = [[k[2 * x + r, 2 * y + c] for y in (0, 1)] for x in (0, 1)]
                    kk = [[(z[0], None if z[1] is None else -z[1]) for z in line] for line in kk]
                else:
                    kk = [[k[2 * r + x, 2 * c + y] for y in (0, 1)] for x in (0, 1)]
                real = a * kk[0][0][0] + d * kk[1][1][0]
                real += cross[0] * (kk[0][1][0] + kk[1][0][0])
                minus = None
                if kk[0][1][1] is not None:
                    minus = kk[1][0][1] - kk[0][1][1]
                    real += cross[1] * minus
                values[end, pl.ds(row, chunks, stride=16), :] = real
                row += 1
                if r != c:
                    imag = cross[1] * (kk[0][1][0] - kk[1][0][0])
                    if kk[0][0][1] is not None:
                        imag += a * kk[0][0][1]
                    if kk[1][1][1] is not None:
                        imag += d * kk[1][1][1]
                    if kk[0][1][1] is not None:
                        imag += cross[0] * kk[0][1][1]
                    if kk[1][0][1] is not None:
                        imag += cross[0] * kk[1][0][1]
                    values[end, pl.ds(row, chunks, stride=16), :] = imag
                    row += 1

    def station_sums():
        acc = jnp.zeros((32, count), F32)
        for g in range(groups):
            starts = [(end, (g * tiles + t) * 16) for end in (0, 1) for t in range(tiles)]
            split = split_rows(jnp.concatenate([values[end, at : at + 16, :] for end, at in starts], axis=1))
            acc += lax.dot_general(split, hots[g], (((1,), (1,)), ((), ())), preferred_element_type=F32)
        return acc[:16] + acc[16:]

    def solve(sums, gain_now, damp):
        numer = sums[:8] + damp * gain_now
        numer = as_matrix([numer[c : c + 1] for c in range(8)])
        diag_a = sums[8:9] + damp
        diag_d = sums[9:10] + damp
        cross_r = sums[10:11]
        cross_i = sums[11:12]
        scale = 1.0 / (diag_a * diag_d - cross_r * cross_r - cross_i * cross_i)
        rows = []
        for r in (0, 1):
            x, y = numer[2 * r], numer[2 * r + 1]
            low = mul(y, (cross_r, -cross_i))
            high = mul(x, (cross_r, cross_i))
            rows += [x[0] * diag_d - low[0], x[1] * diag_d - low[1]]
            rows += [y[0] * diag_a - high[0], y[1] * diag_a - high[1]]
        return jnp.concatenate([value * scale for value in rows], axis=0)

    out_ref[...] = first_ref[...]
    for i in range(SOLVED):
        begin = start_ref[i * 8 : i * 8 + 8, :]
        which = order_ref[i]
        damp = damping_ref[which].astype(F32) * factor
        state[...] = begin
        fetch(begin, 0)
        prepare(i)

        def round_body(r, slot):
            normal_terms(slot)
            updated = solve(station_sums(), state[...], damp)
            state[...] = updated
            fetch(updated, 1)
            return jnp.int32(1)

        lax.fori_loop(0, jnp.minimum(counts_ref[which], LM_ITERS), round_body, jnp.int32(0))
        gains_ref[which] = state[:, :width]

        for tile in range(tiles):
            at = pl.ds(tile * 128, 128)
            coher = as_matrix([own_ref[i, c, :, at] for c in range(8)])
            own = [
                [as_matrix([ends[slot, end, tile * 8 + c : tile * 8 + c + 1, :] for c in range(8)]) for end in (0, 1)]
                for slot in (0, 1)
            ]
            before = apply_gains(own[0][0], coher, own[0][1])
            after = apply_gains(own[1][0], coher, own[1][1])
            for e in range(4):
                change = sub(before[e], after[e])
                out_ref[2 * e, :, at] += change[0]
                out_ref[2 * e + 1, :, at] += change[1]
        if i + 1 == SOLVED:
            break
        p0, q0 = gain_at(0)
        p1, q1 = gain_at(1)
        for a in (0, 1):
            for b in (0, 1):
                for u in (0, 1):
                    for v in (0, 1):
                        delta = sub(mul_conj(p0[2 * a + u], q0[2 * b + v]), mul_conj(p1[2 * a + u], q1[2 * b + v]))
                        row = ((2 * a + b) * 4 + 2 * u + v) * 2
                        moved[i, row] = delta[0]
                        moved[i, row + 1] = delta[1]


def exchange(block, axis, mask):
    return lax.ppermute(block, axis, [(i, i ^ mask) for i in range(lax.axis_size(axis))])


def butterfly_sum(value, axis):
    mask = 1
    while mask < lax.axis_size(axis):
        value = value + exchange(value, axis, mask)
        mask *= 2
    return value


def halving_sum(value, axis, dim):
    index = lax.axis_index(axis)
    mask = lax.axis_size(axis) // 2
    while mask:
        half = value.shape[dim] // 2
        bit = (index // mask) % 2
        kept = lax.dynamic_slice_in_dim(value, bit * half, half, dim)
        sent = lax.dynamic_slice_in_dim(value, (1 - bit) * half, half, dim)
        value = kept + exchange(sent, axis, mask)
        mask //= 2
    return value


def chip_blocks(block, axis):
    chips = lax.axis_size(axis) // 2
    if chips <= 4:
        return jnp.stack([block] + [exchange(block, axis, 2 * j) for j in range(1, chips)])
    parts = block[None]
    while parts.shape[0] < chips:
        parts = jnp.concatenate([parts, exchange(parts, axis, 2 * parts.shape[0])], axis=0)
    return parts


def on_device(visibilities, coherencies, gain_offsets, stations, solve_order, counts, damping):
    groups = lax.axis_size("bl")
    lane, own = lax.axis_index("dir").astype(jnp.int32), lax.axis_index("bl").astype(jnp.int32)
    owned, _, channel_count, baselines = coherencies.shape
    channels = visibilities.shape[1]
    width = gain_offsets.shape[2]
    count = groups * width
    tiles = baselines // 128
    solved = solve_order[:SOLVED]
    mine = (solved // owned == lane).astype(jnp.int32)
    base = (own * width)[None]
    params = pltpu.CompilerParams(vmem_limit_bytes=VMEM_BYTES)

    def call(kernel, name, shapes, scalars, arrays, scratch=(), **static):
        return pl.pallas_call(
            functools.partial(kernel, **static),
            out_shape=[jax.ShapeDtypeStruct(*shape) for shape in shapes],
            in_specs=[pl.BlockSpec(memory_space=pltpu.SMEM)] * len(scalars)
            + [pl.BlockSpec(memory_space=pltpu.VMEM)] * len(arrays),
            out_specs=[pl.BlockSpec(memory_space=pltpu.VMEM)] * len(shapes),
            scratch_shapes=[pltpu.VMEM(*shape) for shape in scratch],
            compiler_params=params,
            name=name,
        )(*scalars, *arrays)

    block = (1,) + coherencies.shape[1:]
    chosen = pl.pallas_call(
        select_kernel,
        out_shape=jax.ShapeDtypeStruct((SOLVED,) + block[1:], BF16),
        grid_spec=pltpu.PrefetchScalarGridSpec(
            num_scalar_prefetch=2,
            grid=(1,),
            in_specs=[pl.BlockSpec(block, lambda g, places, mine, i=i: (places[i], 0, 0, 0)) for i in range(SOLVED)],
            out_specs=pl.BlockSpec((SOLVED,) + block[1:], lambda g, places, mine: (0, 0, 0, 0)),
        ),
        compiler_params=params,
        name="select_solved",
    )(solved % owned, mine, *[coherencies] * SOLVED)
    shared = butterfly_sum(chosen, "dir")

    per = 128 // width
    part_rows = -(-(owned + SOLVED) // per) * 8
    places = jnp.concatenate([lane * owned + jnp.arange(owned, dtype=jnp.int32), solved])
    [packed] = call(
        prep_kernel, "pack_gains", [((part_rows, 128), F32)], [places], [gain_offsets], owned=owned, per=per
    )
    near = chip_blocks(packed, "bl")
    blocks = jnp.stack([near, exchange(near, "bl", 1)], axis=1).reshape(groups, part_rows, 128)
    vis = lax.dynamic_update_slice_in_dim(
        jnp.zeros((8, channel_count, baselines), F32), visibilities, lane * channels, 1
    )
    part, start, begin = call(
        model_kernel,
        "first_model",
        [((8, channel_count, baselines), F32), ((SOLVED * 8, count), F32), ((SOLVED * 8, 2 * baselines), F32)],
        [base],
        [blocks, stations, coherencies, vis],
        [((part_rows * per, count), F32), ((part_rows * per, 2 * baselines), F32)],
        width=width,
    )
    [m_part] = call(
        target_kernel, "target_products", [((tiles, SOLVED * M_ROWS, 128), F32)], [mine], [part, shared, begin]
    )
    kx, own_channels = call(
        product_kernel,
        "coherency_products",
        [((tiles, KX_ROWS, 128), F32), ((SOLVED, 8, channels, baselines), F32)],
        [lane[None]],
        [stations, shared],
    )
    m_near = chip_blocks(butterfly_sum(m_part, "dir"), "bl")
    kx_near = chip_blocks(kx, "bl")
    pieces = [m_near, exchange(m_near, "bl", 1), kx_near, exchange(kx_near, "bl", 1)]
    first = halving_sum(part, "dir", 1)

    chunks = groups * tiles
    gains, residual = call(
        sweep_kernel,
        "sweep",
        [(gain_offsets.shape, F32), (visibilities.shape, F32)],
        [base, solve_order, counts, damping],
        [piece.reshape(-1, 128) for piece in pieces] + [start, gain_offsets, first, own_channels],
        [
            ((groups, count, 2 * baselines), BF16),
            ((2, 2, chunks * 8, 128), F32),
            ((2, chunks * 16, 128), F32),
            ((8, count), F32),
            ((M_ROWS, chunks, 128), F32),
            ((K_ROWS, chunks, 128), F32),
            ((SOLVED - 1, M_ROWS, chunks, 128), F32),
        ],
        groups=groups,
        factor=baselines * groups * channel_count / count,
    )
    return gains, residual


def solution(mesh):
    return jax.shard_map(
        on_device,
        mesh=mesh,
        in_specs=(
            P(None, "dir", "bl"),
            P("dir", None, None, "bl"),
            P(None, None, "bl"),
            P(None, "bl"),
            P(),
            P(),
            P(),
        ),
        out_specs=(P(None, None, "bl"), P(None, "dir", "bl")),
        check_vma=False,
    )
```

```python
import functools

import jax
import jax.numpy as jnp
from jax import lax
from jax.experimental import pallas as pl
from jax.experimental.pallas import tpu as pltpu
from jax.sharding import PartitionSpec as P

LM_ITERS = 2
SOLVED = 4
F32 = jnp.float32
BF16 = jnp.bfloat16
VMEM_BYTES = 24 * 1024 * 1024
GRAM = [(u, v) for u in range(4) for v in range(u, 4)]
M_ROWS = 32
K_ROWS = 16
FIRST = 1


def mul(x, y):
    return (x[0] * y[0] - x[1] * y[1], x[0] * y[1] + x[1] * y[0])


def add(x, y):
    return (x[0] + y[0], x[1] + y[1])


def sub(x, y):
    return (x[0] - y[0], x[1] - y[1])


def conj(x):
    return (x[0], -x[1])


def total(terms):
    return functools.reduce(add, terms)


def mul_conj(x, y):
    return (x[0] * y[0] + x[1] * y[1], x[1] * y[0] - x[0] * y[1])


def matmul(left, right):
    return [add(mul(left[2 * i], right[j]), mul(left[2 * i + 1], right[2 + j])) for i in (0, 1) for j in (0, 1)]


def matmul_adj(left, right):
    return [
        add(mul_conj(left[2 * i], right[2 * j]), mul_conj(left[2 * i + 1], right[2 * j + 1]))
        for i in (0, 1)
        for j in (0, 1)
    ]


def apply_gains(gain_p, coher, gain_q):
    return matmul_adj(matmul(gain_p, coher), gain_q)


def as_matrix(parts):
    return [(parts[2 * e], parts[2 * e + 1]) for e in range(4)]


def split_rows(values):
    high = values.astype(BF16)
    low = (values - high.astype(F32)).astype(BF16)
    return jnp.concatenate([high, low], axis=0)


def one_hot(stations_p, stations_q, count):
    both = jnp.concatenate([stations_p, stations_q], axis=1)
    rows = lax.broadcasted_iota(jnp.int32, (count, both.shape[1]), 0)
    return jnp.where(rows == both, 1.0, 0.0).astype(BF16)


def pick(one_hots, values):
    count = values.shape[0]
    out = jnp.dot(split_rows(values), one_hots, preferred_element_type=F32)
    return out[:count] + out[count:]


def prep_kernel(order_ref, stations_ref, offs_ref, *refs, owned, per):
    *coher_refs, out_ref, first_ref, rest_ref = refs
    lane = lax.axis_index("dir")
    width = offs_ref.shape[2]
    station_rows = 2 * stations_ref.shape[1] // 128
    part_rows = out_ref.shape[0] - 8
    comp = lax.broadcasted_iota(jnp.int32, (8, width), 0)
    ident = jnp.where((comp == 0) | (comp == 6), 1.0, 0.0)
    places = [lane * owned + d for d in range(owned)] + [order_ref[i] for i in range(SOLVED)]
    blocks = [offs_ref[place] + ident for place in places]
    while len(blocks) * 8 < part_rows * per:
        blocks.append(jnp.zeros((8, width), F32))
    each = part_rows // 8
    columns = [jnp.concatenate(blocks[q * each : (q + 1) * each], axis=0) for q in range(per)]
    out_ref[:part_rows] = jnp.concatenate(columns, axis=1)
    out_ref[part_rows:] = jnp.zeros((8, 128), F32)
    for row in range(station_rows):
        end, tile = row // (station_rows // 2), row % (station_rows // 2)
        out_ref[part_rows + row : part_rows + row + 1] = stations_ref[end : end + 1, tile * 128 : tile * 128 + 128].astype(F32)
    for i in range(SOLVED):
        mine = order_ref[i] // owned == lane
        value = jnp.where(mine, coher_refs[i][0], jnp.zeros_like(coher_refs[i][0]))
        if i < FIRST:
            first_ref[i] = value
        else:
            rest_ref[i - FIRST] = value


def fill_table(blocks_ref, table, width):
    groups, rows, lanes = blocks_ref.shape
    part_rows = rows - 8
    per = lanes // width
    lane_of = lax.broadcasted_iota(jnp.int32, (part_rows, lanes), 1) // width
    for tile in range(groups * width // lanes):
        for q in range(per):
            tile_rows = jnp.zeros((part_rows, lanes), F32)
            for u in range(per):
                block = blocks_ref[per * tile + u, :part_rows]
                shift = ((u - q) * width) % lanes
                if shift:
                    block = pltpu.roll(block, shift, 1)
                tile_rows = jnp.where(lane_of == u, block, tile_rows)
            table[q * part_rows : (q + 1) * part_rows, tile * lanes : (tile + 1) * lanes] = tile_rows


def block_stations(blocks_ref, g, tiles, base):
    part_rows = blocks_ref.shape[1] - 8
    rows = blocks_ref[g, part_rows:, :].astype(jnp.int32) ^ base
    return [jnp.concatenate([rows[end * tiles + t : end * tiles + t + 1] for t in range(tiles)], axis=1) for end in (0, 1)]


def lookup_kernel(blocks_ref, hots_ref, ends_ref, start_ref, table, *, width, owned):
    groups = blocks_ref.shape[0]
    baselines = hots_ref.shape[2] // 2
    tiles = baselines // 128
    base = lax.axis_index("bl").astype(jnp.int32) * width
    fill_table(blocks_ref, table, width)
    start = table[owned * 8 : (owned + SOLVED) * 8, :]
    start_ref[...] = start
    split = split_rows(start)
    for g in range(groups):
        half = groups // 2
        rows_p, rows_q = block_stations(blocks_ref, 2 * (g % half) + g // half, tiles, base)
        hots_ref[g] = one_hot(rows_p, rows_q, groups * width)
        out = jnp.dot(split, hots_ref[g], preferred_element_type=F32)
        out = out[: SOLVED * 8] + out[SOLVED * 8 :]
        for i in range(SOLVED):
            for end in (0, 1):
                for t in range(tiles):
                    chunk, column = (g * tiles + t) * 8, (end * tiles + t) * 128
                    ends_ref[i, end, chunk : chunk + 8, :] = out[i * 8 : i * 8 + 8, column : column + 128]


def model_kernel(blocks_ref, coher_ref, vis_ref, part_ref, begin_ref, *refs, width):
    *piece_refs, table, ends = refs
    owned = coher_ref.shape[0]
    baselines = coher_ref.shape[3]
    channels = vis_ref.shape[1]
    lane = lax.axis_index("dir")
    base = lax.axis_index("bl").astype(jnp.int32) * width
    fill_table(blocks_ref, table, width)
    rows_p, rows_q = block_stations(blocks_ref, 0, baselines // 128, base)
    ends[...] = pick(one_hot(rows_p, rows_q, table.shape[1]), table[...])
    begin_ref[...] = ends[owned * 8 : (owned + SOLVED) * 8, :]

    for half in range(baselines // 128):
        at = pl.ds(half * 128, 128)
        at_q = pl.ds(baselines + half * 128, 128)

        def gain(row, where):
            block = ends[pl.ds(pl.multiple_of(row, 8), 8), where]
            return as_matrix([block[c : c + 1] for c in range(8)])

        def add_model(d, acc):
            coher = as_matrix([coher_ref[d, c, :, at].astype(F32) for c in range(8)])
            model = apply_gains(gain(d * 8, at), coher, gain(d * 8, at_q))
            return [sub(x, y) for x, y in zip(acc, model)]

        zeros = jnp.zeros((coher_ref.shape[2], 128), F32)
        acc = lax.fori_loop(0, owned, add_model, [(zeros, zeros)] * 4)
        for c in range(8):
            total_part = acc[c // 2][c % 2]
            lanes = [total_part[x * channels : (x + 1) * channels] for x in range(len(piece_refs))]
            vis = vis_ref[c, :, at]
            for k, piece_ref in enumerate(piece_refs):
                value = lanes[0]
                for x in range(1, len(lanes)):
                    value = jnp.where(lane ^ k == x, lanes[x], value)
                piece_ref[c, :, at] = value + vis if k == 0 else value
            part_ref[c, :, at] = jnp.concatenate([jnp.where(lane == x, y + vis, y) for x, y in enumerate(lanes)], axis=0)


def summed(values):
    return jnp.sum(values, axis=0, keepdims=True)


def target_kernel(order_ref, part_ref, solved_ref, begin_ref, m_ref, *, owned, low):
    baselines = part_ref.shape[2]
    lane = lax.axis_index("dir")
    for half in range(baselines // 128):
        at = pl.ds(half * 128, 128)
        for i in range(solved_ref.shape[0]):
            coher = as_matrix([solved_ref[i, c, :, at].astype(F32) for c in range(8)])
            row = (low + i) * 8
            gain_p, gain_q = [
                as_matrix([begin_ref[row + c : row + c + 1, pl.ds(end * baselines + half * 128, 128)] for c in range(8)])
                for end in (0, 1)
            ]
            model = apply_gains(gain_p, coher, gain_q)
            flag = (order_ref[low + i] // owned == lane).astype(F32)
            target = [
                (part_ref[2 * e, :, at] + flag * model[e][0], part_ref[2 * e + 1, :, at] + flag * model[e][1])
                for e in range(4)
            ]
            out = i * M_ROWS
            for u in range(4):
                for v in range(4):
                    value = mul_conj(target[u], coher[v])
                    m_ref[half, out : out + 1, :] = summed(value[0])
                    m_ref[half, out + 1 : out + 2, :] = summed(value[1])
                    out += 2


def pair_list(low):
    return [(m, i) for i in range(low, SOLVED) for m in range(i)]


def product_kernel(*refs, low):
    *solved_refs, kx_ref, own_ref = refs
    where = [(ref, i) for ref in solved_refs for i in range(ref.shape[0])]
    baselines = solved_refs[0].shape[3]
    channels = own_ref.shape[2]
    lane = lax.axis_index("dir")
    for half in range(baselines // 128):
        at = pl.ds(half * 128, 128)

        def load(i):
            ref, place = where[i]
            return [ref[place, c, :, at].astype(F32) for c in range(8)]

        out = 0
        for i in range(low, len(where)):
            parts = load(i)
            for c in range(8):
                mine = parts[c][:channels]
                for x in range(1, parts[c].shape[0] // channels):
                    mine = jnp.where(lane == x, parts[c][x * channels : (x + 1) * channels], mine)
                own_ref[i - low, c, :, at] = mine
            coher = as_matrix(parts)
            for u, v in GRAM:
                value = mul_conj(coher[u], coher[v])
                kx_ref[half, out : out + 1, :] = summed(value[0])
                out += 1
                if u != v:
                    kx_ref[half, out : out + 1, :] = summed(value[1])
                    out += 1
        if low == 0:
            continue
        for m, i in pair_list(low):
            coher, other = as_matrix(load(i)), as_matrix(load(m))
            for u in range(4):
                for v in range(4):
                    value = mul_conj(other[u], coher[v])
                    kx_ref[half, out : out + 1, :] = summed(value[0])
                    kx_ref[half, out + 1 : out + 2, :] = summed(value[1])
                    out += 2


def sweep_kernel(order_ref, counts_ref, damping_ref, *refs, low, high, tiles, factor, last):
    hots, begin, start_ref = refs[:3]
    near_m, far_m, near_kx, far_kx = refs[3:7]
    refs = refs[7:]
    if last:
        earlier, earlier_gains, earlier_after, offs_ref, own_a, own_b = refs[:6]
        pieces = refs[6:-8]
        gains_ref, out_ref = refs[-8:-6]
    else:
        solved_ref, moved_ref, after_ref = refs[:3]
    ends, values, state, m_now, k_now, moved = refs[-6:]
    groups, count = hots.shape[:2]
    chunks = groups * tiles
    kx_stride = near_kx.shape[0] // (chunks // 2)
    m_stride = near_m.shape[0] // (chunks // 2)
    x_start = kx_stride - M_ROWS * len(pair_list(low)) if low else 0
    k_start = 0 if low else high * M_ROWS

    def m_at(row):
        return jnp.concatenate([ref[pl.ds(row, chunks // 2, stride=m_stride), :] for ref in (near_m, far_m)], axis=0)

    def kx_at(row):
        return jnp.concatenate([ref[pl.ds(row, chunks // 2, stride=kx_stride), :] for ref in (near_kx, far_kx)], axis=0)

    def fetch(gain_now, only=None):
        split = split_rows(gain_now)
        for g in range(groups if only is None else only):
            out = jnp.dot(split, hots[g], preferred_element_type=F32)
            out = out[:8] + out[8:]
            for end in (0, 1):
                for t in range(tiles):
                    chunk, column = (g * tiles + t) * 8, (end * tiles + t) * 128
                    ends[end, chunk : chunk + 8, :] = out[:, column : column + 128]

    def gain_at(ref):
        return [as_matrix([ref[end, pl.ds(c, chunks, stride=8), :] for c in range(8)]) for end in (0, 1)]

    def load_m():
        return [[(m_now[(u * 4 + v) * 2], m_now[(u * 4 + v) * 2 + 1]) for v in range(4)] for u in range(4)]

    def load_k():
        row = 0
        gram = {}
        for u, v in GRAM:
            if u == v:
                gram[u, v] = (k_now[row], None)
                row += 1
            else:
                gram[u, v] = (k_now[row], k_now[row + 1])
                gram[v, u] = conj(gram[u, v])
                row += 2
        return gram

    def prepare(i):
        for row in range(K_ROWS):
            k_now[row] = kx_at(k_start + (i - low) * K_ROWS + row)
        for out in range(4):
            for w in range(4):
                row = (out * 4 + w) * 2
                value = (m_at((i - low) * M_ROWS + row), m_at((i - low) * M_ROWS + row + 1))
                for m in range(i):
                    base = x_start + pair_list(low).index((m, i)) * M_ROWS
                    source = moved.at[m - low] if m >= low else earlier.at[m]
                    for uv in range(4):
                        delta = (source[(out * 4 + uv) * 2], source[(out * 4 + uv) * 2 + 1])
                        at = base + (uv * 4 + w) * 2
                        value = add(value, mul(delta, (kx_at(at), kx_at(at + 1))))
                m_now[row] = value[0]
                m_now[row + 1] = value[1]

    def hermitian(gain):
        a = gain[0][0] ** 2 + gain[0][1] ** 2 + gain[2][0] ** 2 + gain[2][1] ** 2
        d = gain[1][0] ** 2 + gain[1][1] ** 2 + gain[3][0] ** 2 + gain[3][1] ** 2
        cross = add(mul_conj(gain[1], gain[0]), mul_conj(gain[3], gain[2]))
        return a, d, cross

    def normal_terms():
        gain_p, gain_q = gain_at(ends)
        m = load_m()
        k = load_k()
        for end, gain, other in ((0, gain_q, False), (1, gain_p, True)):
            row = 0
            for r in (0, 1):
                for c in (0, 1):
                    if other:
                        terms = [mul_conj(gain[2 * a + b], m[2 * a + r][2 * b + c]) for a in (0, 1) for b in (0, 1)]
                    else:
                        terms = [mul(gain[2 * a + b], m[2 * r + a][2 * c + b]) for a in (0, 1) for b in (0, 1)]
                    value = total(terms)
                    values[end, pl.ds(row, chunks, stride=16), :] = value[0]
                    values[end, pl.ds(row + 1, chunks, stride=16), :] = value[1]
                    row += 2
            a, d, cross = hermitian(gain)
            for r, c in ((0, 0), (1, 1), (0, 1)):
                if other:
                    kk = [[k[2 * x + r, 2 * y + c] for y in (0, 1)] for x in (0, 1)]
                    kk = [[(z[0], None if z[1] is None else -z[1]) for z in line] for line in kk]
                else:
                    kk = [[k[2 * r + x, 2 * c + y] for y in (0, 1)] for x in (0, 1)]
                real = a * kk[0][0][0] + d * kk[1][1][0]
                real += cross[0] * (kk[0][1][0] + kk[1][0][0])
                minus = None
                if kk[0][1][1] is not None:
                    minus = kk[1][0][1] - kk[0][1][1]
                    real += cross[1] * minus
                values[end, pl.ds(row, chunks, stride=16), :] = real
                row += 1
                if r != c:
                    imag = cross[1] * (kk[0][1][0] - kk[1][0][0])
                    if kk[0][0][1] is not None:
                        imag += a * kk[0][0][1]
                    if kk[1][1][1] is not None:
                        imag += d * kk[1][1][1]
                    if kk[0][1][1] is not None:
                        imag += cross[0] * kk[0][1][1]
                    if kk[1][0][1] is not None:
                        imag += cross[0] * kk[1][0][1]
                    values[end, pl.ds(row, chunks, stride=16), :] = imag
                    row += 1

    def station_sums():
        acc = jnp.zeros((32, count), F32)
        for g in range(groups):
            starts = [(end, (g * tiles + t) * 16) for end in (0, 1) for t in range(tiles)]
            split = split_rows(jnp.concatenate([values[end, at : at + 16, :] for end, at in starts], axis=1))
            acc += lax.dot_general(split, hots[g], (((1,), (1,)), ((), ())), preferred_element_type=F32)
        return acc[:16] + acc[16:]

    def solve(sums, gain_now, damp):
        numer = sums[:8] + damp * gain_now
        numer = as_matrix([numer[c : c + 1] for c in range(8)])
        diag_a = sums[8:9] + damp
        diag_d = sums[9:10] + damp
        cross_r = sums[10:11]
        cross_i = sums[11:12]
        scale = 1.0 / (diag_a * diag_d - cross_r * cross_r - cross_i * cross_i)
        rows = []
        for r in (0, 1):
            x, y = numer[2 * r], numer[2 * r + 1]
            low = mul(y, (cross_r, -cross_i))
            high = mul(x, (cross_r, cross_i))
            rows += [x[0] * diag_d - low[0], x[1] * diag_d - low[1]]
            rows += [y[0] * diag_a - high[0], y[1] * diag_a - high[1]]
        return jnp.concatenate([value * scale for value in rows], axis=0)

    def add_change(i, coher_ref, after):
        for tile in range(tiles):
            at = pl.ds(tile * 128, 128)
            coher = as_matrix([coher_ref[c, :, at] for c in range(8)])
            rows = [tile * 8 + c for c in range(8)]
            one = [as_matrix([begin[i, end, row : row + 1, :] for row in rows]) for end in (0, 1)]
            two = [as_matrix([after[end, row : row + 1, :] for row in rows]) for end in (0, 1)]
            before, now = apply_gains(one[0], coher, one[1]), apply_gains(two[0], coher, two[1])
            for e in range(4):
                change = sub(before[e], now[e])
                out_ref[2 * e, :, at] += change[0]
                out_ref[2 * e + 1, :, at] += change[1]

    width = offs_ref.shape[2] if last else None
    if last:
        comp = lax.broadcasted_iota(jnp.int32, (8, width), 0)
        gains_ref[...] = offs_ref[...] + jnp.where((comp == 0) | (comp == 6), 1.0, 0.0)[None]
        out_ref[...] = functools.reduce(lambda x, y: x + y, [piece[...] for piece in pieces])
        for i in range(low):
            gains_ref[order_ref[i]] = earlier_gains[i, :, :width]
            add_change(i, own_a.at[i], earlier_after.at[i])
    values[...] = jnp.zeros(values.shape, F32)
    for i in range(low, high):
        which = order_ref[i]
        damp = damping_ref[which].astype(F32) * factor
        state[...] = start_ref[i * 8 : i * 8 + 8, :]
        ends[...] = begin[i]
        prepare(i)

        def one_round():
            normal_terms()
            state[...] = solve(station_sums(), state[...], damp)

        def more(r, carry):
            one_round()
            fetch(state[...])
            return carry

        lax.fori_loop(0, jnp.minimum(counts_ref[which], LM_ITERS) - 1, more, jnp.int32(0))
        one_round()
        if last:
            gains_ref[which] = state[:, :width]
            fetch(state[...], 1 if i + 1 == high else None)
            add_change(i, own_b.at[i - low], ends)
        else:
            solved_ref[i - low] = state[...]
            fetch(state[...])
            after_ref[i - low] = ends[:, : tiles * 8, :]
        if i + 1 == SOLVED:
            break
        p0, q0 = gain_at(begin.at[i])
        p1, q1 = gain_at(ends)
        store = moved if last else moved_ref
        for a in (0, 1):
            for b in (0, 1):
                for u in (0, 1):
                    for v in (0, 1):
                        delta = sub(mul_conj(p0[2 * a + u], q0[2 * b + v]), mul_conj(p1[2 * a + u], q1[2 * b + v]))
                        row = ((2 * a + b) * 4 + 2 * u + v) * 2
                        store[i - low, row] = delta[0]
                        store[i - low, row + 1] = delta[1]


def exchange(block, axis, mask):
    return lax.ppermute(block, axis, [(i, i ^ mask) for i in range(lax.axis_size(axis))])


def butterfly_sum(value, axis):
    mask = 1
    while mask < lax.axis_size(axis):
        value = value + exchange(value, axis, mask)
        mask *= 2
    return value


def chip_blocks(block, axis):
    chips = lax.axis_size(axis) // 2
    if chips <= 4:
        return jnp.stack([block] + [exchange(block, axis, 2 * j) for j in range(1, chips)])
    parts = block[None]
    while parts.shape[0] < chips:
        parts = jnp.concatenate([parts, exchange(parts, axis, 2 * parts.shape[0])], axis=0)
    return parts


def on_device(visibilities, coherencies, gain_offsets, stations, solve_order, counts, damping):
    groups = lax.axis_size("bl")
    owned, _, channel_count, baselines = coherencies.shape
    channels = visibilities.shape[1]
    width = gain_offsets.shape[2]
    count = groups * width
    tiles = baselines // 128
    lanes = lax.axis_size("dir")
    params = pltpu.CompilerParams(vmem_limit_bytes=VMEM_BYTES)
    rest = SOLVED - FIRST

    def call(kernel, name, shapes, scalars, arrays, scratch=(), **static):
        return pl.pallas_call(
            functools.partial(kernel, **static),
            out_shape=[jax.ShapeDtypeStruct(*shape) for shape in shapes],
            in_specs=[pl.BlockSpec(memory_space=pltpu.SMEM)] * len(scalars)
            + [pl.BlockSpec(memory_space=pltpu.VMEM)] * len(arrays),
            out_specs=[pl.BlockSpec(memory_space=pltpu.VMEM)] * len(shapes),
            scratch_shapes=[pltpu.VMEM(*shape) for shape in scratch],
            compiler_params=params,
            name=name,
        )(*scalars, *arrays)

    per = 128 // width
    part_rows = -(-(owned + SOLVED) // per) * 8
    block = coherencies.shape[1:]
    whole = lambda shape: pl.BlockSpec(shape, lambda g, order: (0,) * len(shape))
    picked = lambda i: pl.BlockSpec((1,) + block, lambda g, order: (order[i] % owned, 0, 0, 0))
    shapes = [(part_rows + 8, 128), (FIRST,) + block, (rest,) + block]
    packed, chosen_first, chosen_rest = pl.pallas_call(
        functools.partial(prep_kernel, owned=owned, per=per),
        out_shape=[jax.ShapeDtypeStruct(shape, dtype) for shape, dtype in zip(shapes, (F32, BF16, BF16))],
        grid_spec=pltpu.PrefetchScalarGridSpec(
            num_scalar_prefetch=1,
            grid=(1,),
            in_specs=[whole(stations.shape), whole(gain_offsets.shape)] + [picked(i) for i in range(SOLVED)],
            out_specs=[whole(shape) for shape in shapes],
        ),
        compiler_params=params,
        name="prepare",
    )(solve_order, stations, gain_offsets, *[coherencies] * SOLVED)

    near = chip_blocks(packed, "bl")
    blocks = jnp.stack([near, exchange(near, "bl", 1)], axis=1).reshape(groups, part_rows + 8, 128)
    shared_first = butterfly_sum(chosen_first, "dir")
    shared_rest = butterfly_sum(chosen_rest, "dir")

    table = ((part_rows * per, count), F32)
    part, begin, *pieces = call(
        model_kernel,
        "first_model",
        [((8, channel_count, baselines), F32), ((SOLVED * 8, 2 * baselines), F32)] + [(visibilities.shape, F32)] * lanes,
        [],
        [blocks, coherencies, visibilities],
        [table, ((part_rows * per, 2 * baselines), F32)],
        width=width,
    )
    [m_first] = call(
        target_kernel, "first_target", [((tiles, FIRST * M_ROWS, 128), F32)], [solve_order],
        [part, shared_first, begin], owned=owned, low=0,
    )
    k_first, own_first = call(
        product_kernel, "first_products",
        [((tiles, FIRST * K_ROWS, 128), F32), ((FIRST, 8, channels, baselines), F32)], [], [shared_first], low=0,
    )
    hots, ends, start = call(
        lookup_kernel, "lookup",
        [
            ((groups, count, 2 * baselines), BF16),
            ((SOLVED, 2, groups * tiles * 8, 128), F32),
            ((SOLVED * 8, count), F32),
        ],
        [], [blocks], [table], width=width, owned=owned,
    )
    [m_rest] = call(
        target_kernel, "other_targets", [((tiles, rest * M_ROWS, 128), F32)], [solve_order],
        [part, shared_rest, begin], owned=owned, low=FIRST,
    )
    kx_rows = rest * K_ROWS + len(pair_list(FIRST)) * M_ROWS
    kx_rest, own_rest = call(
        product_kernel, "other_products",
        [((tiles, kx_rows, 128), F32), ((rest, 8, channels, baselines), F32)], [], [shared_first, shared_rest], low=FIRST,
    )

    first_near = chip_blocks(jnp.concatenate([butterfly_sum(m_first, "dir"), k_first], axis=1), "bl")
    first_far = exchange(first_near, "bl", 1)
    pieces = [pieces[0]] + [exchange(piece, "dir", k) for k, piece in enumerate(pieces) if k]
    kx_near = chip_blocks(kx_rest, "bl")
    kx_far = exchange(kx_near, "bl", 1)
    m_near = chip_blocks(butterfly_sum(m_rest, "dir"), "bl")
    m_far = exchange(m_near, "bl", 1)

    chunks = groups * tiles
    static = dict(tiles=tiles, factor=baselines * groups * channel_count / count)
    scratch = [
        ((2, chunks * 8, 128), F32),
        ((2, chunks * 16, 128), F32),
        ((8, count), F32),
        ((M_ROWS, chunks, 128), F32),
        ((K_ROWS, chunks, 128), F32),
    ]
    flat = lambda *arrays: [array.reshape(-1, 128) for array in arrays]
    scalars = [solve_order, counts, damping]
    solved_first, moved_first, after_first = call(
        sweep_kernel, "first_sweep",
        [((FIRST, 8, count), F32), ((FIRST, M_ROWS, chunks, 128), F32), ((FIRST, 2, tiles * 8, 128), F32)],
        scalars,
        [hots, ends, start] + flat(first_near, first_far, first_near, first_far),
        scratch + [((1, 8, 128), F32)],
        low=0, high=FIRST, last=False, **static,
    )
    gains, residual = call(
        sweep_kernel, "other_sweeps",
        [(gain_offsets.shape, F32), (visibilities.shape, F32)],
        scalars,
        [hots, ends, start] + flat(m_near, m_far, kx_near, kx_far)
        + [moved_first, solved_first, after_first, gain_offsets, own_first, own_rest] + pieces,
        scratch + [((rest, M_ROWS, chunks, 128), F32)],
        low=FIRST, high=SOLVED, last=True, **static,
    )
    return gains, residual


def solution(mesh):
    return jax.shard_map(
        on_device,
        mesh=mesh,
        in_specs=(
            P(None, "dir", "bl"),
            P("dir", None, None, "bl"),
            P(None, None, "bl"),
            P(None, "bl"),
            P(),
            P(),
            P(),
        ),
        out_specs=(P(None, None, "bl"), P(None, "dir", "bl")),
        check_vma=False,
    )
```

```python
import functools

import jax
import jax.numpy as jnp
from jax import lax
from jax.experimental import pallas as pl
from jax.experimental.pallas import tpu as pltpu
from jax.sharding import PartitionSpec as P

LM_ITERS = 2
SOLVED = 4
F32 = jnp.float32
BF16 = jnp.bfloat16
VMEM_BYTES = 24 * 1024 * 1024
MOST_VMEM_BYTES = 60 * 1024 * 1024
GRAM = [(u, v) for u in range(4) for v in range(u, 4)]
M_ROWS = 32
K_ROWS = 16
GROUPS = [(0, 2), (2, 4)]
TARGETS = [(0, 4)]


def mul(x, y):
    return (x[0] * y[0] - x[1] * y[1], x[0] * y[1] + x[1] * y[0])


def add(x, y):
    return (x[0] + y[0], x[1] + y[1])


def sub(x, y):
    return (x[0] - y[0], x[1] - y[1])


def conj(x):
    return (x[0], -x[1])


def total(terms):
    return functools.reduce(add, terms)


def mul_conj(x, y):
    return (x[0] * y[0] + x[1] * y[1], x[1] * y[0] - x[0] * y[1])


def matmul(left, right):
    return [add(mul(left[2 * i], right[j]), mul(left[2 * i + 1], right[2 + j])) for i in (0, 1) for j in (0, 1)]


def matmul_adj(left, right):
    return [
        add(mul_conj(left[2 * i], right[2 * j]), mul_conj(left[2 * i + 1], right[2 * j + 1]))
        for i in (0, 1)
        for j in (0, 1)
    ]


def apply_gains(gain_p, coher, gain_q):
    return matmul_adj(matmul(gain_p, coher), gain_q)


def as_matrix(parts):
    return [(parts[2 * e], parts[2 * e + 1]) for e in range(4)]


def split_rows(values):
    high = values.astype(BF16)
    low = (values - high.astype(F32)).astype(BF16)
    return jnp.concatenate([high, low], axis=0)


def one_hot(stations_p, stations_q, count):
    both = jnp.concatenate([stations_p, stations_q], axis=1)
    rows = lax.broadcasted_iota(jnp.int32, (count, both.shape[1]), 0)
    return jnp.where(rows == both, 1.0, 0.0).astype(BF16)


def pick(one_hots, values):
    count = values.shape[0]
    out = jnp.dot(split_rows(values), one_hots, preferred_element_type=F32)
    return out[:count] + out[count:]


def prep_kernel(order_ref, stations_ref, offs_ref, *refs, owned, per):
    coher_refs, out_ref, chosen_refs = refs[:SOLVED], refs[SOLVED], refs[SOLVED + 1 :]
    lane = lax.axis_index("dir")
    width = offs_ref.shape[2]
    station_rows = 2 * stations_ref.shape[1] // 128
    part_rows = out_ref.shape[0] - 8
    comp = lax.broadcasted_iota(jnp.int32, (8, width), 0)
    ident = jnp.where((comp == 0) | (comp == 6), 1.0, 0.0)
    places = [lane * owned + d for d in range(owned)] + [order_ref[i] for i in range(SOLVED)]
    blocks = [offs_ref[place] + ident for place in places]
    while len(blocks) * 8 < part_rows * per:
        blocks.append(jnp.zeros((8, width), F32))
    each = part_rows // 8
    columns = [jnp.concatenate(blocks[q * each : (q + 1) * each], axis=0) for q in range(per)]
    out_ref[:part_rows] = jnp.concatenate(columns, axis=1)
    out_ref[part_rows:] = jnp.zeros((8, 128), F32)
    for row in range(station_rows):
        end, tile = row // (station_rows // 2), row % (station_rows // 2)
        out_ref[part_rows + row : part_rows + row + 1] = stations_ref[end : end + 1, tile * 128 : tile * 128 + 128].astype(F32)
    for i in range(SOLVED):
        mine = order_ref[i] // owned == lane
        [(low, ref)] = [(low, ref) for (low, high), ref in zip(GROUPS, chosen_refs) if low <= i < high]
        ref[i - low] = jnp.where(mine, coher_refs[i][0], jnp.zeros_like(coher_refs[i][0]))


def fill_table(blocks_ref, table, width):
    groups, rows, lanes = blocks_ref.shape
    part_rows = rows - 8
    per = lanes // width
    lane_of = lax.broadcasted_iota(jnp.int32, (part_rows, lanes), 1) // width
    for tile in range(groups * width // lanes):
        for q in range(per):
            tile_rows = jnp.zeros((part_rows, lanes), F32)
            for u in range(per):
                block = blocks_ref[per * tile + u, :part_rows]
                shift = ((u - q) * width) % lanes
                if shift:
                    block = pltpu.roll(block, shift, 1)
                tile_rows = jnp.where(lane_of == u, block, tile_rows)
            table[q * part_rows : (q + 1) * part_rows, tile * lanes : (tile + 1) * lanes] = tile_rows


def block_stations(blocks_ref, g, tiles, base):
    part_rows = blocks_ref.shape[1] - 8
    rows = blocks_ref[g, part_rows:, :].astype(jnp.int32) ^ base
    return [jnp.concatenate([rows[end * tiles + t : end * tiles + t + 1] for t in range(tiles)], axis=1) for end in (0, 1)]


def lookup_kernel(blocks_ref, hots_ref, ends_ref, start_ref, table, *, width, owned):
    groups = blocks_ref.shape[0]
    baselines = hots_ref.shape[2] // 2
    tiles = baselines // 128
    base = lax.axis_index("bl").astype(jnp.int32) * width
    fill_table(blocks_ref, table, width)
    start = table[owned * 8 : (owned + SOLVED) * 8, :]
    start_ref[...] = start
    split = split_rows(start)
    for g in range(groups):
        half = groups // 2
        rows_p, rows_q = block_stations(blocks_ref, 2 * (g % half) + g // half, tiles, base)
        hots_ref[g] = one_hot(rows_p, rows_q, groups * width)
        out = jnp.dot(split, hots_ref[g], preferred_element_type=F32)
        out = out[: SOLVED * 8] + out[SOLVED * 8 :]
        for i in range(SOLVED):
            for end in (0, 1):
                for t in range(tiles):
                    chunk, column = (g * tiles + t) * 8, (end * tiles + t) * 128
                    ends_ref[i, end, chunk : chunk + 8, :] = out[i * 8 : i * 8 + 8, column : column + 128]


def model_kernel(blocks_ref, coher_ref, vis_ref, part_ref, begin_ref, table, ends, *, width):
    owned = coher_ref.shape[0]
    baselines = coher_ref.shape[3]
    channels = vis_ref.shape[1]
    lane = lax.axis_index("dir")
    base = lax.axis_index("bl").astype(jnp.int32) * width
    fill_table(blocks_ref, table, width)
    rows_p, rows_q = block_stations(blocks_ref, 0, baselines // 128, base)
    ends[...] = pick(one_hot(rows_p, rows_q, table.shape[1]), table[...])
    begin_ref[...] = ends[owned * 8 : (owned + SOLVED) * 8, :]

    for half in range(baselines // 128):
        at = pl.ds(half * 128, 128)
        at_q = pl.ds(baselines + half * 128, 128)

        def gain(row, where):
            block = ends[pl.ds(pl.multiple_of(row, 8), 8), where]
            return as_matrix([block[c : c + 1] for c in range(8)])

        def add_model(d, acc):
            coher = as_matrix([coher_ref[d, c, :, at].astype(F32) for c in range(8)])
            model = apply_gains(gain(d * 8, at), coher, gain(d * 8, at_q))
            return [sub(x, y) for x, y in zip(acc, model)]

        zeros = jnp.zeros((coher_ref.shape[2], 128), F32)
        acc = lax.fori_loop(0, owned, add_model, [(zeros, zeros)] * 4)
        for c in range(8):
            total_part = acc[c // 2][c % 2]
            lanes = [total_part[x : x + channels] for x in range(0, total_part.shape[0], channels)]
            vis = vis_ref[c, :, at]
            part_ref[c, :, at] = jnp.concatenate([jnp.where(lane == x, y + vis, y) for x, y in enumerate(lanes)], axis=0)


def summed(values):
    return jnp.sum(values, axis=0, keepdims=True)


def pair_list(low, high):
    return [(m, i) for i in range(low, high) for m in range(i)]


def load_coher(refs, i, at):
    [(low, ref)] = [(low, ref) for (low, high), ref in zip(GROUPS, refs) if low <= i < high]
    return as_matrix([ref[i - low, c, :, at].astype(F32) for c in range(8)])


def target_kernel(first_ref, begin_ref, *refs, low, high):
    *solved_refs, out_ref = refs
    baselines = first_ref.shape[2]
    for half in range(baselines // 128):
        at = pl.ds(half * 128, 128)
        out = 0
        for i in range(low, high):
            coher = load_coher(solved_refs, i, at)
            gain_p, gain_q = [
                as_matrix([begin_ref[i * 8 + c : i * 8 + c + 1, pl.ds(end * baselines + half * 128, 128)] for c in range(8)])
                for end in (0, 1)
            ]
            model = apply_gains(gain_p, coher, gain_q)
            target = [(first_ref[2 * e, :, at] + model[e][0], first_ref[2 * e + 1, :, at] + model[e][1]) for e in range(4)]
            for u in range(4):
                for v in range(4):
                    value = mul_conj(target[u], coher[v])
                    out_ref[half, out : out + 1, :] = summed(value[0])
                    out_ref[half, out + 1 : out + 2, :] = summed(value[1])
                    out += 2


def product_kernel(*refs, low, high):
    *solved_refs, out_ref = refs
    for half in range(out_ref.shape[0]):
        at = pl.ds(half * 128, 128)
        out = 0
        for i in range(low, high):
            coher = load_coher(solved_refs, i, at)
            for u, v in GRAM:
                value = mul_conj(coher[u], coher[v])
                out_ref[half, out : out + 1, :] = summed(value[0])
                out += 1
                if u != v:
                    out_ref[half, out : out + 1, :] = summed(value[1])
                    out += 1
        for m, i in pair_list(low, high):
            coher, other = load_coher(solved_refs, i, at), load_coher(solved_refs, m, at)
            for u in range(4):
                for v in range(4):
                    value = mul_conj(other[u], coher[v])
                    out_ref[half, out : out + 1, :] = summed(value[0])
                    out_ref[half, out + 1 : out + 2, :] = summed(value[1])
                    out += 2


def own_kernel(first_ref, *refs):
    *solved_refs, res_ref, own_ref = refs
    channels = res_ref.shape[1]
    lane = lax.axis_index("dir")

    def select(value):
        mine = value[:channels]
        for x in range(1, value.shape[0] // channels):
            mine = jnp.where(lane == x, value[x * channels : (x + 1) * channels], mine)
        return mine

    for c in range(8):
        res_ref[c] = select(first_ref[c])
        for (low, high), solved_ref in zip(GROUPS, solved_refs):
            for i in range(low, high):
                own_ref[i, c] = select(solved_ref[i - low, c].astype(F32))


def sweep_kernel(order_ref, counts_ref, damping_ref, *refs, low, high, tiles, factor):
    last = high == SOLVED
    hots, begin, start_ref, res_ref, own_ref = refs[:5]
    targets, refs = refs[5:7], refs[7:]
    products = [refs[2 * g : 2 * g + 2] for g in range(len(GROUPS))]
    ends, values, state, m_now, k_now = refs[-5:]
    refs = refs[2 * len(GROUPS) : -5]
    stages = [stage for stage in TARGETS if stage[1] <= low]
    earlier_moved = {m: (refs[s], m - stage[0]) for s, stage in enumerate(stages) for m in range(*stage)}
    refs = refs[len(stages) :]
    if last:
        earlier_gains = {m: (refs[s], m - stage[0]) for s, stage in enumerate(stages) for m in range(*stage)}
        offs_ref, gains_ref, out_ref, moved = refs[len(stages) :]
    else:
        solved_ref, moved, out_ref = refs
    groups, count = hots.shape[:2]
    chunks = groups * tiles

    def rows_at(pair, row):
        stride = pair[0].shape[0] // (chunks // 2)
        return jnp.concatenate([ref[pl.ds(row, chunks // 2, stride=stride), :] for ref in pair], axis=0)

    def fetch(gain_now, only=None):
        split = split_rows(gain_now)
        for g in range(groups if only is None else only):
            out = jnp.dot(split, hots[g], preferred_element_type=F32)
            out = out[:8] + out[8:]
            for end in (0, 1):
                for t in range(tiles):
                    chunk, column = (g * tiles + t) * 8, (end * tiles + t) * 128
                    ends[end, chunk : chunk + 8, :] = out[:, column : column + 128]

    def gain_at(ref):
        return [as_matrix([ref[end, pl.ds(c, chunks, stride=8), :] for c in range(8)]) for end in (0, 1)]

    def load_m():
        return [[(m_now[(u * 4 + v) * 2], m_now[(u * 4 + v) * 2 + 1]) for v in range(4)] for u in range(4)]

    def load_k():
        row = 0
        gram = {}
        for u, v in GRAM:
            if u == v:
                gram[u, v] = (k_now[row], None)
                row += 1
            else:
                gram[u, v] = (k_now[row], k_now[row + 1])
                gram[v, u] = conj(gram[u, v])
                row += 2
        return gram

    def prepare(i):
        [(pair, first, end)] = [(pair, *group) for pair, group in zip(products, GROUPS) if group[0] <= i < group[1]]
        for row in range(K_ROWS):
            k_now[row] = rows_at(pair, (i - first) * K_ROWS + row)
        for w in range(4):
            value = []
            for out in range(4):
                row = (i - low) * M_ROWS + (out * 4 + w) * 2
                value.append((rows_at(targets, row), rows_at(targets, row + 1)))
            for m in range(i):
                base = (end - first) * K_ROWS + pair_list(first, end).index((m, i)) * M_ROWS
                ref, place = (moved, m - low) if m >= low else earlier_moved[m]
                for uv in range(4):
                    at = base + (uv * 4 + w) * 2
                    cross = (rows_at(pair, at), rows_at(pair, at + 1))
                    for out in range(4):
                        row = (out * 4 + uv) * 2
                        value[out] = add(value[out], mul((ref[place, row], ref[place, row + 1]), cross))
            for out in range(4):
                m_now[(out * 4 + w) * 2] = value[out][0]
                m_now[(out * 4 + w) * 2 + 1] = value[out][1]

    def hermitian(gain):
        a = gain[0][0] ** 2 + gain[0][1] ** 2 + gain[2][0] ** 2 + gain[2][1] ** 2
        d = gain[1][0] ** 2 + gain[1][1] ** 2 + gain[3][0] ** 2 + gain[3][1] ** 2
        cross = add(mul_conj(gain[1], gain[0]), mul_conj(gain[3], gain[2]))
        return a, d, cross

    def normal_terms():
        gain_p, gain_q = gain_at(ends)
        m = load_m()
        k = load_k()
        for end, gain, other in ((0, gain_q, False), (1, gain_p, True)):
            row = 0
            for r in (0, 1):
                for c in (0, 1):
                    if other:
                        terms = [mul_conj(gain[2 * a + b], m[2 * a + r][2 * b + c]) for a in (0, 1) for b in (0, 1)]
                    else:
                        terms = [mul(gain[2 * a + b], m[2 * r + a][2 * c + b]) for a in (0, 1) for b in (0, 1)]
                    value = total(terms)
                    values[end, pl.ds(row, chunks, stride=16), :] = value[0]
                    values[end, pl.ds(row + 1, chunks, stride=16), :] = value[1]
                    row += 2
            a, d, cross = hermitian(gain)
            for r, c in ((0, 0), (1, 1), (0, 1)):
                if other:
                    kk = [[k[2 * x + r, 2 * y + c] for y in (0, 1)] for x in (0, 1)]
                    kk = [[(z[0], None if z[1] is None else -z[1]) for z in line] for line in kk]
                else:
                    kk = [[k[2 * r + x, 2 * c + y] for y in (0, 1)] for x in (0, 1)]
                real = a * kk[0][0][0] + d * kk[1][1][0]
                real += cross[0] * (kk[0][1][0] + kk[1][0][0])
                minus = None
                if kk[0][1][1] is not None:
                    minus = kk[1][0][1] - kk[0][1][1]
                    real += cross[1] * minus
                values[end, pl.ds(row, chunks, stride=16), :] = real
                row += 1
                if r != c:
                    imag = cross[1] * (kk[0][1][0] - kk[1][0][0])
                    if kk[0][0][1] is not None:
                        imag += a * kk[0][0][1]
                    if kk[1][1][1] is not None:
                        imag += d * kk[1][1][1]
                    if kk[0][1][1] is not None:
                        imag += cross[0] * kk[0][1][1]
                    if kk[1][0][1] is not None:
                        imag += cross[0] * kk[1][0][1]
                    values[end, pl.ds(row, chunks, stride=16), :] = imag
                    row += 1

    def station_sums():
        acc = jnp.zeros((32, count), F32)
        for g in range(groups):
            starts = [(end, (g * tiles + t) * 16) for end in (0, 1) for t in range(tiles)]
            split = split_rows(jnp.concatenate([values[end, at : at + 16, :] for end, at in starts], axis=1))
            acc += lax.dot_general(split, hots[g], (((1,), (1,)), ((), ())), preferred_element_type=F32)
        return acc[:16] + acc[16:]

    def solve(sums, gain_now, damp):
        numer = sums[:8] + damp * gain_now
        numer = as_matrix([numer[c : c + 1] for c in range(8)])
        diag_a = sums[8:9] + damp
        diag_d = sums[9:10] + damp
        cross_r = sums[10:11]
        cross_i = sums[11:12]
        scale = 1.0 / (diag_a * diag_d - cross_r * cross_r - cross_i * cross_i)
        rows = []
        for r in (0, 1):
            x, y = numer[2 * r], numer[2 * r + 1]
            low = mul(y, (cross_r, -cross_i))
            high = mul(x, (cross_r, cross_i))
            rows += [x[0] * diag_d - low[0], x[1] * diag_d - low[1]]
            rows += [y[0] * diag_a - high[0], y[1] * diag_a - high[1]]
        return jnp.concatenate([value * scale for value in rows], axis=0)

    def add_change(i):
        for tile in range(tiles):
            at = pl.ds(tile * 128, 128)
            coher = as_matrix([own_ref[i, c, :, at] for c in range(8)])
            rows = [tile * 8 + c for c in range(8)]
            one = [as_matrix([begin[i, end, row : row + 1, :] for row in rows]) for end in (0, 1)]
            two = [as_matrix([ends[end, row : row + 1, :] for row in rows]) for end in (0, 1)]
            before, now = apply_gains(one[0], coher, one[1]), apply_gains(two[0], coher, two[1])
            for e in range(4):
                change = sub(before[e], now[e])
                out_ref[2 * e, :, at] += change[0]
                out_ref[2 * e + 1, :, at] += change[1]

    out_ref[...] = res_ref[...]
    if last:
        width = offs_ref.shape[2]
        comp = lax.broadcasted_iota(jnp.int32, (8, width), 0)
        gains_ref[...] = offs_ref[...] + jnp.where((comp == 0) | (comp == 6), 1.0, 0.0)[None]
        for i in range(low):
            ref, place = earlier_gains[i]
            gains_ref[order_ref[i]] = ref[place, :, :width]
    values[...] = jnp.zeros(values.shape, F32)
    for i in range(low, high):
        which = order_ref[i]
        damp = damping_ref[which].astype(F32) * factor
        state[...] = start_ref[i * 8 : i * 8 + 8, :]
        ends[...] = begin[i]
        prepare(i)

        def one_round():
            normal_terms()
            state[...] = solve(station_sums(), state[...], damp)

        def more(r, carry):
            one_round()
            fetch(state[...])
            return carry

        lax.fori_loop(0, jnp.minimum(counts_ref[which], LM_ITERS) - 1, more, jnp.int32(0))
        one_round()
        fetch(state[...], 1 if i + 1 == SOLVED else None)
        if last:
            gains_ref[which] = state[:, :width]
        else:
            solved_ref[i - low] = state[...]
        add_change(i)
        if i + 1 == SOLVED:
            break
        p0, q0 = gain_at(begin.at[i])
        p1, q1 = gain_at(ends)
        for a in (0, 1):
            for b in (0, 1):
                for u in (0, 1):
                    for v in (0, 1):
                        delta = sub(mul_conj(p0[2 * a + u], q0[2 * b + v]), mul_conj(p1[2 * a + u], q1[2 * b + v]))
                        row = ((2 * a + b) * 4 + 2 * u + v) * 2
                        moved[i - low, row] = delta[0]
                        moved[i - low, row + 1] = delta[1]


def exchange(block, axis, mask):
    return lax.ppermute(block, axis, [(i, i ^ mask) for i in range(lax.axis_size(axis))])


def butterfly_sum(value, axis):
    mask = 1
    while mask < lax.axis_size(axis):
        value = value + exchange(value, axis, mask)
        mask *= 2
    return value


def chip_blocks(block, axis):
    chips = lax.axis_size(axis) // 2
    if chips <= 4:
        return jnp.stack([block] + [exchange(block, axis, 2 * j) for j in range(1, chips)])
    parts = block[None]
    while parts.shape[0] < chips:
        parts = jnp.concatenate([parts, exchange(parts, axis, 2 * parts.shape[0])], axis=0)
    return parts


def on_device(visibilities, coherencies, gain_offsets, stations, solve_order, counts, damping):
    groups = lax.axis_size("bl")
    owned, _, channel_count, baselines = coherencies.shape
    channels = visibilities.shape[1]
    width = gain_offsets.shape[2]
    count = groups * width
    tiles = baselines // 128
    params = pltpu.CompilerParams(vmem_limit_bytes=VMEM_BYTES)

    def call(kernel, name, shapes, scalars, arrays, scratch=(), **static):
        return pl.pallas_call(
            functools.partial(kernel, **static),
            out_shape=[jax.ShapeDtypeStruct(*shape) for shape in shapes],
            in_specs=[pl.BlockSpec(memory_space=pltpu.SMEM)] * len(scalars)
            + [pl.BlockSpec(memory_space=pltpu.VMEM)] * len(arrays),
            out_specs=[pl.BlockSpec(memory_space=pltpu.VMEM)] * len(shapes),
            scratch_shapes=[pltpu.VMEM(*shape) for shape in scratch],
            compiler_params=params,
            name=name,
        )(*scalars, *arrays)

    per = 128 // width
    part_rows = -(-(owned + SOLVED) // per) * 8
    block = coherencies.shape[1:]
    whole = lambda shape: pl.BlockSpec(shape, lambda g, order: (0,) * len(shape))
    picked = lambda i: pl.BlockSpec((1,) + block, lambda g, order: (order[i] % owned, 0, 0, 0))
    shapes = [(part_rows + 8, 128)] + [(high - low,) + block for low, high in GROUPS]
    packed, *chosen = pl.pallas_call(
        functools.partial(prep_kernel, owned=owned, per=per),
        out_shape=[jax.ShapeDtypeStruct(shape, dtype) for shape, dtype in zip(shapes, [F32] + [BF16] * len(GROUPS))],
        grid_spec=pltpu.PrefetchScalarGridSpec(
            num_scalar_prefetch=1,
            grid=(1,),
            in_specs=[whole(stations.shape), whole(gain_offsets.shape)] + [picked(i) for i in range(SOLVED)],
            out_specs=[whole(shape) for shape in shapes],
        ),
        compiler_params=pltpu.CompilerParams(vmem_limit_bytes=MOST_VMEM_BYTES),
        name="prepare",
    )(solve_order, stations, gain_offsets, *[coherencies] * SOLVED)

    near = chip_blocks(packed, "bl")
    blocks = jnp.stack([near, exchange(near, "bl", 1)], axis=1).reshape(groups, part_rows + 8, 128)
    shared = [butterfly_sum(value, "dir") for value in chosen]

    table = ((part_rows * per, count), F32)
    part, begin = call(
        model_kernel,
        "first_model",
        [((8, channel_count, baselines), F32), ((SOLVED * 8, 2 * baselines), F32)],
        [],
        [blocks, coherencies, visibilities],
        [table, ((part_rows * per, 2 * baselines), F32)],
        width=width,
    )
    chunks = groups * tiles
    hots, ends, start = call(
        lookup_kernel,
        "lookup",
        [((groups, count, 2 * baselines), BF16), ((SOLVED, 2, chunks * 8, 128), F32), ((SOLVED * 8, count), F32)],
        [],
        [blocks],
        [table],
        width=width,
        owned=owned,
    )
    first = butterfly_sum(part, "dir")
    res, own = call(
        own_kernel,
        "own_channels",
        [(visibilities.shape, F32), ((SOLVED, 8, channels, baselines), F32)],
        [],
        [first, *shared],
    )
    moved, solved = [], []
    flat = lambda near: [near.reshape(-1, 128), exchange(near, "bl", 1).reshape(-1, 128)]
    products = []
    for g, (low, high) in enumerate(GROUPS):
        rows = (high - low) * K_ROWS + len(pair_list(low, high)) * M_ROWS
        [value] = call(
            product_kernel, "products", [((tiles, rows, 128), F32)], [], shared[: g + 1], low=low, high=high
        )
        products += flat(chip_blocks(value, "bl"))
    for low, high in TARGETS:
        [value] = call(
            target_kernel,
            "targets",
            [((tiles, (high - low) * M_ROWS, 128), F32)],
            [],
            [first, begin] + shared,
            low=low,
            high=high,
        )
        targets = flat(chip_blocks(value, "bl"))
        last = high == SOLVED
        moved_shape = ((high - low, M_ROWS, chunks, 128), F32)
        outs = call(
            sweep_kernel,
            "sweep",
            [(gain_offsets.shape, F32), (visibilities.shape, F32)]
            if last
            else [((high - low, 8, count), F32), moved_shape, (visibilities.shape, F32)],
            [solve_order, counts, damping],
            [hots, ends, start, res, own]
            + targets
            + products
            + moved
            + (solved + [gain_offsets] if last else []),
            ([moved_shape] if last else [])
            + [
                ((2, chunks * 8, 128), F32),
                ((2, chunks * 16, 128), F32),
                ((8, count), F32),
                ((M_ROWS, chunks, 128), F32),
                ((K_ROWS, chunks, 128), F32),
            ],
            low=low,
            high=high,
            tiles=tiles,
            factor=baselines * groups * channel_count / count,
        )
        if not last:
            solved.append(outs[0])
            moved.append(outs[1])
            res = outs[2]
    return outs[0], outs[1]


def solution(mesh):
    return jax.shard_map(
        on_device,
        mesh=mesh,
        in_specs=(
            P(None, "dir", "bl"),
            P("dir", None, None, "bl"),
            P(None, None, "bl"),
            P(None, "bl"),
            P(),
            P(),
            P(),
        ),
        out_specs=(P(None, None, "bl"), P(None, "dir", "bl")),
        check_vma=False,
    )
```

```python
import functools

import jax
import jax.numpy as jnp
from jax import lax
from jax.experimental import pallas as pl
from jax.experimental.pallas import tpu as pltpu
from jax.sharding import PartitionSpec as P

LM_ITERS = 2
SOLVED = 4
F32 = jnp.float32
BF16 = jnp.bfloat16
VMEM_BYTES = 24 * 1024 * 1024
MOST_VMEM_BYTES = 60 * 1024 * 1024
GRAM = [(u, v) for u in range(4) for v in range(u, 4)]
M_ROWS = 32
K_ROWS = 16
GROUPS = [(0, 2), (2, 4)]
TARGETS = [(0, 4)]


def mul(x, y):
    return (x[0] * y[0] - x[1] * y[1], x[0] * y[1] + x[1] * y[0])


def add(x, y):
    return (x[0] + y[0], x[1] + y[1])


def sub(x, y):
    return (x[0] - y[0], x[1] - y[1])


def conj(x):
    return (x[0], -x[1])


def total(terms):
    return functools.reduce(add, terms)


def mul_conj(x, y):
    return (x[0] * y[0] + x[1] * y[1], x[1] * y[0] - x[0] * y[1])


def matmul(left, right):
    return [add(mul(left[2 * i], right[j]), mul(left[2 * i + 1], right[2 + j])) for i in (0, 1) for j in (0, 1)]


def matmul_adj(left, right):
    return [
        add(mul_conj(left[2 * i], right[2 * j]), mul_conj(left[2 * i + 1], right[2 * j + 1]))
        for i in (0, 1)
        for j in (0, 1)
    ]


def apply_gains(gain_p, coher, gain_q):
    return matmul_adj(matmul(gain_p, coher), gain_q)


def as_matrix(parts):
    return [(parts[2 * e], parts[2 * e + 1]) for e in range(4)]


def split_rows(values):
    high = values.astype(BF16)
    low = (values - high.astype(F32)).astype(BF16)
    return jnp.concatenate([high, low], axis=0)


def one_hot(stations_p, stations_q, count):
    both = jnp.concatenate([stations_p, stations_q], axis=1)
    rows = lax.broadcasted_iota(jnp.int32, (count, both.shape[1]), 0)
    return jnp.where(rows == both, 1.0, 0.0).astype(BF16)


def pick(one_hots, values):
    count = values.shape[0]
    out = jnp.dot(split_rows(values), one_hots, preferred_element_type=F32)
    return out[:count] + out[count:]


def prep_kernel(order_ref, stations_ref, offs_ref, *refs, owned, per):
    coher_refs, out_ref, chosen_refs = refs[:SOLVED], refs[SOLVED], refs[SOLVED + 1 :]
    lane = lax.axis_index("dir")
    width = offs_ref.shape[2]
    station_rows = 2 * stations_ref.shape[1] // 128
    part_rows = out_ref.shape[0] - 8
    comp = lax.broadcasted_iota(jnp.int32, (8, width), 0)
    ident = jnp.where((comp == 0) | (comp == 6), 1.0, 0.0)
    places = [lane * owned + d for d in range(owned)] + [order_ref[i] for i in range(SOLVED)]
    blocks = [offs_ref[place] + ident for place in places]
    while len(blocks) * 8 < part_rows * per:
        blocks.append(jnp.zeros((8, width), F32))
    each = part_rows // 8
    columns = [jnp.concatenate(blocks[q * each : (q + 1) * each], axis=0) for q in range(per)]
    out_ref[:part_rows] = jnp.concatenate(columns, axis=1)
    out_ref[part_rows:] = jnp.zeros((8, 128), F32)
    for row in range(station_rows):
        end, tile = row // (station_rows // 2), row % (station_rows // 2)
        out_ref[part_rows + row : part_rows + row + 1] = stations_ref[end : end + 1, tile * 128 : tile * 128 + 128].astype(F32)
    for i in range(SOLVED):
        mine = order_ref[i] // owned == lane
        [(low, ref)] = [(low, ref) for (low, high), ref in zip(GROUPS, chosen_refs) if low <= i < high]
        ref[i - low] = jnp.where(mine, coher_refs[i][0], jnp.zeros_like(coher_refs[i][0]))


def keep_kernel(one_ref, out_ref):
    out_ref[...] = one_ref[...]


def fill_table(blocks, table, width):
    rows, lanes = blocks[0].shape[1:]
    groups = 2 * blocks[0].shape[0]
    part_rows = rows - 8
    per = lanes // width
    lane_of = lax.broadcasted_iota(jnp.int32, (part_rows, lanes), 1) // width
    for tile in range(groups * width // lanes):
        for q in range(per):
            tile_rows = jnp.zeros((part_rows, lanes), F32)
            for u in range(per):
                j = per * tile + u
                block = blocks[j % 2][j // 2, :part_rows]
                shift = ((u - q) * width) % lanes
                if shift:
                    block = pltpu.roll(block, shift, 1)
                tile_rows = jnp.where(lane_of == u, block, tile_rows)
            table[q * part_rows : (q + 1) * part_rows, tile * lanes : (tile + 1) * lanes] = tile_rows


def block_stations(block, tiles, base):
    part_rows = block.shape[0] - 8
    rows = block[part_rows:, :].astype(jnp.int32) ^ base
    return [jnp.concatenate([rows[end * tiles + t : end * tiles + t + 1] for t in range(tiles)], axis=1) for end in (0, 1)]


def lookup_kernel(near_ref, far_ref, hots_ref, ends_ref, start_ref, table, *, width, owned):
    groups = hots_ref.shape[0]
    baselines = hots_ref.shape[2] // 2
    tiles = baselines // 128
    base = lax.axis_index("bl").astype(jnp.int32) * width
    fill_table([near_ref, far_ref], table, width)
    start = table[owned * 8 : (owned + SOLVED) * 8, :]
    start_ref[...] = start
    split = split_rows(start)
    for g in range(groups):
        half = groups // 2
        rows_p, rows_q = block_stations((near_ref, far_ref)[g // half].at[g % half], tiles, base)
        hots_ref[g] = one_hot(rows_p, rows_q, groups * width)
        out = jnp.dot(split, hots_ref[g], preferred_element_type=F32)
        out = out[: SOLVED * 8] + out[SOLVED * 8 :]
        for i in range(SOLVED):
            for end in (0, 1):
                for t in range(tiles):
                    chunk, column = (g * tiles + t) * 8, (end * tiles + t) * 128
                    ends_ref[i, end, chunk : chunk + 8, :] = out[i * 8 : i * 8 + 8, column : column + 128]


def model_kernel(near_ref, far_ref, coher_ref, vis_ref, part_ref, begin_ref, table, ends, *, width):
    owned = coher_ref.shape[0]
    baselines = coher_ref.shape[3]
    channels = vis_ref.shape[1]
    lane = lax.axis_index("dir")
    base = lax.axis_index("bl").astype(jnp.int32) * width
    fill_table([near_ref, far_ref], table, width)
    rows_p, rows_q = block_stations(near_ref.at[0], baselines // 128, base)
    ends[...] = pick(one_hot(rows_p, rows_q, table.shape[1]), table[...])
    begin_ref[...] = ends[owned * 8 : (owned + SOLVED) * 8, :]

    for half in range(baselines // 128):
        at = pl.ds(half * 128, 128)
        at_q = pl.ds(baselines + half * 128, 128)

        def gain(row, where):
            block = ends[pl.ds(pl.multiple_of(row, 8), 8), where]
            return as_matrix([block[c : c + 1] for c in range(8)])

        def add_model(d, acc):
            coher = as_matrix([coher_ref[d, c, :, at].astype(F32) for c in range(8)])
            model = apply_gains(gain(d * 8, at), coher, gain(d * 8, at_q))
            return [sub(x, y) for x, y in zip(acc, model)]

        zeros = jnp.zeros((coher_ref.shape[2], 128), F32)
        acc = lax.fori_loop(0, owned, add_model, [(zeros, zeros)] * 4)
        for c in range(8):
            total_part = acc[c // 2][c % 2]
            lanes = [total_part[x : x + channels] for x in range(0, total_part.shape[0], channels)]
            vis = vis_ref[c, :, at]
            part_ref[c, :, at] = jnp.concatenate([jnp.where(lane == x, y + vis, y) for x, y in enumerate(lanes)], axis=0)


def summed(values):
    return jnp.sum(values, axis=0, keepdims=True)


def pair_list(low, high):
    return [(m, i) for i in range(low, high) for m in range(i)]


def load_coher(refs, i, at):
    [(low, ref)] = [(low, ref) for (low, high), ref in zip(GROUPS, refs) if low <= i < high]
    return as_matrix([ref[i - low, c, :, at].astype(F32) for c in range(8)])


def target_kernel(first_ref, begin_ref, *refs, low, high):
    *solved_refs, out_ref = refs
    baselines = first_ref.shape[2]
    for half in range(baselines // 128):
        at = pl.ds(half * 128, 128)
        out = 0
        for i in range(low, high):
            coher = load_coher(solved_refs, i, at)
            gain_p, gain_q = [
                as_matrix([begin_ref[i * 8 + c : i * 8 + c + 1, pl.ds(end * baselines + half * 128, 128)] for c in range(8)])
                for end in (0, 1)
            ]
            model = apply_gains(gain_p, coher, gain_q)
            target = [(first_ref[2 * e, :, at] + model[e][0], first_ref[2 * e + 1, :, at] + model[e][1]) for e in range(4)]
            for u in range(4):
                for v in range(4):
                    value = mul_conj(target[u], coher[v])
                    out_ref[half, out : out + 1, :] = summed(value[0])
                    out_ref[half, out + 1 : out + 2, :] = summed(value[1])
                    out += 2


def product_kernel(*refs, low, high):
    *solved_refs, out_ref = refs
    for half in range(out_ref.shape[0]):
        at = pl.ds(half * 128, 128)
        out = 0
        for i in range(low, high):
            coher = load_coher(solved_refs, i, at)
            for u, v in GRAM:
                value = mul_conj(coher[u], coher[v])
                out_ref[half, out : out + 1, :] = summed(value[0])
                out += 1
                if u != v:
                    out_ref[half, out : out + 1, :] = summed(value[1])
                    out += 1
        for m, i in pair_list(low, high):
            coher, other = load_coher(solved_refs, i, at), load_coher(solved_refs, m, at)
            for u in range(4):
                for v in range(4):
                    value = mul_conj(other[u], coher[v])
                    out_ref[half, out : out + 1, :] = summed(value[0])
                    out_ref[half, out + 1 : out + 2, :] = summed(value[1])
                    out += 2


def own_kernel(first_ref, *refs):
    *solved_refs, res_ref, own_ref = refs
    channels = res_ref.shape[1]
    lane = lax.axis_index("dir")

    def select(value):
        mine = value[:channels]
        for x in range(1, value.shape[0] // channels):
            mine = jnp.where(lane == x, value[x * channels : (x + 1) * channels], mine)
        return mine

    for c in range(8):
        res_ref[c] = select(first_ref[c])
        for (low, high), solved_ref in zip(GROUPS, solved_refs):
            for i in range(low, high):
                own_ref[i, c] = select(solved_ref[i - low, c].astype(F32))


def sweep_kernel(order_ref, counts_ref, damping_ref, *refs, low, high, tiles, factor):
    last = high == SOLVED
    hots, begin, start_ref, res_ref, own_ref = refs[:5]
    targets, refs = refs[5:7], refs[7:]
    pair, refs = refs[:2], refs[2:]
    ends, values, state, m_now, k_now = refs[-5:]
    refs = refs[:-5]
    stages = [stage for stage in TARGETS if stage[1] <= low]
    earlier_moved = {m: (refs[s], m - stage[0]) for s, stage in enumerate(stages) for m in range(*stage)}
    refs = refs[len(stages) :]
    if last:
        earlier_gains = {m: (refs[s], m - stage[0]) for s, stage in enumerate(stages) for m in range(*stage)}
        offs_ref, gains_ref, out_ref, moved = refs[len(stages) :]
    else:
        solved_ref, moved, out_ref = refs
    groups, count = hots.shape[:2]
    chunks = groups * tiles

    def rows_at(pair, row):
        stride = pair[0].shape[0] // (chunks // 2)
        return jnp.concatenate([ref[pl.ds(row, chunks // 2, stride=stride), :] for ref in pair], axis=0)

    def fetch(gain_now, only=None):
        split = split_rows(gain_now)
        for g in range(groups if only is None else only):
            out = jnp.dot(split, hots[g], preferred_element_type=F32)
            out = out[:8] + out[8:]
            for end in (0, 1):
                for t in range(tiles):
                    chunk, column = (g * tiles + t) * 8, (end * tiles + t) * 128
                    ends[end, chunk : chunk + 8, :] = out[:, column : column + 128]

    def gain_at(ref):
        return [as_matrix([ref[end, pl.ds(c, chunks, stride=8), :] for c in range(8)]) for end in (0, 1)]

    def load_m():
        return [[(m_now[(u * 4 + v) * 2], m_now[(u * 4 + v) * 2 + 1]) for v in range(4)] for u in range(4)]

    def load_k():
        row = 0
        gram = {}
        for u, v in GRAM:
            if u == v:
                gram[u, v] = (k_now[row], None)
                row += 1
            else:
                gram[u, v] = (k_now[row], k_now[row + 1])
                gram[v, u] = conj(gram[u, v])
                row += 2
        return gram

    def prepare(i):
        for row in range(K_ROWS):
            k_now[row] = rows_at(pair, i * K_ROWS + row)
        for w in range(4):
            value = []
            for out in range(4):
                row = (i - low) * M_ROWS + (out * 4 + w) * 2
                value.append((rows_at(targets, row), rows_at(targets, row + 1)))
            for m in range(i):
                base = SOLVED * K_ROWS + pair_list(0, SOLVED).index((m, i)) * M_ROWS
                ref, place = (moved, m - low) if m >= low else earlier_moved[m]
                for uv in range(4):
                    at = base + (uv * 4 + w) * 2
                    cross = (rows_at(pair, at), rows_at(pair, at + 1))
                    for out in range(4):
                        row = (out * 4 + uv) * 2
                        value[out] = add(value[out], mul((ref[place, row], ref[place, row + 1]), cross))
            for out in range(4):
                m_now[(out * 4 + w) * 2] = value[out][0]
                m_now[(out * 4 + w) * 2 + 1] = value[out][1]

    def hermitian(gain):
        a = gain[0][0] ** 2 + gain[0][1] ** 2 + gain[2][0] ** 2 + gain[2][1] ** 2
        d = gain[1][0] ** 2 + gain[1][1] ** 2 + gain[3][0] ** 2 + gain[3][1] ** 2
        cross = add(mul_conj(gain[1], gain[0]), mul_conj(gain[3], gain[2]))
        return a, d, cross

    def normal_terms():
        gain_p, gain_q = gain_at(ends)
        m = load_m()
        k = load_k()
        for end, gain, other in ((0, gain_q, False), (1, gain_p, True)):
            row = 0
            for r in (0, 1):
                for c in (0, 1):
                    if other:
                        terms = [mul_conj(gain[2 * a + b], m[2 * a + r][2 * b + c]) for a in (0, 1) for b in (0, 1)]
                    else:
                        terms = [mul(gain[2 * a + b], m[2 * r + a][2 * c + b]) for a in (0, 1) for b in (0, 1)]
                    value = total(terms)
                    values[end, pl.ds(row, chunks, stride=16), :] = value[0]
                    values[end, pl.ds(row + 1, chunks, stride=16), :] = value[1]
                    row += 2
            a, d, cross = hermitian(gain)
            for r, c in ((0, 0), (1, 1), (0, 1)):
                if other:
                    kk = [[k[2 * x + r, 2 * y + c] for y in (0, 1)] for x in (0, 1)]
                    kk = [[(z[0], None if z[1] is None else -z[1]) for z in line] for line in kk]
                else:
                    kk = [[k[2 * r + x, 2 * c + y] for y in (0, 1)] for x in (0, 1)]
                real = a * kk[0][0][0] + d * kk[1][1][0]
                real += cross[0] * (kk[0][1][0] + kk[1][0][0])
                minus = None
                if kk[0][1][1] is not None:
                    minus = kk[1][0][1] - kk[0][1][1]
                    real += cross[1] * minus
                values[end, pl.ds(row, chunks, stride=16), :] = real
                row += 1
                if r != c:
                    imag = cross[1] * (kk[0][1][0] - kk[1][0][0])
                    if kk[0][0][1] is not None:
                        imag += a * kk[0][0][1]
                    if kk[1][1][1] is not None:
                        imag += d * kk[1][1][1]
                    if kk[0][1][1] is not None:
                        imag += cross[0] * kk[0][1][1]
                    if kk[1][0][1] is not None:
                        imag += cross[0] * kk[1][0][1]
                    values[end, pl.ds(row, chunks, stride=16), :] = imag
                    row += 1

    def station_sums():
        acc = jnp.zeros((32, count), F32)
        for g in range(groups):
            starts = [(end, (g * tiles + t) * 16) for end in (0, 1) for t in range(tiles)]
            split = split_rows(jnp.concatenate([values[end, at : at + 16, :] for end, at in starts], axis=1))
            acc += lax.dot_general(split, hots[g], (((1,), (1,)), ((), ())), preferred_element_type=F32)
        return acc[:16] + acc[16:]

    def solve(sums, gain_now, damp):
        numer = sums[:8] + damp * gain_now
        numer = as_matrix([numer[c : c + 1] for c in range(8)])
        diag_a = sums[8:9] + damp
        diag_d = sums[9:10] + damp
        cross_r = sums[10:11]
        cross_i = sums[11:12]
        scale = 1.0 / (diag_a * diag_d - cross_r * cross_r - cross_i * cross_i)
        rows = []
        for r in (0, 1):
            x, y = numer[2 * r], numer[2 * r + 1]
            low = mul(y, (cross_r, -cross_i))
            high = mul(x, (cross_r, cross_i))
            rows += [x[0] * diag_d - low[0], x[1] * diag_d - low[1]]
            rows += [y[0] * diag_a - high[0], y[1] * diag_a - high[1]]
        return jnp.concatenate([value * scale for value in rows], axis=0)

    def add_change(i):
        for tile in range(tiles):
            at = pl.ds(tile * 128, 128)
            coher = as_matrix([own_ref[i, c, :, at] for c in range(8)])
            rows = [tile * 8 + c for c in range(8)]
            one = [as_matrix([begin[i, end, row : row + 1, :] for row in rows]) for end in (0, 1)]
            two = [as_matrix([ends[end, row : row + 1, :] for row in rows]) for end in (0, 1)]
            before, now = apply_gains(one[0], coher, one[1]), apply_gains(two[0], coher, two[1])
            for e in range(4):
                change = sub(before[e], now[e])
                out_ref[2 * e, :, at] += change[0]
                out_ref[2 * e + 1, :, at] += change[1]

    out_ref[...] = res_ref[...]
    if last:
        width = offs_ref.shape[2]
        comp = lax.broadcasted_iota(jnp.int32, (8, width), 0)
        gains_ref[...] = offs_ref[...] + jnp.where((comp == 0) | (comp == 6), 1.0, 0.0)[None]
        for i in range(low):
            ref, place = earlier_gains[i]
            gains_ref[order_ref[i]] = ref[place, :, :width]
    values[...] = jnp.zeros(values.shape, F32)
    for i in range(low, high):
        which = order_ref[i]
        damp = damping_ref[which].astype(F32) * factor
        state[...] = start_ref[i * 8 : i * 8 + 8, :]
        ends[...] = begin[i]
        prepare(i)

        def one_round():
            normal_terms()
            state[...] = solve(station_sums(), state[...], damp)

        def more(r, carry):
            one_round()
            fetch(state[...])
            return carry

        lax.fori_loop(0, jnp.minimum(counts_ref[which], LM_ITERS) - 1, more, jnp.int32(0))
        one_round()
        fetch(state[...], 1 if i + 1 == SOLVED else None)
        if last:
            gains_ref[which] = state[:, :width]
        else:
            solved_ref[i - low] = state[...]
        add_change(i)
        if i + 1 == SOLVED:
            break
        p0, q0 = gain_at(begin.at[i])
        p1, q1 = gain_at(ends)
        for a in (0, 1):
            for b in (0, 1):
                for u in (0, 1):
                    for v in (0, 1):
                        delta = sub(mul_conj(p0[2 * a + u], q0[2 * b + v]), mul_conj(p1[2 * a + u], q1[2 * b + v]))
                        row = ((2 * a + b) * 4 + 2 * u + v) * 2
                        moved[i - low, row] = delta[0]
                        moved[i - low, row + 1] = delta[1]


def exchange(block, axis, mask):
    return lax.ppermute(block, axis, [(i, i ^ mask) for i in range(lax.axis_size(axis))])


def butterfly_sums(value, axis):
    sums = [value]
    while 1 << (len(sums) - 1) < lax.axis_size(axis):
        sums.append(sums[-1] + exchange(sums[-1], axis, 1 << (len(sums) - 1)))
    return sums


def chip_blocks(block, axis):
    chips = lax.axis_size(axis) // 2
    if chips <= 4:
        return jnp.stack([block] + [exchange(block, axis, 2 * j) for j in range(1, chips)])
    parts = block[None]
    while parts.shape[0] < chips:
        parts = jnp.concatenate([parts, exchange(parts, axis, 2 * parts.shape[0])], axis=0)
    return parts


def on_device(visibilities, coherencies, gain_offsets, stations, solve_order, counts, damping):
    groups = lax.axis_size("bl")
    owned, _, channel_count, baselines = coherencies.shape
    channels = visibilities.shape[1]
    width = gain_offsets.shape[2]
    count = groups * width
    tiles = baselines // 128
    params = pltpu.CompilerParams(vmem_limit_bytes=VMEM_BYTES)

    def call(kernel, name, shapes, scalars, arrays, scratch=(), after=(), **static):
        first, skip = len(scalars) + len(arrays), len(after)

        def body(*refs):
            kernel(*refs[:first], *refs[first + skip :], **static)

        return pl.pallas_call(
            body,
            out_shape=[jax.ShapeDtypeStruct(*shape) for shape in shapes],
            in_specs=[pl.BlockSpec(memory_space=pltpu.SMEM)] * len(scalars)
            + [pl.BlockSpec(memory_space=pltpu.VMEM)] * len(arrays)
            + [pl.BlockSpec(memory_space=pl.ANY)] * skip,
            out_specs=[pl.BlockSpec(memory_space=pltpu.VMEM)] * len(shapes),
            scratch_shapes=[pltpu.VMEM(*shape) for shape in scratch],
            compiler_params=params,
            name=name,
        )(*scalars, *arrays, *after)

    per = 128 // width
    part_rows = -(-(owned + SOLVED) // per) * 8
    block = coherencies.shape[1:]
    whole = lambda shape: pl.BlockSpec(shape, lambda g, order: (0,) * len(shape))
    picked = lambda i: pl.BlockSpec((1,) + block, lambda g, order: (order[i] % owned, 0, 0, 0))
    shapes = [(part_rows + 8, 128)] + [(high - low,) + block for low, high in GROUPS]
    packed, *chosen = pl.pallas_call(
        functools.partial(prep_kernel, owned=owned, per=per),
        out_shape=[jax.ShapeDtypeStruct(shape, dtype) for shape, dtype in zip(shapes, [F32] + [BF16] * len(GROUPS))],
        grid_spec=pltpu.PrefetchScalarGridSpec(
            num_scalar_prefetch=1,
            grid=(1,),
            in_specs=[whole(stations.shape), whole(gain_offsets.shape)] + [picked(i) for i in range(SOLVED)],
            out_specs=[whole(shape) for shape in shapes],
        ),
        compiler_params=pltpu.CompilerParams(vmem_limit_bytes=MOST_VMEM_BYTES),
        name="prepare",
    )(solve_order, stations, gain_offsets, *[coherencies] * SOLVED)

    near = chip_blocks(packed, "bl")
    blocks = [near, exchange(near, "bl", 1)]
    shared = [butterfly_sums(value, "dir")[-1] for value in chosen]

    table = ((part_rows * per, count), F32)
    part, begin = call(
        model_kernel,
        "first_model",
        [((8, channel_count, baselines), F32), ((SOLVED * 8, 2 * baselines), F32)],
        [],
        blocks + [coherencies, visibilities],
        [table, ((part_rows * per, 2 * baselines), F32)],
        width=width,
    )
    chunks = groups * tiles
    hots, ends, start = call(
        lookup_kernel,
        "lookup",
        [((groups, count, 2 * baselines), BF16), ((SOLVED, 2, chunks * 8, 128), F32), ((SOLVED * 8, count), F32)],
        [],
        blocks,
        [table],
        width=width,
        owned=owned,
        after=[part],
    )
    partials = butterfly_sums(part, "dir")
    first = partials[-1]
    res, own = call(
        own_kernel,
        "own_channels",
        [(visibilities.shape, F32), ((SOLVED, 8, channels, baselines), F32)],
        [],
        [first, *shared],
    )
    moved, solved = [], []
    flat = lambda near: [near.reshape(-1, 128), exchange(near, "bl", 1).reshape(-1, 128)]
    rows = SOLVED * K_ROWS + len(pair_list(0, SOLVED)) * M_ROWS
    [value] = call(
        product_kernel, "products", [((tiles, rows, 128), F32)], [], shared, after=[part], low=0, high=SOLVED
    )
    kx_near = chip_blocks(value, "bl")
    for low, high in TARGETS:
        [value] = call(
            target_kernel,
            "targets",
            [((tiles, (high - low) * M_ROWS, 128), F32)],
            [],
            [first, begin] + shared,
            low=low,
            high=high,
            after=[value],
        )
        [kx_near] = call(keep_kernel, "keep", [(kx_near.shape, F32)], [], [kx_near], after=[value])
        products = flat(kx_near)
        targets = flat(chip_blocks(value, "bl"))
        last = high == SOLVED
        moved_shape = ((high - low, M_ROWS, chunks, 128), F32)
        outs = call(
            sweep_kernel,
            "sweep",
            [(gain_offsets.shape, F32), (visibilities.shape, F32)]
            if last
            else [((high - low, 8, count), F32), moved_shape, (visibilities.shape, F32)],
            [solve_order, counts, damping],
            [hots, ends, start, res, own]
            + targets
            + products
            + moved
            + (solved + [gain_offsets] if last else []),
            ([moved_shape] if last else [])
            + [
                ((2, chunks * 8, 128), F32),
                ((2, chunks * 16, 128), F32),
                ((8, count), F32),
                ((M_ROWS, chunks, 128), F32),
                ((K_ROWS, chunks, 128), F32),
            ],
            low=low,
            high=high,
            tiles=tiles,
            factor=baselines * groups * channel_count / count,
        )
        if not last:
            solved.append(outs[0])
            moved.append(outs[1])
            res = outs[2]
    return outs[0], outs[1]


def solution(mesh):
    return jax.shard_map(
        on_device,
        mesh=mesh,
        in_specs=(
            P(None, "dir", "bl"),
            P("dir", None, None, "bl"),
            P(None, None, "bl"),
            P(None, "bl"),
            P(),
            P(),
            P(),
        ),
        out_specs=(P(None, None, "bl"), P(None, "dir", "bl")),
        check_vma=False,
    )
```

```python
import functools

import jax
import jax.numpy as jnp
from jax import lax
from jax.experimental import pallas as pl
from jax.experimental.pallas import tpu as pltpu
from jax.sharding import PartitionSpec as P

LM_ITERS = 2
SOLVED = 4
F32 = jnp.float32
BF16 = jnp.bfloat16
VMEM_BYTES = 24 * 1024 * 1024
MOST_VMEM_BYTES = 60 * 1024 * 1024
GRAM = [(u, v) for u in range(4) for v in range(u, 4)]
M_ROWS = 32
K_ROWS = 16
GROUPS = [(0, 2), (2, 4)]
TARGETS = [(0, 4)]


def mul(x, y):
    return (x[0] * y[0] - x[1] * y[1], x[0] * y[1] + x[1] * y[0])


def add(x, y):
    return (x[0] + y[0], x[1] + y[1])


def sub(x, y):
    return (x[0] - y[0], x[1] - y[1])


def conj(x):
    return (x[0], -x[1])


def total(terms):
    return functools.reduce(add, terms)


def mul_conj(x, y):
    return (x[0] * y[0] + x[1] * y[1], x[1] * y[0] - x[0] * y[1])


def matmul(left, right):
    return [add(mul(left[2 * i], right[j]), mul(left[2 * i + 1], right[2 + j])) for i in (0, 1) for j in (0, 1)]


def matmul_adj(left, right):
    return [
        add(mul_conj(left[2 * i], right[2 * j]), mul_conj(left[2 * i + 1], right[2 * j + 1]))
        for i in (0, 1)
        for j in (0, 1)
    ]


def apply_gains(gain_p, coher, gain_q):
    return matmul_adj(matmul(gain_p, coher), gain_q)


def as_matrix(parts):
    return [(parts[2 * e], parts[2 * e + 1]) for e in range(4)]


def split_rows(values):
    high = values.astype(BF16)
    low = (values - high.astype(F32)).astype(BF16)
    return jnp.concatenate([high, low], axis=0)


def one_hot(stations_p, stations_q, count):
    both = jnp.concatenate([stations_p, stations_q], axis=1)
    rows = lax.broadcasted_iota(jnp.int32, (count, both.shape[1]), 0)
    return jnp.where(rows == both, 1.0, 0.0).astype(BF16)


def pick(one_hots, values):
    count = values.shape[0]
    out = jnp.dot(split_rows(values), one_hots, preferred_element_type=F32)
    return out[:count] + out[count:]


def prep_kernel(order_ref, stations_ref, offs_ref, *refs, owned, per):
    coher_refs, out_ref, chosen_refs = refs[:SOLVED], refs[SOLVED], refs[SOLVED + 1 :]
    lane = lax.axis_index("dir")
    width = offs_ref.shape[2]
    station_rows = 2 * stations_ref.shape[1] // 128
    part_rows = out_ref.shape[0] - 8
    comp = lax.broadcasted_iota(jnp.int32, (8, width), 0)
    ident = jnp.where((comp == 0) | (comp == 6), 1.0, 0.0)
    places = [lane * owned + d for d in range(owned)] + [order_ref[i] for i in range(SOLVED)]
    blocks = [offs_ref[place] + ident for place in places]
    while len(blocks) * 8 < part_rows * per:
        blocks.append(jnp.zeros((8, width), F32))
    each = part_rows // 8
    columns = [jnp.concatenate(blocks[q * each : (q + 1) * each], axis=0) for q in range(per)]
    out_ref[:part_rows] = jnp.concatenate(columns, axis=1)
    out_ref[part_rows:] = jnp.zeros((8, 128), F32)
    for row in range(station_rows):
        end, tile = row // (station_rows // 2), row % (station_rows // 2)
        out_ref[part_rows + row : part_rows + row + 1] = stations_ref[end : end + 1, tile * 128 : tile * 128 + 128].astype(F32)
    for i in range(SOLVED):
        mine = order_ref[i] // owned == lane
        [(low, ref)] = [(low, ref) for (low, high), ref in zip(GROUPS, chosen_refs) if low <= i < high]
        ref[i - low] = jnp.where(mine, coher_refs[i][0], jnp.zeros_like(coher_refs[i][0]))


def keep_kernel(one_ref, out_ref):
    out_ref[...] = one_ref[...]


def fill_table(blocks, table, width):
    rows, lanes = blocks[0].shape[1:]
    groups = 2 * blocks[0].shape[0]
    part_rows = rows - 8
    per = lanes // width
    lane_of = lax.broadcasted_iota(jnp.int32, (part_rows, lanes), 1) // width
    for tile in range(groups * width // lanes):
        for q in range(per):
            tile_rows = jnp.zeros((part_rows, lanes), F32)
            for u in range(per):
                j = per * tile + u
                block = blocks[j % 2][j // 2, :part_rows]
                shift = ((u - q) * width) % lanes
                if shift:
                    block = pltpu.roll(block, shift, 1)
                tile_rows = jnp.where(lane_of == u, block, tile_rows)
            table[q * part_rows : (q + 1) * part_rows, tile * lanes : (tile + 1) * lanes] = tile_rows


def block_stations(block, tiles, base):
    part_rows = block.shape[0] - 8
    rows = block[part_rows:, :].astype(jnp.int32) ^ base
    return [jnp.concatenate([rows[end * tiles + t : end * tiles + t + 1] for t in range(tiles)], axis=1) for end in (0, 1)]


def fetch_columns(rows, hots, part, at):
    count = rows.shape[0]
    parts = rows.shape[1] // 128
    wide = jnp.concatenate([rows[:, w * 128 : w * 128 + 128] for w in range(parts)], axis=0)
    out = jnp.dot(split_rows(wide), hots[:, at], preferred_element_type=F32)
    out = out[: parts * count] + out[parts * count :]
    which = jnp.concatenate([part[:, at]] * (count // 8), axis=0)
    value = out[:count]
    for w in range(1, parts):
        value = jnp.where(which == w, out[w * count : w * count + count], value)
    return value


def lookup_kernel(near_ref, far_ref, hots_ref, turned_ref, part_ref, ends_ref, start_ref, table, *, width, owned, tiles):
    half = near_ref.shape[0]
    chunks = 2 * half * tiles
    base = lax.axis_index("bl").astype(jnp.int32) * width
    fill_table([near_ref, far_ref], table, width)
    start = table[owned * 8 : (owned + SOLVED) * 8, :]
    start_ref[...] = start
    pairs = [block_stations(ref.at[j], tiles, base) for ref in (near_ref, far_ref) for j in range(half)]
    step = min(8, chunks)
    for end in (0, 1):
        rows = jnp.concatenate([pair[end] for pair in pairs], axis=1)
        for first in range(0, chunks, step):
            at = pl.ds((end * chunks + first) * 128, step * 128)
            here = rows[:, first * 128 : (first + step) * 128]
            index = lax.broadcasted_iota(jnp.int32, (128, step * 128), 0)
            hot = jnp.where(index == (here & 127), 1.0, 0.0)
            hots_ref[:, at] = hot.astype(BF16)
            turned_ref[at, :] = jnp.transpose(hot).astype(BF16)
            part_ref[:, at] = jnp.broadcast_to(here >> 7, (8, step * 128))
            out = fetch_columns(start, hots_ref, part_ref, at)
            for i in range(SOLVED):
                for t in range(step):
                    ends_ref[i, end, (first + t) * 8 : (first + t) * 8 + 8, :] = out[i * 8 : i * 8 + 8, t * 128 : t * 128 + 128]


def model_kernel(near_ref, far_ref, coher_ref, vis_ref, part_ref, begin_ref, table, ends, *, width):
    owned = coher_ref.shape[0]
    baselines = coher_ref.shape[3]
    channels = vis_ref.shape[1]
    lane = lax.axis_index("dir")
    base = lax.axis_index("bl").astype(jnp.int32) * width
    fill_table([near_ref, far_ref], table, width)
    rows_p, rows_q = block_stations(near_ref.at[0], baselines // 128, base)
    ends[...] = pick(one_hot(rows_p, rows_q, table.shape[1]), table[...])
    begin_ref[...] = ends[owned * 8 : (owned + SOLVED) * 8, :]

    for half in range(baselines // 128):
        at = pl.ds(half * 128, 128)
        at_q = pl.ds(baselines + half * 128, 128)

        def gain(row, where):
            block = ends[pl.ds(pl.multiple_of(row, 8), 8), where]
            return as_matrix([block[c : c + 1] for c in range(8)])

        def add_model(d, acc):
            coher = as_matrix([coher_ref[d, c, :, at].astype(F32) for c in range(8)])
            model = apply_gains(gain(d * 8, at), coher, gain(d * 8, at_q))
            return [sub(x, y) for x, y in zip(acc, model)]

        zeros = jnp.zeros((coher_ref.shape[2], 128), F32)
        acc = lax.fori_loop(0, owned, add_model, [(zeros, zeros)] * 4)
        for c in range(8):
            total_part = acc[c // 2][c % 2]
            lanes = [total_part[x : x + channels] for x in range(0, total_part.shape[0], channels)]
            vis = vis_ref[c, :, at]
            part_ref[c, :, at] = jnp.concatenate([jnp.where(lane == x, y + vis, y) for x, y in enumerate(lanes)], axis=0)


def summed(values):
    return jnp.sum(values, axis=0, keepdims=True)


def pair_list(low, high):
    return [(m, i) for i in range(low, high) for m in range(i)]


def load_coher(refs, i, at):
    [(low, ref)] = [(low, ref) for (low, high), ref in zip(GROUPS, refs) if low <= i < high]
    return as_matrix([ref[i - low, c, :, at].astype(F32) for c in range(8)])


def target_kernel(first_ref, begin_ref, *refs, low, high):
    *solved_refs, out_ref = refs
    baselines = first_ref.shape[2]
    for half in range(baselines // 128):
        at = pl.ds(half * 128, 128)
        out = 0
        for i in range(low, high):
            coher = load_coher(solved_refs, i, at)
            gain_p, gain_q = [
                as_matrix([begin_ref[i * 8 + c : i * 8 + c + 1, pl.ds(end * baselines + half * 128, 128)] for c in range(8)])
                for end in (0, 1)
            ]
            model = apply_gains(gain_p, coher, gain_q)
            target = [(first_ref[2 * e, :, at] + model[e][0], first_ref[2 * e + 1, :, at] + model[e][1]) for e in range(4)]
            for u in range(4):
                for v in range(4):
                    value = mul_conj(target[u], coher[v])
                    out_ref[half, out : out + 1, :] = summed(value[0])
                    out_ref[half, out + 1 : out + 2, :] = summed(value[1])
                    out += 2


def product_kernel(*refs, low, high):
    *solved_refs, out_ref = refs
    for half in range(out_ref.shape[0]):
        at = pl.ds(half * 128, 128)
        out = 0
        for i in range(low, high):
            coher = load_coher(solved_refs, i, at)
            for u, v in GRAM:
                value = mul_conj(coher[u], coher[v])
                out_ref[half, out : out + 1, :] = summed(value[0])
                out += 1
                if u != v:
                    out_ref[half, out : out + 1, :] = summed(value[1])
                    out += 1
        for m, i in pair_list(low, high):
            coher, other = load_coher(solved_refs, i, at), load_coher(solved_refs, m, at)
            for u in range(4):
                for v in range(4):
                    value = mul_conj(other[u], coher[v])
                    out_ref[half, out : out + 1, :] = summed(value[0])
                    out_ref[half, out + 1 : out + 2, :] = summed(value[1])
                    out += 2


def own_kernel(offs_ref, first_ref, *refs):
    *solved_refs, res_ref, own_ref, gains_ref = refs
    channels = res_ref.shape[1]
    comp = lax.broadcasted_iota(jnp.int32, offs_ref.shape[1:], 0)
    gains_ref[...] = offs_ref[...] + jnp.where((comp == 0) | (comp == 6), 1.0, 0.0)[None]
    lane = lax.axis_index("dir")

    def select(value):
        mine = value[:channels]
        for x in range(1, value.shape[0] // channels):
            mine = jnp.where(lane == x, value[x * channels : (x + 1) * channels], mine)
        return mine

    for c in range(8):
        res_ref[c] = select(first_ref[c])
        for (low, high), solved_ref in zip(GROUPS, solved_refs):
            for i in range(low, high):
                own_ref[i, c] = select(solved_ref[i - low, c].astype(F32))


def sweep_kernel(order_ref, counts_ref, damping_ref, *refs, low, high, tiles, factor):
    last = high == SOLVED
    hots, turned, part, begin, start_ref, res_ref, own_ref = refs[:7]
    targets, refs = refs[7:9], refs[9:]
    pair, refs = refs[:2], refs[2:]
    ends, values, state, m_now, k_now = refs[-5:]
    refs = refs[:-5]
    stages = [stage for stage in TARGETS if stage[1] <= low]
    earlier_moved = {m: (refs[s], m - stage[0]) for s, stage in enumerate(stages) for m in range(*stage)}
    refs = refs[len(stages) :]
    if last:
        earlier_gains = {m: (refs[s], m - stage[0]) for s, stage in enumerate(stages) for m in range(*stage)}
        start_own, gains_ref, out_ref, moved = refs[len(stages) :]
    else:
        solved_ref, moved, out_ref = refs
    chunks = hots.shape[1] // 256
    parts = start_ref.shape[1] // 128

    def rows_at(pair, row):
        stride = pair[0].shape[0] // (chunks // 2)
        return jnp.concatenate([ref[pl.ds(row, chunks // 2, stride=stride), :] for ref in pair], axis=0)

    def fetch(gain_now, only=None):
        step = min(8, chunks) if only is None else only
        for end in (0, 1):
            for first in range(0, chunks if only is None else only, step):
                at = pl.ds((end * chunks + first) * 128, step * 128)
                out = fetch_columns(gain_now, hots, part, at)
                for t in range(step):
                    ends[end, (first + t) * 8 : (first + t) * 8 + 8, :] = out[:, t * 128 : t * 128 + 128]

    def gain_at(ref):
        return [as_matrix([ref[end, pl.ds(c, chunks, stride=8), :] for c in range(8)]) for end in (0, 1)]

    def load_m():
        return [[(m_now[(u * 4 + v) * 2], m_now[(u * 4 + v) * 2 + 1]) for v in range(4)] for u in range(4)]

    def load_k():
        row = 0
        gram = {}
        for u, v in GRAM:
            if u == v:
                gram[u, v] = (k_now[row], None)
                row += 1
            else:
                gram[u, v] = (k_now[row], k_now[row + 1])
                gram[v, u] = conj(gram[u, v])
                row += 2
        return gram

    def prepare(i):
        for row in range(K_ROWS):
            k_now[row] = rows_at(pair, i * K_ROWS + row)
        for w in range(4):
            value = []
            for out in range(4):
                row = (i - low) * M_ROWS + (out * 4 + w) * 2
                value.append((rows_at(targets, row), rows_at(targets, row + 1)))
            for m in range(i):
                base = SOLVED * K_ROWS + pair_list(0, SOLVED).index((m, i)) * M_ROWS
                ref, place = (moved, m - low) if m >= low else earlier_moved[m]
                for uv in range(4):
                    at = base + (uv * 4 + w) * 2
                    cross = (rows_at(pair, at), rows_at(pair, at + 1))
                    for out in range(4):
                        row = (out * 4 + uv) * 2
                        value[out] = add(value[out], mul((ref[place, row], ref[place, row + 1]), cross))
            for out in range(4):
                m_now[(out * 4 + w) * 2] = value[out][0]
                m_now[(out * 4 + w) * 2 + 1] = value[out][1]

    def hermitian(gain):
        a = gain[0][0] ** 2 + gain[0][1] ** 2 + gain[2][0] ** 2 + gain[2][1] ** 2
        d = gain[1][0] ** 2 + gain[1][1] ** 2 + gain[3][0] ** 2 + gain[3][1] ** 2
        cross = add(mul_conj(gain[1], gain[0]), mul_conj(gain[3], gain[2]))
        return a, d, cross

    def normal_terms():
        gain_p, gain_q = gain_at(ends)
        m = load_m()
        k = load_k()
        for end, gain, other in ((0, gain_q, False), (1, gain_p, True)):
            row = 0
            for r in (0, 1):
                for c in (0, 1):
                    if other:
                        terms = [mul_conj(gain[2 * a + b], m[2 * a + r][2 * b + c]) for a in (0, 1) for b in (0, 1)]
                    else:
                        terms = [mul(gain[2 * a + b], m[2 * r + a][2 * c + b]) for a in (0, 1) for b in (0, 1)]
                    value = total(terms)
                    values[end, pl.ds(row, chunks, stride=16), :] = value[0]
                    values[end, pl.ds(row + 1, chunks, stride=16), :] = value[1]
                    row += 2
            a, d, cross = hermitian(gain)
            for r, c in ((0, 0), (1, 1), (0, 1)):
                if other:
                    kk = [[k[2 * x + r, 2 * y + c] for y in (0, 1)] for x in (0, 1)]
                    kk = [[(z[0], None if z[1] is None else -z[1]) for z in line] for line in kk]
                else:
                    kk = [[k[2 * r + x, 2 * c + y] for y in (0, 1)] for x in (0, 1)]
                real = a * kk[0][0][0] + d * kk[1][1][0]
                real += cross[0] * (kk[0][1][0] + kk[1][0][0])
                minus = None
                if kk[0][1][1] is not None:
                    minus = kk[1][0][1] - kk[0][1][1]
                    real += cross[1] * minus
                values[end, pl.ds(row, chunks, stride=16), :] = real
                row += 1
                if r != c:
                    imag = cross[1] * (kk[0][1][0] - kk[1][0][0])
                    if kk[0][0][1] is not None:
                        imag += a * kk[0][0][1]
                    if kk[1][1][1] is not None:
                        imag += d * kk[1][1][1]
                    if kk[0][1][1] is not None:
                        imag += cross[0] * kk[0][1][1]
                    if kk[1][0][1] is not None:
                        imag += cross[0] * kk[1][0][1]
                    values[end, pl.ds(row, chunks, stride=16), :] = imag
                    row += 1

    def station_sums():
        rows = jnp.concatenate([values[end, at * 16 : at * 16 + 16, :] for end in (0, 1) for at in range(chunks)], axis=1)
        which = jnp.concatenate([part[...]] * 2, axis=0)
        wide = [split_rows(jnp.where(which == w, rows, jnp.zeros_like(rows))) for w in range(parts)]
        acc = jnp.dot(jnp.concatenate(wide, axis=0), turned[...], preferred_element_type=F32)
        return jnp.concatenate([acc[w * 32 : w * 32 + 16] + acc[w * 32 + 16 : w * 32 + 32] for w in range(parts)], axis=1)

    def solve(sums, gain_now, damp):
        numer = sums[:8] + damp * gain_now
        numer = as_matrix([numer[c : c + 1] for c in range(8)])
        diag_a = sums[8:9] + damp
        diag_d = sums[9:10] + damp
        cross_r = sums[10:11]
        cross_i = sums[11:12]
        scale = 1.0 / (diag_a * diag_d - cross_r * cross_r - cross_i * cross_i)
        rows = []
        for r in (0, 1):
            x, y = numer[2 * r], numer[2 * r + 1]
            low = mul(y, (cross_r, -cross_i))
            high = mul(x, (cross_r, cross_i))
            rows += [x[0] * diag_d - low[0], x[1] * diag_d - low[1]]
            rows += [y[0] * diag_a - high[0], y[1] * diag_a - high[1]]
        return jnp.concatenate([value * scale for value in rows], axis=0)

    def add_change(i):
        for tile in range(tiles):
            at = pl.ds(tile * 128, 128)
            coher = as_matrix([own_ref[i, c, :, at] for c in range(8)])
            rows = [tile * 8 + c for c in range(8)]
            one = [as_matrix([begin[i, end, row : row + 1, :] for row in rows]) for end in (0, 1)]
            two = [as_matrix([ends[end, row : row + 1, :] for row in rows]) for end in (0, 1)]
            before, now = apply_gains(one[0], coher, one[1]), apply_gains(two[0], coher, two[1])
            for e in range(4):
                change = sub(before[e], now[e])
                out_ref[2 * e, :, at] += change[0]
                out_ref[2 * e + 1, :, at] += change[1]

    out_ref[...] = res_ref[...]
    if last:
        width = start_own.shape[2]
        gains_ref[...] = start_own[...]
        for i in range(low):
            ref, place = earlier_gains[i]
            gains_ref[order_ref[i]] = ref[place, :, :width]
    values[...] = jnp.zeros(values.shape, F32)
    for i in range(low, high):
        which = order_ref[i]
        damp = damping_ref[which].astype(F32) * factor
        state[...] = start_ref[i * 8 : i * 8 + 8, :]
        ends[...] = begin[i]
        prepare(i)

        def one_round():
            normal_terms()
            state[...] = solve(station_sums(), state[...], damp)

        def more(r, carry):
            one_round()
            fetch(state[...])
            return carry

        lax.fori_loop(0, jnp.minimum(counts_ref[which], LM_ITERS) - 1, more, jnp.int32(0))
        one_round()
        fetch(state[...], tiles if i + 1 == SOLVED else None)
        if last:
            gains_ref[which] = state[:, :width]
        else:
            solved_ref[i - low] = state[...]
        add_change(i)
        if i + 1 == SOLVED:
            break
        p0, q0 = gain_at(begin.at[i])
        p1, q1 = gain_at(ends)
        for a in (0, 1):
            for b in (0, 1):
                for u in (0, 1):
                    for v in (0, 1):
                        delta = sub(mul_conj(p0[2 * a + u], q0[2 * b + v]), mul_conj(p1[2 * a + u], q1[2 * b + v]))
                        row = ((2 * a + b) * 4 + 2 * u + v) * 2
                        moved[i - low, row] = delta[0]
                        moved[i - low, row + 1] = delta[1]


def exchange(block, axis, mask):
    return lax.ppermute(block, axis, [(i, i ^ mask) for i in range(lax.axis_size(axis))])


def butterfly_sums(value, axis):
    sums = [value]
    while 1 << (len(sums) - 1) < lax.axis_size(axis):
        sums.append(sums[-1] + exchange(sums[-1], axis, 1 << (len(sums) - 1)))
    return sums


def chip_blocks(block, axis):
    chips = lax.axis_size(axis) // 2
    if chips <= 4:
        return jnp.stack([block] + [exchange(block, axis, 2 * j) for j in range(1, chips)])
    parts = block[None]
    while parts.shape[0] < chips:
        parts = jnp.concatenate([parts, exchange(parts, axis, 2 * parts.shape[0])], axis=0)
    return parts


def on_device(visibilities, coherencies, gain_offsets, stations, solve_order, counts, damping):
    groups = lax.axis_size("bl")
    owned, _, channel_count, baselines = coherencies.shape
    channels = visibilities.shape[1]
    width = gain_offsets.shape[2]
    count = groups * width
    tiles = baselines // 128
    params = pltpu.CompilerParams(vmem_limit_bytes=VMEM_BYTES)

    def call(kernel, name, shapes, scalars, arrays, scratch=(), after=(), **static):
        first, skip = len(scalars) + len(arrays), len(after)

        def body(*refs):
            kernel(*refs[:first], *refs[first + skip :], **static)

        return pl.pallas_call(
            body,
            out_shape=[jax.ShapeDtypeStruct(*shape) for shape in shapes],
            in_specs=[pl.BlockSpec(memory_space=pltpu.SMEM)] * len(scalars)
            + [pl.BlockSpec(memory_space=pltpu.VMEM)] * len(arrays)
            + [pl.BlockSpec(memory_space=pl.ANY)] * skip,
            out_specs=[pl.BlockSpec(memory_space=pltpu.VMEM)] * len(shapes),
            scratch_shapes=[pltpu.VMEM(*shape) for shape in scratch],
            compiler_params=params,
            name=name,
        )(*scalars, *arrays, *after)

    per = 128 // width
    part_rows = -(-(owned + SOLVED) // per) * 8
    block = coherencies.shape[1:]
    whole = lambda shape: pl.BlockSpec(shape, lambda g, order: (0,) * len(shape))
    picked = lambda i: pl.BlockSpec((1,) + block, lambda g, order: (order[i] % owned, 0, 0, 0))
    shapes = [(part_rows + 8, 128)] + [(high - low,) + block for low, high in GROUPS]
    packed, *chosen = pl.pallas_call(
        functools.partial(prep_kernel, owned=owned, per=per),
        out_shape=[jax.ShapeDtypeStruct(shape, dtype) for shape, dtype in zip(shapes, [F32] + [BF16] * len(GROUPS))],
        grid_spec=pltpu.PrefetchScalarGridSpec(
            num_scalar_prefetch=1,
            grid=(1,),
            in_specs=[whole(stations.shape), whole(gain_offsets.shape)] + [picked(i) for i in range(SOLVED)],
            out_specs=[whole(shape) for shape in shapes],
        ),
        compiler_params=pltpu.CompilerParams(vmem_limit_bytes=MOST_VMEM_BYTES),
        name="prepare",
    )(solve_order, stations, gain_offsets, *[coherencies] * SOLVED)

    near = chip_blocks(packed, "bl")
    blocks = [near, exchange(near, "bl", 1)]
    shared = [butterfly_sums(value, "dir")[-1] for value in chosen]

    table = ((part_rows * per, count), F32)
    part, begin = call(
        model_kernel,
        "first_model",
        [((8, channel_count, baselines), F32), ((SOLVED * 8, 2 * baselines), F32)],
        [],
        blocks + [coherencies, visibilities],
        [table, ((part_rows * per, 2 * baselines), F32)],
        width=width,
    )
    chunks = groups * tiles
    hots, turned, hot_part, ends, start = call(
        lookup_kernel,
        "lookup",
        [
            ((128, 256 * chunks), BF16),
            ((256 * chunks, 128), BF16),
            ((8, 256 * chunks), jnp.int32),
            ((SOLVED, 2, chunks * 8, 128), F32),
            ((SOLVED * 8, count), F32),
        ],
        [],
        blocks,
        [table],
        width=width,
        owned=owned,
        tiles=tiles,
        after=[part],
    )
    partials = butterfly_sums(part, "dir")
    first = partials[-1]
    res, own, start_own = call(
        own_kernel,
        "own_channels",
        [(visibilities.shape, F32), ((SOLVED, 8, channels, baselines), F32), (gain_offsets.shape, F32)],
        [],
        [gain_offsets, first, *shared],
    )
    moved, solved = [], []
    flat = lambda near: [near.reshape(-1, 128), exchange(near, "bl", 1).reshape(-1, 128)]
    rows = SOLVED * K_ROWS + len(pair_list(0, SOLVED)) * M_ROWS
    [value] = call(
        product_kernel, "products", [((tiles, rows, 128), F32)], [], shared, after=[part], low=0, high=SOLVED
    )
    kx_near = chip_blocks(value, "bl")
    for low, high in TARGETS:
        [value] = call(
            target_kernel,
            "targets",
            [((tiles, (high - low) * M_ROWS, 128), F32)],
            [],
            [first, begin] + shared,
            low=low,
            high=high,
            after=[value, hots],
        )
        [kx_near] = call(keep_kernel, "keep", [(kx_near.shape, F32)], [], [kx_near], after=[value])
        products = flat(kx_near)
        targets = flat(chip_blocks(value, "bl"))
        last = high == SOLVED
        moved_shape = ((high - low, M_ROWS, chunks, 128), F32)
        outs = call(
            sweep_kernel,
            "sweep",
            [(gain_offsets.shape, F32), (visibilities.shape, F32)]
            if last
            else [((high - low, 8, count), F32), moved_shape, (visibilities.shape, F32)],
            [solve_order, counts, damping],
            [hots, turned, hot_part, ends, start, res, own]
            + targets
            + products
            + moved
            + (solved + [start_own] if last else []),
            ([moved_shape] if last else [])
            + [
                ((2, chunks * 8, 128), F32),
                ((2, chunks * 16, 128), F32),
                ((8, count), F32),
                ((M_ROWS, chunks, 128), F32),
                ((K_ROWS, chunks, 128), F32),
            ],
            low=low,
            high=high,
            tiles=tiles,
            factor=baselines * groups * channel_count / count,
        )
        if not last:
            solved.append(outs[0])
            moved.append(outs[1])
            res = outs[2]
    return outs[0], outs[1]


def solution(mesh):
    return jax.shard_map(
        on_device,
        mesh=mesh,
        in_specs=(
            P(None, "dir", "bl"),
            P("dir", None, None, "bl"),
            P(None, None, "bl"),
            P(None, "bl"),
            P(),
            P(),
            P(),
        ),
        out_specs=(P(None, None, "bl"), P(None, "dir", "bl")),
        check_vma=False,
    )
```

```python
import functools

import jax
import jax.numpy as jnp
from jax import lax
from jax.experimental import pallas as pl
from jax.experimental.pallas import tpu as pltpu
from jax.sharding import PartitionSpec as P

LM_ITERS = 2
SOLVED = 4
F32 = jnp.float32
BF16 = jnp.bfloat16
VMEM_BYTES = 24 * 1024 * 1024
MOST_VMEM_BYTES = 60 * 1024 * 1024
GRAM = [(u, v) for u in range(4) for v in range(u, 4)]
M_ROWS = 32
K_ROWS = 16
GROUPS = [(0, 2), (2, 4)]
TARGETS = [(0, 4)]


def mul(x, y):
    return (x[0] * y[0] - x[1] * y[1], x[0] * y[1] + x[1] * y[0])


def add(x, y):
    return (x[0] + y[0], x[1] + y[1])


def sub(x, y):
    return (x[0] - y[0], x[1] - y[1])


def conj(x):
    return (x[0], -x[1])


def total(terms):
    return functools.reduce(add, terms)


def mul_conj(x, y):
    return (x[0] * y[0] + x[1] * y[1], x[1] * y[0] - x[0] * y[1])


def matmul(left, right):
    return [add(mul(left[2 * i], right[j]), mul(left[2 * i + 1], right[2 + j])) for i in (0, 1) for j in (0, 1)]


def matmul_adj(left, right):
    return [
        add(mul_conj(left[2 * i], right[2 * j]), mul_conj(left[2 * i + 1], right[2 * j + 1]))
        for i in (0, 1)
        for j in (0, 1)
    ]


def apply_gains(gain_p, coher, gain_q):
    return matmul_adj(matmul(gain_p, coher), gain_q)


def as_matrix(parts):
    return [(parts[2 * e], parts[2 * e + 1]) for e in range(4)]


def split_rows(values):
    high = values.astype(BF16)
    low = (values - high.astype(F32)).astype(BF16)
    return jnp.concatenate([high, low], axis=0)


def one_hot(stations_p, stations_q, count):
    both = jnp.concatenate([stations_p, stations_q], axis=1)
    rows = lax.broadcasted_iota(jnp.int32, (count, both.shape[1]), 0)
    return jnp.where(rows == both, 1.0, 0.0).astype(BF16)


def pick(one_hots, values):
    count = values.shape[0]
    out = jnp.dot(split_rows(values), one_hots, preferred_element_type=F32)
    return out[:count] + out[count:]


def prep_kernel(order_ref, stations_ref, offs_ref, *refs, owned, per):
    coher_refs, out_ref, chosen_refs = refs[:SOLVED], refs[SOLVED], refs[SOLVED + 1 :]
    lane = lax.axis_index("dir")
    width = offs_ref.shape[2]
    station_rows = 2 * stations_ref.shape[1] // 128
    part_rows = out_ref.shape[0] - 8
    comp = lax.broadcasted_iota(jnp.int32, (8, width), 0)
    ident = jnp.where((comp == 0) | (comp == 6), 1.0, 0.0)
    places = [lane * owned + d for d in range(owned)] + [order_ref[i] for i in range(SOLVED)]
    blocks = [offs_ref[place] + ident for place in places]
    while len(blocks) * 8 < part_rows * per:
        blocks.append(jnp.zeros((8, width), F32))
    each = part_rows // 8
    columns = [jnp.concatenate(blocks[q * each : (q + 1) * each], axis=0) for q in range(per)]
    out_ref[:part_rows] = jnp.concatenate(columns, axis=1)
    out_ref[part_rows:] = jnp.zeros((8, 128), F32)
    for row in range(station_rows):
        end, tile = row // (station_rows // 2), row % (station_rows // 2)
        out_ref[part_rows + row : part_rows + row + 1] = stations_ref[end : end + 1, tile * 128 : tile * 128 + 128].astype(F32)
    for i in range(SOLVED):
        mine = order_ref[i] // owned == lane
        [(low, ref)] = [(low, ref) for (low, high), ref in zip(GROUPS, chosen_refs) if low <= i < high]
        ref[i - low] = jnp.where(mine, coher_refs[i][0], jnp.zeros_like(coher_refs[i][0]))


def keep_kernel(one_ref, out_ref):
    out_ref[...] = one_ref[...]


def fill_table(blocks, table, width):
    rows, lanes = blocks[0].shape[1:]
    groups = 2 * blocks[0].shape[0]
    part_rows = rows - 8
    per = lanes // width
    lane_of = lax.broadcasted_iota(jnp.int32, (part_rows, lanes), 1) // width
    for tile in range(groups * width // lanes):
        for q in range(per):
            tile_rows = jnp.zeros((part_rows, lanes), F32)
            for u in range(per):
                j = per * tile + u
                block = blocks[j % 2][j // 2, :part_rows]
                shift = ((u - q) * width) % lanes
                if shift:
                    block = pltpu.roll(block, shift, 1)
                tile_rows = jnp.where(lane_of == u, block, tile_rows)
            table[q * part_rows : (q + 1) * part_rows, tile * lanes : (tile + 1) * lanes] = tile_rows


def block_stations(block, tiles, base):
    part_rows = block.shape[0] - 8
    rows = block[part_rows:, :].astype(jnp.int32) ^ base
    return [jnp.concatenate([rows[end * tiles + t : end * tiles + t + 1] for t in range(tiles)], axis=1) for end in (0, 1)]


def fetch_columns(rows, hots, part, at):
    count = rows.shape[0]
    parts = rows.shape[1] // 128
    wide = jnp.concatenate([rows[:, w * 128 : w * 128 + 128] for w in range(parts)], axis=0)
    out = jnp.dot(split_rows(wide), hots[:, at], preferred_element_type=F32)
    out = out[: parts * count] + out[parts * count :]
    which = jnp.concatenate([part[:, at]] * (count // 8), axis=0)
    value = out[:count]
    for w in range(1, parts):
        value = jnp.where(which == w, out[w * count : w * count + count], value)
    return value


def lookup_kernel(
    order_ref, counts_ref, damping_ref, offs_ref, near_ref, far_ref, hots_ref, turned_ref, part_ref, ends_ref, start_ref,
    gains_ref, table, *, width, owned, tiles,
):
    half = near_ref.shape[0]
    chunks = 2 * half * tiles
    comp = lax.broadcasted_iota(jnp.int32, offs_ref.shape[1:], 0)
    gains_ref[...] = offs_ref[...] + jnp.where((comp == 0) | (comp == 6), 1.0, 0.0)[None]
    base = lax.axis_index("bl").astype(jnp.int32) * width
    fill_table([near_ref, far_ref], table, width)
    start = table[owned * 8 : (owned + SOLVED) * 8, :]
    start_ref[...] = start
    pairs = [block_stations(ref.at[j], tiles, base) for ref in (near_ref, far_ref) for j in range(half)]
    step = min(8, chunks)
    for end in (0, 1):
        rows = jnp.concatenate([pair[end] for pair in pairs], axis=1)
        for first in range(0, chunks, step):
            at = pl.ds((end * chunks + first) * 128, step * 128)
            here = rows[:, first * 128 : (first + step) * 128]
            index = lax.broadcasted_iota(jnp.int32, (128, step * 128), 0)
            hot = jnp.where(index == (here & 127), 1.0, 0.0)
            hots_ref[:, at] = hot.astype(BF16)
            turned_ref[at, :] = jnp.transpose(hot).astype(BF16)
            part_ref[:, at] = jnp.broadcast_to(here >> 7, (8, step * 128))
            out = fetch_columns(start, hots_ref, part_ref, at)
            for i in range(SOLVED):
                for t in range(step):
                    ends_ref[i, end, (first + t) * 8 : (first + t) * 8 + 8, :] = out[i * 8 : i * 8 + 8, t * 128 : t * 128 + 128]


def model_kernel(near_ref, far_ref, coher_ref, vis_ref, part_ref, begin_ref, table, ends, *, width):
    owned = coher_ref.shape[0]
    baselines = coher_ref.shape[3]
    channels = vis_ref.shape[1]
    lane = lax.axis_index("dir")
    base = lax.axis_index("bl").astype(jnp.int32) * width
    fill_table([near_ref, far_ref], table, width)
    rows_p, rows_q = block_stations(near_ref.at[0], baselines // 128, base)
    ends[...] = pick(one_hot(rows_p, rows_q, table.shape[1]), table[...])
    begin_ref[...] = ends[owned * 8 : (owned + SOLVED) * 8, :]

    for half in range(baselines // 128):
        at = pl.ds(half * 128, 128)
        at_q = pl.ds(baselines + half * 128, 128)

        def gain(row, where):
            block = ends[pl.ds(pl.multiple_of(row, 8), 8), where]
            return as_matrix([block[c : c + 1] for c in range(8)])

        def add_model(d, acc):
            coher = as_matrix([coher_ref[d, c, :, at].astype(F32) for c in range(8)])
            model = apply_gains(gain(d * 8, at), coher, gain(d * 8, at_q))
            return [sub(x, y) for x, y in zip(acc, model)]

        zeros = jnp.zeros((coher_ref.shape[2], 128), F32)
        acc = lax.fori_loop(0, owned, add_model, [(zeros, zeros)] * 4)
        for c in range(8):
            total_part = acc[c // 2][c % 2]
            lanes = [total_part[x : x + channels] for x in range(0, total_part.shape[0], channels)]
            vis = vis_ref[c, :, at]
            part_ref[c, :, at] = jnp.concatenate([jnp.where(lane == x, y + vis, y) for x, y in enumerate(lanes)], axis=0)


def summed(values):
    return jnp.sum(values, axis=0, keepdims=True)


def pair_list(low, high):
    return [(m, i) for i in range(low, high) for m in range(i)]


def load_coher(refs, i, at):
    [(low, ref)] = [(low, ref) for (low, high), ref in zip(GROUPS, refs) if low <= i < high]
    return as_matrix([ref[i - low, c, :, at].astype(F32) for c in range(8)])


def target_kernel(first_ref, begin_ref, *refs, low, high):
    *solved_refs, out_ref = refs
    baselines = first_ref.shape[2]
    for half in range(baselines // 128):
        at = pl.ds(half * 128, 128)
        out = 0
        for i in range(low, high):
            coher = load_coher(solved_refs, i, at)
            gain_p, gain_q = [
                as_matrix([begin_ref[i * 8 + c : i * 8 + c + 1, pl.ds(end * baselines + half * 128, 128)] for c in range(8)])
                for end in (0, 1)
            ]
            model = apply_gains(gain_p, coher, gain_q)
            target = [(first_ref[2 * e, :, at] + model[e][0], first_ref[2 * e + 1, :, at] + model[e][1]) for e in range(4)]
            for u in range(4):
                for v in range(4):
                    value = mul_conj(target[u], coher[v])
                    out_ref[half, out : out + 1, :] = summed(value[0])
                    out_ref[half, out + 1 : out + 2, :] = summed(value[1])
                    out += 2


def product_kernel(*refs, low, high):
    *solved_refs, out_ref = refs
    for half in range(out_ref.shape[0]):
        at = pl.ds(half * 128, 128)
        out = 0
        for i in range(low, high):
            coher = load_coher(solved_refs, i, at)
            for u, v in GRAM:
                value = mul_conj(coher[u], coher[v])
                out_ref[half, out : out + 1, :] = summed(value[0])
                out += 1
                if u != v:
                    out_ref[half, out : out + 1, :] = summed(value[1])
                    out += 1
        for m, i in pair_list(low, high):
            coher, other = load_coher(solved_refs, i, at), load_coher(solved_refs, m, at)
            for u in range(4):
                for v in range(4):
                    value = mul_conj(other[u], coher[v])
                    out_ref[half, out : out + 1, :] = summed(value[0])
                    out_ref[half, out + 1 : out + 2, :] = summed(value[1])
                    out += 2


def own_kernel(first_ref, *refs):
    *solved_refs, res_ref, own_ref = refs
    channels = res_ref.shape[1]
    lane = lax.axis_index("dir")

    def select(value):
        mine = value[:channels]
        for x in range(1, value.shape[0] // channels):
            mine = jnp.where(lane == x, value[x * channels : (x + 1) * channels], mine)
        return mine

    for c in range(8):
        res_ref[c] = select(first_ref[c])
        for (low, high), solved_ref in zip(GROUPS, solved_refs):
            for i in range(low, high):
                own_ref[i, c] = select(solved_ref[i - low, c].astype(F32))


def sweep_kernel(order_ref, counts_ref, damping_ref, *refs, low, high, tiles, factor):
    last = high == SOLVED
    hots, turned, part, begin, start_ref, res_ref, own_ref = refs[:7]
    targets, refs = refs[7:9], refs[9:]
    pair, refs = refs[:2], refs[2:]
    ends, values, state, m_now, k_now = refs[-5:]
    refs = refs[:-5]
    stages = [stage for stage in TARGETS if stage[1] <= low]
    earlier_moved = {m: (refs[s], m - stage[0]) for s, stage in enumerate(stages) for m in range(*stage)}
    refs = refs[len(stages) :]
    if last:
        earlier_gains = {m: (refs[s], m - stage[0]) for s, stage in enumerate(stages) for m in range(*stage)}
        start_own, gains_ref, out_ref, moved = refs[len(stages) :]
    else:
        solved_ref, moved, out_ref = refs
    chunks = hots.shape[1] // 256
    parts = start_ref.shape[1] // 128

    def rows_at(pair, row):
        stride = pair[0].shape[0] // (chunks // 2)
        return jnp.concatenate([ref[pl.ds(row, chunks // 2, stride=stride), :] for ref in pair], axis=0)

    def fetch(gain_now, only=None):
        step = min(8, chunks) if only is None else only
        for end in (0, 1):
            for first in range(0, chunks if only is None else only, step):
                at = pl.ds((end * chunks + first) * 128, step * 128)
                out = fetch_columns(gain_now, hots, part, at)
                for t in range(step):
                    ends[end, (first + t) * 8 : (first + t) * 8 + 8, :] = out[:, t * 128 : t * 128 + 128]

    def gain_at(ref):
        return [as_matrix([ref[end, pl.ds(c, chunks, stride=8), :] for c in range(8)]) for end in (0, 1)]

    def load_m():
        return [[(m_now[(u * 4 + v) * 2], m_now[(u * 4 + v) * 2 + 1]) for v in range(4)] for u in range(4)]

    def load_k():
        row = 0
        gram = {}
        for u, v in GRAM:
            if u == v:
                gram[u, v] = (k_now[row], None)
                row += 1
            else:
                gram[u, v] = (k_now[row], k_now[row + 1])
                gram[v, u] = conj(gram[u, v])
                row += 2
        return gram

    def prepare(i):
        for row in range(K_ROWS):
            k_now[row] = rows_at(pair, i * K_ROWS + row)
        for w in range(4):
            value = []
            for out in range(4):
                row = (i - low) * M_ROWS + (out * 4 + w) * 2
                value.append((rows_at(targets, row), rows_at(targets, row + 1)))
            for m in range(i):
                base = SOLVED * K_ROWS + pair_list(0, SOLVED).index((m, i)) * M_ROWS
                ref, place = (moved, m - low) if m >= low else earlier_moved[m]
                for uv in range(4):
                    at = base + (uv * 4 + w) * 2
                    cross = (rows_at(pair, at), rows_at(pair, at + 1))
                    for out in range(4):
                        row = (out * 4 + uv) * 2
                        value[out] = add(value[out], mul((ref[place, row], ref[place, row + 1]), cross))
            for out in range(4):
                m_now[(out * 4 + w) * 2] = value[out][0]
                m_now[(out * 4 + w) * 2 + 1] = value[out][1]

    def hermitian(gain):
        a = gain[0][0] ** 2 + gain[0][1] ** 2 + gain[2][0] ** 2 + gain[2][1] ** 2
        d = gain[1][0] ** 2 + gain[1][1] ** 2 + gain[3][0] ** 2 + gain[3][1] ** 2
        cross = add(mul_conj(gain[1], gain[0]), mul_conj(gain[3], gain[2]))
        return a, d, cross

    def normal_terms():
        gain_p, gain_q = gain_at(ends)
        m = load_m()
        k = load_k()
        for end, gain, other in ((0, gain_q, False), (1, gain_p, True)):
            row = 0
            for r in (0, 1):
                for c in (0, 1):
                    if other:
                        terms = [mul_conj(gain[2 * a + b], m[2 * a + r][2 * b + c]) for a in (0, 1) for b in (0, 1)]
                    else:
                        terms = [mul(gain[2 * a + b], m[2 * r + a][2 * c + b]) for a in (0, 1) for b in (0, 1)]
                    value = total(terms)
                    values[end, pl.ds(row, chunks, stride=16), :] = value[0]
                    values[end, pl.ds(row + 1, chunks, stride=16), :] = value[1]
                    row += 2
            a, d, cross = hermitian(gain)
            for r, c in ((0, 0), (1, 1), (0, 1)):
                if other:
                    kk = [[k[2 * x + r, 2 * y + c] for y in (0, 1)] for x in (0, 1)]
                    kk = [[(z[0], None if z[1] is None else -z[1]) for z in line] for line in kk]
                else:
                    kk = [[k[2 * r + x, 2 * c + y] for y in (0, 1)] for x in (0, 1)]
                real = a * kk[0][0][0] + d * kk[1][1][0]
                real += cross[0] * (kk[0][1][0] + kk[1][0][0])
                minus = None
                if kk[0][1][1] is not None:
                    minus = kk[1][0][1] - kk[0][1][1]
                    real += cross[1] * minus
                values[end, pl.ds(row, chunks, stride=16), :] = real
                row += 1
                if r != c:
                    imag = cross[1] * (kk[0][1][0] - kk[1][0][0])
                    if kk[0][0][1] is not None:
                        imag += a * kk[0][0][1]
                    if kk[1][1][1] is not None:
                        imag += d * kk[1][1][1]
                    if kk[0][1][1] is not None:
                        imag += cross[0] * kk[0][1][1]
                    if kk[1][0][1] is not None:
                        imag += cross[0] * kk[1][0][1]
                    values[end, pl.ds(row, chunks, stride=16), :] = imag
                    row += 1

    def station_sums():
        rows = jnp.concatenate([values[end, at * 16 : at * 16 + 16, :] for end in (0, 1) for at in range(chunks)], axis=1)
        which = jnp.concatenate([part[...]] * 2, axis=0)
        wide = [split_rows(jnp.where(which == w, rows, jnp.zeros_like(rows))) for w in range(parts)]
        acc = jnp.dot(jnp.concatenate(wide, axis=0), turned[...], preferred_element_type=F32)
        return jnp.concatenate([acc[w * 32 : w * 32 + 16] + acc[w * 32 + 16 : w * 32 + 32] for w in range(parts)], axis=1)

    def solve(sums, gain_now, damp):
        numer = sums[:8] + damp * gain_now
        numer = as_matrix([numer[c : c + 1] for c in range(8)])
        diag_a = sums[8:9] + damp
        diag_d = sums[9:10] + damp
        cross_r = sums[10:11]
        cross_i = sums[11:12]
        scale = 1.0 / (diag_a * diag_d - cross_r * cross_r - cross_i * cross_i)
        rows = []
        for r in (0, 1):
            x, y = numer[2 * r], numer[2 * r + 1]
            low = mul(y, (cross_r, -cross_i))
            high = mul(x, (cross_r, cross_i))
            rows += [x[0] * diag_d - low[0], x[1] * diag_d - low[1]]
            rows += [y[0] * diag_a - high[0], y[1] * diag_a - high[1]]
        return jnp.concatenate([value * scale for value in rows], axis=0)

    def add_change(i):
        for tile in range(tiles):
            at = pl.ds(tile * 128, 128)
            coher = as_matrix([own_ref[i, c, :, at] for c in range(8)])
            rows = [tile * 8 + c for c in range(8)]
            one = [as_matrix([begin[i, end, row : row + 1, :] for row in rows]) for end in (0, 1)]
            two = [as_matrix([ends[end, row : row + 1, :] for row in rows]) for end in (0, 1)]
            before, now = apply_gains(one[0], coher, one[1]), apply_gains(two[0], coher, two[1])
            for e in range(4):
                change = sub(before[e], now[e])
                out_ref[2 * e, :, at] += change[0]
                out_ref[2 * e + 1, :, at] += change[1]

    out_ref[...] = res_ref[...]
    if last:
        width = start_own.shape[2]
        gains_ref[...] = start_own[...]
        for i in range(low):
            ref, place = earlier_gains[i]
            gains_ref[order_ref[i]] = ref[place, :, :width]
    values[...] = jnp.zeros(values.shape, F32)
    for i in range(low, high):
        which = order_ref[i]
        damp = damping_ref[which].astype(F32) * factor
        state[...] = start_ref[i * 8 : i * 8 + 8, :]
        ends[...] = begin[i]
        prepare(i)

        def one_round():
            normal_terms()
            state[...] = solve(station_sums(), state[...], damp)

        def more(r, carry):
            one_round()
            fetch(state[...])
            return carry

        lax.fori_loop(0, jnp.minimum(counts_ref[which], LM_ITERS) - 1, more, jnp.int32(0))
        one_round()
        fetch(state[...], tiles if i + 1 == SOLVED else None)
        if last:
            gains_ref[which] = state[:, :width]
        else:
            solved_ref[i - low] = state[...]
        add_change(i)
        if i + 1 == SOLVED:
            break
        p0, q0 = gain_at(begin.at[i])
        p1, q1 = gain_at(ends)
        for a in (0, 1):
            for b in (0, 1):
                for u in (0, 1):
                    for v in (0, 1):
                        delta = sub(mul_conj(p0[2 * a + u], q0[2 * b + v]), mul_conj(p1[2 * a + u], q1[2 * b + v]))
                        row = ((2 * a + b) * 4 + 2 * u + v) * 2
                        moved[i - low, row] = delta[0]
                        moved[i - low, row + 1] = delta[1]


def exchange(block, axis, mask):
    return lax.ppermute(block, axis, [(i, i ^ mask) for i in range(lax.axis_size(axis))])


def butterfly_sums(value, axis):
    sums = [value]
    while 1 << (len(sums) - 1) < lax.axis_size(axis):
        sums.append(sums[-1] + exchange(sums[-1], axis, 1 << (len(sums) - 1)))
    return sums


def chip_blocks(block, axis, parts_out=False):
    chips = lax.axis_size(axis) // 2
    if chips <= 4:
        blocks = [block] + [exchange(block, axis, 2 * j) for j in range(1, chips)]
        return (jnp.stack(blocks), blocks[1]) if parts_out else jnp.stack(blocks)
    parts = block[None]
    while parts.shape[0] < chips:
        parts = jnp.concatenate([parts, exchange(parts, axis, 2 * parts.shape[0])], axis=0)
    return (parts, parts) if parts_out else parts


def on_device(visibilities, coherencies, gain_offsets, stations, solve_order, counts, damping):
    groups = lax.axis_size("bl")
    owned, _, channel_count, baselines = coherencies.shape
    channels = visibilities.shape[1]
    width = gain_offsets.shape[2]
    count = groups * width
    tiles = baselines // 128
    params = pltpu.CompilerParams(vmem_limit_bytes=VMEM_BYTES)

    def call(kernel, name, shapes, scalars, arrays, scratch=(), after=(), **static):
        first, skip = len(scalars) + len(arrays), len(after)

        def body(*refs):
            kernel(*refs[:first], *refs[first + skip :], **static)

        return pl.pallas_call(
            body,
            out_shape=[jax.ShapeDtypeStruct(*shape) for shape in shapes],
            in_specs=[pl.BlockSpec(memory_space=pltpu.SMEM)] * len(scalars)
            + [pl.BlockSpec(memory_space=pltpu.VMEM)] * len(arrays)
            + [pl.BlockSpec(memory_space=pl.ANY)] * skip,
            out_specs=[pl.BlockSpec(memory_space=pltpu.VMEM)] * len(shapes),
            scratch_shapes=[pltpu.VMEM(*shape) for shape in scratch],
            compiler_params=params,
            name=name,
        )(*scalars, *arrays, *after)

    per = 128 // width
    part_rows = -(-(owned + SOLVED) // per) * 8
    block = coherencies.shape[1:]
    whole = lambda shape: pl.BlockSpec(shape, lambda g, order: (0,) * len(shape))
    picked = lambda i: pl.BlockSpec((1,) + block, lambda g, order: (order[i] % owned, 0, 0, 0))
    shapes = [(part_rows + 8, 128)] + [(high - low,) + block for low, high in GROUPS]
    packed, *chosen = pl.pallas_call(
        functools.partial(prep_kernel, owned=owned, per=per),
        out_shape=[jax.ShapeDtypeStruct(shape, dtype) for shape, dtype in zip(shapes, [F32] + [BF16] * len(GROUPS))],
        grid_spec=pltpu.PrefetchScalarGridSpec(
            num_scalar_prefetch=1,
            grid=(1,),
            in_specs=[whole(stations.shape), whole(gain_offsets.shape)] + [picked(i) for i in range(SOLVED)],
            out_specs=[whole(shape) for shape in shapes],
        ),
        compiler_params=pltpu.CompilerParams(vmem_limit_bytes=MOST_VMEM_BYTES),
        name="prepare",
    )(solve_order, stations, gain_offsets, *[coherencies] * SOLVED)

    near = chip_blocks(packed, "bl")
    blocks = [near, exchange(near, "bl", 1)]
    shared = [butterfly_sums(value, "dir")[-1] for value in chosen]

    table = ((part_rows * per, count), F32)
    part, begin = call(
        model_kernel,
        "first_model",
        [((8, channel_count, baselines), F32), ((SOLVED * 8, 2 * baselines), F32)],
        [],
        blocks + [coherencies, visibilities],
        [table, ((part_rows * per, 2 * baselines), F32)],
        width=width,
    )
    chunks = groups * tiles
    hots, turned, hot_part, ends, start, start_own = call(
        lookup_kernel,
        "lookup",
        [
            ((128, 256 * chunks), BF16),
            ((256 * chunks, 128), BF16),
            ((8, 256 * chunks), jnp.int32),
            ((SOLVED, 2, chunks * 8, 128), F32),
            ((SOLVED * 8, count), F32),
            (gain_offsets.shape, F32),
        ],
        [solve_order, counts, damping],
        [gain_offsets] + blocks,
        [table],
        width=width,
        owned=owned,
        tiles=tiles,
        after=[part],
    )
    partials = butterfly_sums(part, "dir")
    first = partials[-1]
    res, own = call(
        own_kernel,
        "own_channels",
        [(visibilities.shape, F32), ((SOLVED, 8, channels, baselines), F32)],
        [],
        [first, *shared],
    )
    moved, solved = [], []
    flat = lambda near: [near.reshape(-1, 128), exchange(near, "bl", 1).reshape(-1, 128)]
    rows = SOLVED * K_ROWS + len(pair_list(0, SOLVED)) * M_ROWS
    [value] = call(
        product_kernel, "products", [((tiles, rows, 128), F32)], [], shared, after=[part], low=0, high=SOLVED
    )
    kx_near = chip_blocks(value, "bl")
    for low, high in TARGETS:
        [value] = call(
            target_kernel,
            "targets",
            [((tiles, (high - low) * M_ROWS, 128), F32)],
            [],
            [first, begin] + shared,
            low=low,
            high=high,
            after=[value, hots],
        )
        near, near_x = chip_blocks(value, "bl", True)
        [kx_near] = call(keep_kernel, "keep", [(kx_near.shape, F32)], [], [kx_near], after=[value])
        products = flat(kx_near)
        targets = flat(near)
        last = high == SOLVED
        moved_shape = ((high - low, M_ROWS, chunks, 128), F32)
        outs = call(
            sweep_kernel,
            "sweep",
            [(gain_offsets.shape, F32), (visibilities.shape, F32)]
            if last
            else [((high - low, 8, count), F32), moved_shape, (visibilities.shape, F32)],
            [solve_order, counts, damping],
            [hots, turned, hot_part, ends, start, res, own]
            + targets
            + products
            + moved
            + (solved + [start_own] if last else []),
            ([moved_shape] if last else [])
            + [
                ((2, chunks * 8, 128), F32),
                ((2, chunks * 16, 128), F32),
                ((8, count), F32),
                ((M_ROWS, chunks, 128), F32),
                ((K_ROWS, chunks, 128), F32),
            ],
            low=low,
            high=high,
            tiles=tiles,
            factor=baselines * groups * channel_count / count,
        )
        if not last:
            solved.append(outs[0])
            moved.append(outs[1])
            res = outs[2]
    return outs[0], outs[1]


def solution(mesh):
    return jax.shard_map(
        on_device,
        mesh=mesh,
        in_specs=(
            P(None, "dir", "bl"),
            P("dir", None, None, "bl"),
            P(None, None, "bl"),
            P(None, "bl"),
            P(),
            P(),
            P(),
        ),
        out_specs=(P(None, None, "bl"), P(None, "dir", "bl")),
        check_vma=False,
    )
```

```python
import functools

import jax
import jax.numpy as jnp
from jax import lax
from jax.experimental import pallas as pl
from jax.experimental.pallas import tpu as pltpu
from jax.sharding import PartitionSpec as P

LM_ITERS = 2
SOLVED = 4
F32 = jnp.float32
BF16 = jnp.bfloat16
VMEM_BYTES = 24 * 1024 * 1024
MOST_VMEM_BYTES = 60 * 1024 * 1024
GRAM = [(u, v) for u in range(4) for v in range(u, 4)]
M_ROWS = 32
K_ROWS = 16
GROUPS = [(0, 2), (2, 4)]
TARGETS = [(0, 4)]


def mul(x, y):
    return (x[0] * y[0] - x[1] * y[1], x[0] * y[1] + x[1] * y[0])


def add(x, y):
    return (x[0] + y[0], x[1] + y[1])


def sub(x, y):
    return (x[0] - y[0], x[1] - y[1])


def conj(x):
    return (x[0], -x[1])


def total(terms):
    return functools.reduce(add, terms)


def mul_conj(x, y):
    return (x[0] * y[0] + x[1] * y[1], x[1] * y[0] - x[0] * y[1])


def matmul(left, right):
    return [add(mul(left[2 * i], right[j]), mul(left[2 * i + 1], right[2 + j])) for i in (0, 1) for j in (0, 1)]


def matmul_adj(left, right):
    return [
        add(mul_conj(left[2 * i], right[2 * j]), mul_conj(left[2 * i + 1], right[2 * j + 1]))
        for i in (0, 1)
        for j in (0, 1)
    ]


def apply_gains(gain_p, coher, gain_q):
    return matmul_adj(matmul(gain_p, coher), gain_q)


def as_matrix(parts):
    return [(parts[2 * e], parts[2 * e + 1]) for e in range(4)]


def split_rows(values):
    high = values.astype(BF16)
    low = (values - high.astype(F32)).astype(BF16)
    return jnp.concatenate([high, low], axis=0)


def one_hot(stations_p, stations_q, count):
    both = jnp.concatenate([stations_p, stations_q], axis=1)
    rows = lax.broadcasted_iota(jnp.int32, (count, both.shape[1]), 0)
    return jnp.where(rows == both, 1.0, 0.0).astype(BF16)


def pick(one_hots, values):
    count = values.shape[0]
    out = jnp.dot(split_rows(values), one_hots, preferred_element_type=F32)
    return out[:count] + out[count:]


def prep_kernel(order_ref, stations_ref, offs_ref, *refs, owned, per):
    coher_refs, out_ref, chosen_refs = refs[:SOLVED], refs[SOLVED], refs[SOLVED + 1 :]
    lane = lax.axis_index("dir")
    width = offs_ref.shape[2]
    station_rows = 2 * stations_ref.shape[1] // 128
    part_rows = out_ref.shape[0] - 8
    comp = lax.broadcasted_iota(jnp.int32, (8, width), 0)
    ident = jnp.where((comp == 0) | (comp == 6), 1.0, 0.0)
    places = [lane * owned + d for d in range(owned)] + [order_ref[i] for i in range(SOLVED)]
    blocks = [offs_ref[place] + ident for place in places]
    while len(blocks) * 8 < part_rows * per:
        blocks.append(jnp.zeros((8, width), F32))
    each = part_rows // 8
    columns = [jnp.concatenate(blocks[q * each : (q + 1) * each], axis=0) for q in range(per)]
    out_ref[:part_rows] = jnp.concatenate(columns, axis=1)
    out_ref[part_rows:] = jnp.zeros((8, 128), F32)
    for row in range(station_rows):
        end, tile = row // (station_rows // 2), row % (station_rows // 2)
        out_ref[part_rows + row : part_rows + row + 1] = stations_ref[end : end + 1, tile * 128 : tile * 128 + 128].astype(F32)
    for i in range(SOLVED):
        mine = order_ref[i] // owned == lane
        [(low, ref)] = [(low, ref) for (low, high), ref in zip(GROUPS, chosen_refs) if low <= i < high]
        ref[i - low] = jnp.where(mine, coher_refs[i][0], jnp.zeros_like(coher_refs[i][0]))


def keep_kernel(one_ref, *out_refs):
    each = one_ref.shape[0] // len(out_refs)
    for n, out_ref in enumerate(out_refs):
        out_ref[...] = one_ref[n * each : (n + 1) * each]


def fill_table(blocks, table, width):
    rows, lanes = blocks[0].shape[1:]
    groups = 2 * blocks[0].shape[0]
    part_rows = rows - 8
    per = lanes // width
    lane_of = lax.broadcasted_iota(jnp.int32, (part_rows, lanes), 1) // width
    for tile in range(groups * width // lanes):
        for q in range(per):
            tile_rows = jnp.zeros((part_rows, lanes), F32)
            for u in range(per):
                j = per * tile + u
                block = blocks[j % 2][j // 2, :part_rows]
                shift = ((u - q) * width) % lanes
                if shift:
                    block = pltpu.roll(block, shift, 1)
                tile_rows = jnp.where(lane_of == u, block, tile_rows)
            table[q * part_rows : (q + 1) * part_rows, tile * lanes : (tile + 1) * lanes] = tile_rows


def block_stations(block, tiles, base):
    part_rows = block.shape[0] - 8
    rows = block[part_rows:, :].astype(jnp.int32) ^ base
    return [jnp.concatenate([rows[end * tiles + t : end * tiles + t + 1] for t in range(tiles)], axis=1) for end in (0, 1)]


def fetch_columns(wide, parts, hots, part, at):
    count = wide.shape[0] // parts
    out = jnp.dot(split_rows(wide), hots[:, at], preferred_element_type=F32)
    out = out[: parts * count] + out[parts * count :]
    which = jnp.concatenate([part[:, at]] * (count // 8), axis=0)
    value = out[:count]
    for w in range(1, parts):
        value = jnp.where(which == w, out[w * count : w * count + count], value)
    return value


def lookup_kernel(
    order_ref, counts_ref, damping_ref, offs_ref, near_ref, far_ref, hots_ref, turned_ref, part_ref, ends_ref, start_ref,
    gains_ref, table, *, width, owned, tiles,
):
    half = near_ref.shape[0]
    chunks = 2 * half * tiles
    comp = lax.broadcasted_iota(jnp.int32, offs_ref.shape[1:], 0)
    gains_ref[...] = offs_ref[...] + jnp.where((comp == 0) | (comp == 6), 1.0, 0.0)[None]
    base = lax.axis_index("bl").astype(jnp.int32) * width
    fill_table([near_ref, far_ref], table, width)
    start = table[owned * 8 : (owned + SOLVED) * 8, :]
    parts = start.shape[1] // 128
    columns = [start[:, w * 128 : w * 128 + 128] for w in range(parts)]
    for i in range(SOLVED):
        start_ref[i] = jnp.concatenate([column[i * 8 : i * 8 + 8] for column in columns], axis=0)
    wide = jnp.concatenate(columns, axis=0)
    pairs = [block_stations(ref.at[j], tiles, base) for ref in (near_ref, far_ref) for j in range(half)]
    step = min(8, chunks)
    for end in (0, 1):
        rows = jnp.concatenate([pair[end] for pair in pairs], axis=1)
        for first in range(0, chunks, step):
            at = pl.ds((end * chunks + first) * 128, step * 128)
            here = rows[:, first * 128 : (first + step) * 128]
            index = lax.broadcasted_iota(jnp.int32, (128, step * 128), 0)
            hot = jnp.where(index == (here & 127), 1.0, 0.0)
            hots_ref[:, at] = hot.astype(BF16)
            turned_ref[at, :] = jnp.transpose(hot).astype(BF16)
            part_ref[:, at] = jnp.broadcast_to(here >> 7, (8, step * 128))
            out = fetch_columns(wide, parts, hots_ref, part_ref, at)
            for i in range(SOLVED):
                for t in range(step):
                    ends_ref[i, end, (first + t) * 8 : (first + t) * 8 + 8, :] = out[i * 8 : i * 8 + 8, t * 128 : t * 128 + 128]


def model_kernel(near_ref, far_ref, coher_ref, vis_ref, part_ref, begin_ref, table, ends, *, width):
    owned = coher_ref.shape[0]
    baselines = coher_ref.shape[3]
    channels = vis_ref.shape[1]
    lane = lax.axis_index("dir")
    base = lax.axis_index("bl").astype(jnp.int32) * width
    fill_table([near_ref, far_ref], table, width)
    rows_p, rows_q = block_stations(near_ref.at[0], baselines // 128, base)
    ends[...] = pick(one_hot(rows_p, rows_q, table.shape[1]), table[...])
    begin_ref[...] = ends[owned * 8 : (owned + SOLVED) * 8, :]

    for half in range(baselines // 128):
        at = pl.ds(half * 128, 128)
        at_q = pl.ds(baselines + half * 128, 128)

        def gain(row, where):
            block = ends[pl.ds(pl.multiple_of(row, 8), 8), where]
            return as_matrix([block[c : c + 1] for c in range(8)])

        def add_model(d, acc):
            coher = as_matrix([coher_ref[d, c, :, at].astype(F32) for c in range(8)])
            model = apply_gains(gain(d * 8, at), coher, gain(d * 8, at_q))
            return [sub(x, y) for x, y in zip(acc, model)]

        zeros = jnp.zeros((coher_ref.shape[2], 128), F32)
        acc = lax.fori_loop(0, owned, add_model, [(zeros, zeros)] * 4)
        for c in range(8):
            total_part = acc[c // 2][c % 2]
            lanes = [total_part[x : x + channels] for x in range(0, total_part.shape[0], channels)]
            vis = vis_ref[c, :, at]
            part_ref[c, :, at] = jnp.concatenate([jnp.where(lane == x, y + vis, y) for x, y in enumerate(lanes)], axis=0)


class RowSums:
    def __init__(self, ref, half):
        self.ref, self.half, self.row, self.waiting = ref, half, 0, []

    def put(self, *arrays):
        for array in arrays:
            rows = [array[at : at + 8] for at in range(0, array.shape[0], 8)]
            self.waiting.append(functools.reduce(lambda x, y: x + y, rows))
            if len(self.waiting) == 8:
                self.ref[self.half, self.row : self.row + 8, :] = self.merged(self.waiting)
                self.row, self.waiting = self.row + 8, []

    @staticmethod
    def merged(parts):
        row = lax.broadcasted_iota(jnp.int32, parts[0].shape, 0)
        low = (row & 4) == 0
        parts = [
            jnp.where(low, x, y) + pltpu.roll(jnp.where(low, y, x), 4, 0) for x, y in zip(parts[:4], parts[4:])
        ]
        for step in (2, 1):
            low = (row & step) == 0
            half = len(parts) // 2
            parts = [
                jnp.where(low, x + pltpu.roll(x, 8 - step, 0), y + pltpu.roll(y, step, 0))
                for x, y in zip(parts[:half], parts[half:])
            ]
        return parts[0]


def pair_list(low, high):
    return [(m, i) for i in range(low, high) for m in range(i)]


def load_coher(refs, i, at):
    [(low, ref)] = [(low, ref) for (low, high), ref in zip(GROUPS, refs) if low <= i < high]
    return as_matrix([ref[i - low, c, :, at].astype(F32) for c in range(8)])


def target_kernel(first_ref, begin_ref, *refs, low, high):
    *solved_refs, out_ref = refs
    baselines = first_ref.shape[2]
    for half in range(baselines // 128):
        at = pl.ds(half * 128, 128)
        sums = RowSums(out_ref, half)
        for i in range(low, high):
            coher = load_coher(solved_refs, i, at)
            gain_p, gain_q = [
                as_matrix([begin_ref[i * 8 + c : i * 8 + c + 1, pl.ds(end * baselines + half * 128, 128)] for c in range(8)])
                for end in (0, 1)
            ]
            model = apply_gains(gain_p, coher, gain_q)
            target = [(first_ref[2 * e, :, at] + model[e][0], first_ref[2 * e + 1, :, at] + model[e][1]) for e in range(4)]
            for u in range(4):
                for v in range(4):
                    sums.put(*mul_conj(target[u], coher[v]))


def product_kernel(*refs, low, high):
    *solved_refs, out_ref = refs
    for half in range(out_ref.shape[0]):
        at = pl.ds(half * 128, 128)
        sums = RowSums(out_ref, half)
        for i in range(low, high):
            coher = load_coher(solved_refs, i, at)
            for u, v in GRAM:
                sums.put(*mul_conj(coher[u], coher[v])[: 1 + (u != v)])
        for m, i in pair_list(low, high):
            coher, other = load_coher(solved_refs, i, at), load_coher(solved_refs, m, at)
            for u in range(4):
                for v in range(4):
                    sums.put(*mul_conj(other[u], coher[v]))


def own_kernel(first_ref, *refs):
    *solved_refs, res_ref, own_ref = refs
    channels = res_ref.shape[1]
    lane = lax.axis_index("dir")

    def select(value):
        mine = value[:channels]
        for x in range(1, value.shape[0] // channels):
            mine = jnp.where(lane == x, value[x * channels : (x + 1) * channels], mine)
        return mine

    for c in range(8):
        res_ref[c] = select(first_ref[c])
        for (low, high), solved_ref in zip(GROUPS, solved_refs):
            for i in range(low, high):
                own_ref[i, c] = select(solved_ref[i - low, c].astype(F32))


def sweep_kernel(order_ref, counts_ref, damping_ref, *refs, low, high, tiles, factor):
    last = high == SOLVED
    hots, turned, part, begin, start_ref, res_ref, own_ref = refs[:7]
    targets, refs = refs[7:9], refs[9:]
    pair, refs = refs[:2], refs[2:]
    ends, values, state, sums, m_now, k_now = refs[-6:]
    refs = refs[:-6]
    stages = [stage for stage in TARGETS if stage[1] <= low]
    earlier_moved = {m: (refs[s], m - stage[0]) for s, stage in enumerate(stages) for m in range(*stage)}
    refs = refs[len(stages) :]
    if last:
        earlier_gains = {m: (refs[s], m - stage[0]) for s, stage in enumerate(stages) for m in range(*stage)}
        start_own, gains_ref, out_ref, moved = refs[len(stages) :]
    else:
        solved_ref, moved, out_ref = refs
    chunks = hots.shape[1] // 256
    parts = start_ref.shape[1] // 8

    def rows_at(pair, row):
        stride = pair[0].shape[0] // (chunks // 2)
        return jnp.concatenate([ref[pl.ds(row, chunks // 2, stride=stride), :] for ref in pair], axis=0)

    def fetch(gain_now, only=None):
        step = min(8, chunks) if only is None else only
        for end in (0, 1):
            for first in range(0, chunks if only is None else only, step):
                at = pl.ds((end * chunks + first) * 128, step * 128)
                out = fetch_columns(gain_now, parts, hots, part, at)
                for t in range(step):
                    ends[end, (first + t) * 8 : (first + t) * 8 + 8, :] = out[:, t * 128 : t * 128 + 128]

    def gain_at(ref):
        return [as_matrix([ref[end, pl.ds(c, chunks, stride=8), :] for c in range(8)]) for end in (0, 1)]

    def load_m():
        return [[(m_now[(u * 4 + v) * 2], m_now[(u * 4 + v) * 2 + 1]) for v in range(4)] for u in range(4)]

    def load_k():
        row = 0
        gram = {}
        for u, v in GRAM:
            if u == v:
                gram[u, v] = (k_now[row], None)
                row += 1
            else:
                gram[u, v] = (k_now[row], k_now[row + 1])
                gram[v, u] = conj(gram[u, v])
                row += 2
        return gram

    def prepare(i):
        for row in range(K_ROWS):
            k_now[row] = rows_at(pair, i * K_ROWS + row)
        for w in range(4):
            value = []
            for out in range(4):
                row = (i - low) * M_ROWS + (out * 4 + w) * 2
                value.append((rows_at(targets, row), rows_at(targets, row + 1)))
            for m in range(i):
                base = SOLVED * K_ROWS + pair_list(0, SOLVED).index((m, i)) * M_ROWS
                ref, place = (moved, m - low) if m >= low else earlier_moved[m]
                for uv in range(4):
                    at = base + (uv * 4 + w) * 2
                    cross = (rows_at(pair, at), rows_at(pair, at + 1))
                    for out in range(4):
                        row = (out * 4 + uv) * 2
                        value[out] = add(value[out], mul((ref[place, row], ref[place, row + 1]), cross))
            for out in range(4):
                m_now[(out * 4 + w) * 2] = value[out][0]
                m_now[(out * 4 + w) * 2 + 1] = value[out][1]

    def hermitian(gain):
        a = gain[0][0] ** 2 + gain[0][1] ** 2 + gain[2][0] ** 2 + gain[2][1] ** 2
        d = gain[1][0] ** 2 + gain[1][1] ** 2 + gain[3][0] ** 2 + gain[3][1] ** 2
        cross = add(mul_conj(gain[1], gain[0]), mul_conj(gain[3], gain[2]))
        return a, d, cross

    def normal_terms():
        gain_p, gain_q = gain_at(ends)
        m = load_m()
        k = load_k()
        for end, gain, other in ((0, gain_q, False), (1, gain_p, True)):
            row = 0
            for r in (0, 1):
                for c in (0, 1):
                    if other:
                        terms = [mul_conj(gain[2 * a + b], m[2 * a + r][2 * b + c]) for a in (0, 1) for b in (0, 1)]
                    else:
                        terms = [mul(gain[2 * a + b], m[2 * r + a][2 * c + b]) for a in (0, 1) for b in (0, 1)]
                    value = total(terms)
                    values[end, pl.ds(row, chunks, stride=16), :] = value[0]
                    values[end, pl.ds(row + 1, chunks, stride=16), :] = value[1]
                    row += 2
            a, d, cross = hermitian(gain)
            for r, c in ((0, 0), (1, 1), (0, 1)):
                if other:
                    kk = [[k[2 * x + r, 2 * y + c] for y in (0, 1)] for x in (0, 1)]
                    kk = [[(z[0], None if z[1] is None else -z[1]) for z in line] for line in kk]
                else:
                    kk = [[k[2 * r + x, 2 * c + y] for y in (0, 1)] for x in (0, 1)]
                real = a * kk[0][0][0] + d * kk[1][1][0]
                real += cross[0] * (kk[0][1][0] + kk[1][0][0])
                minus = None
                if kk[0][1][1] is not None:
                    minus = kk[1][0][1] - kk[0][1][1]
                    real += cross[1] * minus
                values[end, pl.ds(row, chunks, stride=16), :] = real
                row += 1
                if r != c:
                    imag = cross[1] * (kk[0][1][0] - kk[1][0][0])
                    if kk[0][0][1] is not None:
                        imag += a * kk[0][0][1]
                    if kk[1][1][1] is not None:
                        imag += d * kk[1][1][1]
                    if kk[0][1][1] is not None:
                        imag += cross[0] * kk[0][1][1]
                    if kk[1][0][1] is not None:
                        imag += cross[0] * kk[1][0][1]
                    values[end, pl.ds(row, chunks, stride=16), :] = imag
                    row += 1

    def station_sums():
        rows = jnp.concatenate([values[end, at * 16 : at * 16 + 16, :] for end in (0, 1) for at in range(chunks)], axis=1)
        which = jnp.concatenate([part[...]] * 2, axis=0)
        wide = [split_rows(jnp.where(which == w, rows, jnp.zeros_like(rows))) for w in range(parts)]
        acc = jnp.dot(jnp.concatenate(wide, axis=0), turned[...], preferred_element_type=F32)
        for w in range(parts):
            sums[w * 16 : w * 16 + 16, :] = acc[w * 32 : w * 32 + 16] + acc[w * 32 + 16 : w * 32 + 32]

    def solve(damp):
        total_rows = [sums[pl.ds(c, parts, stride=16), :] for c in range(12)]
        now = [state[pl.ds(c, parts, stride=8), :] for c in range(8)]
        numer = as_matrix([total_rows[c] + damp * now[c] for c in range(8)])
        diag_a = total_rows[8] + damp
        diag_d = total_rows[9] + damp
        cross_r, cross_i = total_rows[10:]
        scale = 1.0 / (diag_a * diag_d - cross_r * cross_r - cross_i * cross_i)
        rows = []
        for r in (0, 1):
            x, y = numer[2 * r], numer[2 * r + 1]
            low = mul(y, (cross_r, -cross_i))
            high = mul(x, (cross_r, cross_i))
            rows += [x[0] * diag_d - low[0], x[1] * diag_d - low[1]]
            rows += [y[0] * diag_a - high[0], y[1] * diag_a - high[1]]
        for c in range(8):
            state[pl.ds(c, parts, stride=8), :] = rows[c] * scale

    def add_change(i):
        for tile in range(tiles):
            at = pl.ds(tile * 128, 128)
            coher = as_matrix([own_ref[i, c, :, at] for c in range(8)])
            rows = [tile * 8 + c for c in range(8)]
            one = [as_matrix([begin[i, end, row : row + 1, :] for row in rows]) for end in (0, 1)]
            two = [as_matrix([ends[end, row : row + 1, :] for row in rows]) for end in (0, 1)]
            before, now = apply_gains(one[0], coher, one[1]), apply_gains(two[0], coher, two[1])
            for e in range(4):
                change = sub(before[e], now[e])
                out_ref[2 * e, :, at] += change[0]
                out_ref[2 * e + 1, :, at] += change[1]

    out_ref[...] = res_ref[...]
    if last:
        width = start_own.shape[2]
        gains_ref[...] = start_own[...]
        for i in range(low):
            ref, place = earlier_gains[i]
            gains_ref[order_ref[i]] = ref[place, :8, :width]
    values[...] = jnp.zeros(values.shape, F32)
    for i in range(low, high):
        which = order_ref[i]
        damp = damping_ref[which].astype(F32) * factor
        state[...] = start_ref[i]
        ends[...] = begin[i]
        prepare(i)

        def one_round():
            normal_terms()
            station_sums()
            solve(damp)

        def more(r, carry):
            one_round()
            fetch(state[...])
            return carry

        lax.fori_loop(0, jnp.minimum(counts_ref[which], LM_ITERS) - 1, more, jnp.int32(0))
        one_round()
        fetch(state[...], tiles if i + 1 == SOLVED else None)
        if last:
            gains_ref[which] = state[:8, :width]
        else:
            solved_ref[i - low] = state[...]
        add_change(i)
        if i + 1 == SOLVED:
            break
        p0, q0 = gain_at(begin.at[i])
        p1, q1 = gain_at(ends)
        for a in (0, 1):
            for b in (0, 1):
                for u in (0, 1):
                    for v in (0, 1):
                        delta = sub(mul_conj(p0[2 * a + u], q0[2 * b + v]), mul_conj(p1[2 * a + u], q1[2 * b + v]))
                        row = ((2 * a + b) * 4 + 2 * u + v) * 2
                        moved[i - low, row] = delta[0]
                        moved[i - low, row + 1] = delta[1]


def exchange(block, axis, mask):
    return lax.ppermute(block, axis, [(i, i ^ mask) for i in range(lax.axis_size(axis))])


def butterfly_sums(value, axis):
    sums = [value]
    while 1 << (len(sums) - 1) < lax.axis_size(axis):
        sums.append(sums[-1] + exchange(sums[-1], axis, 1 << (len(sums) - 1)))
    return sums


def chip_blocks(block, axis, parts_out=False):
    chips = lax.axis_size(axis) // 2
    if chips <= 4:
        blocks = [block] + [exchange(block, axis, 2 * j) for j in range(1, chips)]
        return (jnp.stack(blocks), blocks[1]) if parts_out else jnp.stack(blocks)
    parts = block[None]
    while parts.shape[0] < chips:
        parts = jnp.concatenate([parts, exchange(parts, axis, 2 * parts.shape[0])], axis=0)
    return (parts, parts) if parts_out else parts


def on_device(visibilities, coherencies, gain_offsets, stations, solve_order, counts, damping):
    groups = lax.axis_size("bl")
    owned, _, channel_count, baselines = coherencies.shape
    channels = visibilities.shape[1]
    width = gain_offsets.shape[2]
    count = groups * width
    tiles = baselines // 128
    params = pltpu.CompilerParams(vmem_limit_bytes=VMEM_BYTES)

    def call(kernel, name, shapes, scalars, arrays, scratch=(), after=(), **static):
        first, skip = len(scalars) + len(arrays), len(after)

        def body(*refs):
            kernel(*refs[:first], *refs[first + skip :], **static)

        return pl.pallas_call(
            body,
            out_shape=[jax.ShapeDtypeStruct(*shape) for shape in shapes],
            in_specs=[pl.BlockSpec(memory_space=pltpu.SMEM)] * len(scalars)
            + [pl.BlockSpec(memory_space=pltpu.VMEM)] * len(arrays)
            + [pl.BlockSpec(memory_space=pl.ANY)] * skip,
            out_specs=[pl.BlockSpec(memory_space=pltpu.VMEM)] * len(shapes),
            scratch_shapes=[pltpu.VMEM(*shape) for shape in scratch],
            compiler_params=params,
            name=name,
        )(*scalars, *arrays, *after)

    per = 128 // width
    part_rows = -(-(owned + SOLVED) // per) * 8
    block = coherencies.shape[1:]
    whole = lambda shape: pl.BlockSpec(shape, lambda g, order: (0,) * len(shape))
    picked = lambda i: pl.BlockSpec((1,) + block, lambda g, order: (order[i] % owned, 0, 0, 0))
    shapes = [(part_rows + 8, 128)] + [(high - low,) + block for low, high in GROUPS]
    packed, *chosen = pl.pallas_call(
        functools.partial(prep_kernel, owned=owned, per=per),
        out_shape=[jax.ShapeDtypeStruct(shape, dtype) for shape, dtype in zip(shapes, [F32] + [BF16] * len(GROUPS))],
        grid_spec=pltpu.PrefetchScalarGridSpec(
            num_scalar_prefetch=1,
            grid=(1,),
            in_specs=[whole(stations.shape), whole(gain_offsets.shape)] + [picked(i) for i in range(SOLVED)],
            out_specs=[whole(shape) for shape in shapes],
        ),
        compiler_params=pltpu.CompilerParams(vmem_limit_bytes=MOST_VMEM_BYTES),
        name="prepare",
    )(solve_order, stations, gain_offsets, *[coherencies] * SOLVED)

    near = chip_blocks(packed, "bl")
    blocks = [near, exchange(near, "bl", 1)]
    shared = [butterfly_sums(value, "dir")[-1] for value in chosen]

    table = ((part_rows * per, count), F32)
    part, begin = call(
        model_kernel,
        "first_model",
        [((8, channel_count, baselines), F32), ((SOLVED * 8, 2 * baselines), F32)],
        [],
        blocks + [coherencies, visibilities],
        [table, ((part_rows * per, 2 * baselines), F32)],
        width=width,
    )
    chunks = groups * tiles
    hots, turned, hot_part, ends, start, start_own = call(
        lookup_kernel,
        "lookup",
        [
            ((128, 256 * chunks), BF16),
            ((256 * chunks, 128), BF16),
            ((8, 256 * chunks), jnp.int32),
            ((SOLVED, 2, chunks * 8, 128), F32),
            ((SOLVED, count // 16, 128), F32),
            (gain_offsets.shape, F32),
        ],
        [solve_order, counts, damping],
        [gain_offsets] + blocks,
        [table],
        width=width,
        owned=owned,
        tiles=tiles,
        after=[part],
    )
    partials = butterfly_sums(part, "dir")
    first = partials[-1]
    res, own = call(
        own_kernel,
        "own_channels",
        [(visibilities.shape, F32), ((SOLVED, 8, channels, baselines), F32)],
        [],
        [first, *shared],
    )
    moved, solved = [], []
    flat = lambda near: [near.reshape(-1, 128), exchange(near, "bl", 1).reshape(-1, 128)]
    rows = SOLVED * K_ROWS + len(pair_list(0, SOLVED)) * M_ROWS
    [value] = call(
        product_kernel, "products", [((tiles, rows, 128), F32)], [], shared, after=[part], low=0, high=SOLVED
    )
    kx_near = chip_blocks(value, "bl")
    for low, high in TARGETS:
        [value] = call(
            target_kernel,
            "targets",
            [((tiles, (high - low) * M_ROWS, 128), F32)],
            [],
            [first, begin] + shared,
            low=low,
            high=high,
            after=[value, hots],
        )
        near, near_x = chip_blocks(value, "bl", True)
        count_pieces = min(2, kx_near.shape[0])
        shape = (kx_near.shape[0] // count_pieces,) + kx_near.shape[1:]
        kept = call(keep_kernel, "keep", [(shape, F32)] * count_pieces, [], [kx_near], after=[value])
        crossed = jnp.concatenate([exchange(piece, "bl", 1) for piece in kept], axis=0)
        products = [kx_near.reshape(-1, 128), crossed.reshape(-1, 128)]
        targets = flat(near)
        last = high == SOLVED
        moved_shape = ((high - low, M_ROWS, chunks, 128), F32)
        outs = call(
            sweep_kernel,
            "sweep",
            [(gain_offsets.shape, F32), (visibilities.shape, F32)]
            if last
            else [((high - low, count // 16, 128), F32), moved_shape, (visibilities.shape, F32)],
            [solve_order, counts, damping],
            [hots, turned, hot_part, ends, start, res, own]
            + targets
            + products
            + moved
            + (solved + [start_own] if last else []),
            ([moved_shape] if last else [])
            + [
                ((2, chunks * 8, 128), F32),
                ((2, chunks * 16, 128), F32),
                ((count // 16, 128), F32),
                ((count // 8, 128), F32),
                ((M_ROWS, chunks, 128), F32),
                ((K_ROWS, chunks, 128), F32),
            ],
            low=low,
            high=high,
            tiles=tiles,
            factor=baselines * groups * channel_count / count,
        )
        if not last:
            solved.append(outs[0])
            moved.append(outs[1])
            res = outs[2]
    return outs[0], outs[1]


def solution(mesh):
    return jax.shard_map(
        on_device,
        mesh=mesh,
        in_specs=(
            P(None, "dir", "bl"),
            P("dir", None, None, "bl"),
            P(None, None, "bl"),
            P(None, "bl"),
            P(),
            P(),
            P(),
        ),
        out_specs=(P(None, None, "bl"), P(None, "dir", "bl")),
        check_vma=False,
    )
```

```python
import functools

import jax
import jax.numpy as jnp
from jax import lax
from jax.experimental import pallas as pl
from jax.experimental.pallas import tpu as pltpu
from jax.sharding import PartitionSpec as P

LM_ITERS = 2
SOLVED = 4
F32 = jnp.float32
BF16 = jnp.bfloat16
VMEM_BYTES = 24 * 1024 * 1024
MOST_VMEM_BYTES = 60 * 1024 * 1024
GRAM = [(u, v) for u in range(4) for v in range(u, 4)]
M_ROWS = 32
K_ROWS = 16
GROUPS = [(0, 2), (2, 4)]
TARGETS = [(0, 4)]


def mul(x, y):
    return (x[0] * y[0] - x[1] * y[1], x[0] * y[1] + x[1] * y[0])


def add(x, y):
    return (x[0] + y[0], x[1] + y[1])


def sub(x, y):
    return (x[0] - y[0], x[1] - y[1])


def conj(x):
    return (x[0], -x[1])


def total(terms):
    return functools.reduce(add, terms)


def mul_conj(x, y):
    return (x[0] * y[0] + x[1] * y[1], x[1] * y[0] - x[0] * y[1])


def matmul(left, right):
    return [add(mul(left[2 * i], right[j]), mul(left[2 * i + 1], right[2 + j])) for i in (0, 1) for j in (0, 1)]


def matmul_adj(left, right):
    return [
        add(mul_conj(left[2 * i], right[2 * j]), mul_conj(left[2 * i + 1], right[2 * j + 1]))
        for i in (0, 1)
        for j in (0, 1)
    ]


def apply_gains(gain_p, coher, gain_q):
    return matmul_adj(matmul(gain_p, coher), gain_q)


def as_matrix(parts):
    return [(parts[2 * e], parts[2 * e + 1]) for e in range(4)]


def split_rows(values):
    high = values.astype(BF16)
    low = (values - high.astype(F32)).astype(BF16)
    return jnp.concatenate([high, low], axis=0)


def one_hot(stations_p, stations_q, count):
    both = jnp.concatenate([stations_p, stations_q], axis=1)
    rows = lax.broadcasted_iota(jnp.int32, (count, both.shape[1]), 0)
    return jnp.where(rows == both, 1.0, 0.0).astype(BF16)


def pick(one_hots, values):
    count = values.shape[0]
    out = jnp.dot(split_rows(values), one_hots, preferred_element_type=F32)
    return out[:count] + out[count:]


def prep_kernel(order_ref, stations_ref, offs_ref, *refs, owned, per):
    coher_refs, out_ref, chosen_refs = refs[:SOLVED], refs[SOLVED], refs[SOLVED + 1 :]
    lane = lax.axis_index("dir")
    width = offs_ref.shape[2]
    station_rows = 2 * stations_ref.shape[1] // 128
    part_rows = out_ref.shape[0] - 8
    comp = lax.broadcasted_iota(jnp.int32, (8, width), 0)
    ident = jnp.where((comp == 0) | (comp == 6), 1.0, 0.0)
    places = [lane * owned + d for d in range(owned)] + [order_ref[i] for i in range(SOLVED)]
    blocks = [offs_ref[place] + ident for place in places]
    while len(blocks) * 8 < part_rows * per:
        blocks.append(jnp.zeros((8, width), F32))
    each = part_rows // 8
    columns = [jnp.concatenate(blocks[q * each : (q + 1) * each], axis=0) for q in range(per)]
    out_ref[:part_rows] = jnp.concatenate(columns, axis=1)
    out_ref[part_rows:] = jnp.zeros((8, 128), F32)
    for row in range(station_rows):
        end, tile = row // (station_rows // 2), row % (station_rows // 2)
        out_ref[part_rows + row : part_rows + row + 1] = stations_ref[end : end + 1, tile * 128 : tile * 128 + 128].astype(F32)
    for i in range(SOLVED):
        mine = order_ref[i] // owned == lane
        [(low, ref)] = [(low, ref) for (low, high), ref in zip(GROUPS, chosen_refs) if low <= i < high]
        ref[i - low] = jnp.where(mine, coher_refs[i][0], jnp.zeros_like(coher_refs[i][0]))


def keep_kernel(one_ref, *out_refs):
    each = one_ref.shape[0] // len(out_refs)
    for n, out_ref in enumerate(out_refs):
        out_ref[...] = one_ref[n * each : (n + 1) * each]


def fill_table(blocks, table, width):
    rows, lanes = blocks[0].shape[1:]
    groups = 2 * blocks[0].shape[0]
    part_rows = rows - 8
    per = lanes // width
    lane_of = lax.broadcasted_iota(jnp.int32, (part_rows, lanes), 1) // width
    for tile in range(groups * width // lanes):
        for q in range(per):
            tile_rows = jnp.zeros((part_rows, lanes), F32)
            for u in range(per):
                j = per * tile + u
                block = blocks[j % 2][j // 2, :part_rows]
                shift = ((u - q) * width) % lanes
                if shift:
                    block = pltpu.roll(block, shift, 1)
                tile_rows = jnp.where(lane_of == u, block, tile_rows)
            table[q * part_rows : (q + 1) * part_rows, tile * lanes : (tile + 1) * lanes] = tile_rows


def block_stations(block, tiles, base):
    part_rows = block.shape[0] - 8
    rows = block[part_rows:, :].astype(jnp.int32) ^ base
    return [jnp.concatenate([rows[end * tiles + t : end * tiles + t + 1] for t in range(tiles)], axis=1) for end in (0, 1)]


def fetch_columns(wide, parts, hots, part, at):
    count = wide.shape[0] // parts
    out = jnp.dot(split_rows(wide), hots[:, at], preferred_element_type=F32)
    out = out[: parts * count] + out[parts * count :]
    which = jnp.concatenate([part[:, at]] * (count // 8), axis=0)
    value = out[:count]
    for w in range(1, parts):
        value = jnp.where(which == w, out[w * count : w * count + count], value)
    return value


def lookup_kernel(
    order_ref, counts_ref, damping_ref, offs_ref, near_ref, far_ref, hots_ref, turned_ref, part_ref, ends_ref, start_ref,
    gains_ref, table, *, width, owned, tiles,
):
    half = near_ref.shape[0]
    chunks = 2 * half * tiles
    comp = lax.broadcasted_iota(jnp.int32, offs_ref.shape[1:], 0)
    gains_ref[...] = offs_ref[...] + jnp.where((comp == 0) | (comp == 6), 1.0, 0.0)[None]
    base = lax.axis_index("bl").astype(jnp.int32) * width
    fill_table([near_ref, far_ref], table, width)
    start = table[owned * 8 : (owned + SOLVED) * 8, :]
    parts = start.shape[1] // 128
    columns = [start[:, w * 128 : w * 128 + 128] for w in range(parts)]
    for i in range(SOLVED):
        start_ref[i] = jnp.concatenate([column[i * 8 : i * 8 + 8] for column in columns], axis=0)
    wide = jnp.concatenate(columns, axis=0)
    pairs = [block_stations(ref.at[j], tiles, base) for ref in (near_ref, far_ref) for j in range(half)]
    step = min(8, chunks)
    for end in (0, 1):
        rows = jnp.concatenate([pair[end] for pair in pairs], axis=1)
        for first in range(0, chunks, step):
            at = pl.ds((end * chunks + first) * 128, step * 128)
            here = rows[:, first * 128 : (first + step) * 128]
            index = lax.broadcasted_iota(jnp.int32, (128, step * 128), 0)
            hot = jnp.where(index == (here & 127), 1.0, 0.0)
            hots_ref[:, at] = hot.astype(BF16)
            turned_ref[at, :] = jnp.transpose(hot).astype(BF16)
            part_ref[:, at] = jnp.broadcast_to(here >> 7, (8, step * 128))
            out = fetch_columns(wide, parts, hots_ref, part_ref, at)
            for i in range(SOLVED):
                for t in range(step):
                    ends_ref[i, end, (first + t) * 8 : (first + t) * 8 + 8, :] = out[i * 8 : i * 8 + 8, t * 128 : t * 128 + 128]


def model_kernel(near_ref, far_ref, coher_ref, vis_ref, part_ref, begin_ref, table, ends, *, width):
    owned = coher_ref.shape[0]
    baselines = coher_ref.shape[3]
    channels = vis_ref.shape[1]
    lane = lax.axis_index("dir")
    base = lax.axis_index("bl").astype(jnp.int32) * width
    fill_table([near_ref, far_ref], table, width)
    rows_p, rows_q = block_stations(near_ref.at[0], baselines // 128, base)
    ends[...] = pick(one_hot(rows_p, rows_q, table.shape[1]), table[...])
    begin_ref[...] = ends[owned * 8 : (owned + SOLVED) * 8, :]

    for half in range(baselines // 128):
        at = pl.ds(half * 128, 128)
        at_q = pl.ds(baselines + half * 128, 128)

        def gain(row, where):
            block = ends[pl.ds(pl.multiple_of(row, 8), 8), where]
            return as_matrix([block[c : c + 1] for c in range(8)])

        def add_model(d, acc):
            coher = as_matrix([coher_ref[d, c, :, at].astype(F32) for c in range(8)])
            model = apply_gains(gain(d * 8, at), coher, gain(d * 8, at_q))
            return [sub(x, y) for x, y in zip(acc, model)]

        zeros = jnp.zeros((coher_ref.shape[2], 128), F32)
        acc = lax.fori_loop(0, owned, add_model, [(zeros, zeros)] * 4)
        for c in range(8):
            total_part = acc[c // 2][c % 2]
            lanes = [total_part[x : x + channels] for x in range(0, total_part.shape[0], channels)]
            vis = vis_ref[c, :, at]
            part_ref[c, :, at] = jnp.concatenate([jnp.where(lane == x, y + vis, y) for x, y in enumerate(lanes)], axis=0)


class RowSums:
    def __init__(self, ref, half, plus=None):
        self.ref, self.half, self.row, self.waiting, self.plus = ref, half, 0, [], plus

    def put(self, *arrays):
        for array in arrays:
            rows = [array[at : at + 8] for at in range(0, array.shape[0], 8)]
            self.waiting.append(functools.reduce(lambda x, y: x + y, rows))
            if len(self.waiting) == 8:
                value = self.merged(self.waiting)
                if self.plus is not None:
                    value += self.plus[self.half, self.row : self.row + 8, :]
                self.ref[self.half, self.row : self.row + 8, :] = value
                self.row, self.waiting = self.row + 8, []

    @staticmethod
    def merged(parts):
        row = lax.broadcasted_iota(jnp.int32, parts[0].shape, 0)
        low = (row & 4) == 0
        parts = [
            jnp.where(low, x, y) + pltpu.roll(jnp.where(low, y, x), 4, 0) for x, y in zip(parts[:4], parts[4:])
        ]
        for step in (2, 1):
            low = (row & step) == 0
            half = len(parts) // 2
            parts = [
                jnp.where(low, x + pltpu.roll(x, 8 - step, 0), y + pltpu.roll(y, step, 0))
                for x, y in zip(parts[:half], parts[half:])
            ]
        return parts[0]


def pair_list(low, high):
    return [(m, i) for i in range(low, high) for m in range(i)]


def load_coher(refs, i, at):
    [(low, ref)] = [(low, ref) for (low, high), ref in zip(GROUPS, refs) if low <= i < high]
    return as_matrix([ref[i - low, c, :, at].astype(F32) for c in range(8)])


def own_target_kernel(begin_ref, *refs, low, high):
    *solved_refs, out_ref = refs
    baselines = begin_ref.shape[1] // 2
    for half in range(baselines // 128):
        at = pl.ds(half * 128, 128)
        sums = RowSums(out_ref, half)
        for i in range(low, high):
            coher = load_coher(solved_refs, i, at)
            gain_p, gain_q = [
                as_matrix([begin_ref[i * 8 + c : i * 8 + c + 1, pl.ds(end * baselines + half * 128, 128)] for c in range(8)])
                for end in (0, 1)
            ]
            model = apply_gains(gain_p, coher, gain_q)
            for u in range(4):
                for v in range(4):
                    sums.put(*mul_conj(model[u], coher[v]))


def target_kernel(first_ref, plus_ref, *refs, low, high):
    *solved_refs, out_ref = refs
    for half in range(first_ref.shape[2] // 128):
        at = pl.ds(half * 128, 128)
        sums = RowSums(out_ref, half, plus_ref)
        target = [(first_ref[2 * e, :, at], first_ref[2 * e + 1, :, at]) for e in range(4)]
        for i in range(low, high):
            coher = load_coher(solved_refs, i, at)
            for u in range(4):
                for v in range(4):
                    sums.put(*mul_conj(target[u], coher[v]))


def product_kernel(*refs, low, high):
    *solved_refs, out_ref = refs
    for half in range(out_ref.shape[0]):
        at = pl.ds(half * 128, 128)
        sums = RowSums(out_ref, half)
        for i in range(low, high):
            coher = load_coher(solved_refs, i, at)
            for u, v in GRAM:
                sums.put(*mul_conj(coher[u], coher[v])[: 1 + (u != v)])
        for m, i in pair_list(low, high):
            coher, other = load_coher(solved_refs, i, at), load_coher(solved_refs, m, at)
            for u in range(4):
                for v in range(4):
                    sums.put(*mul_conj(other[u], coher[v]))


def own_kernel(first_ref, *refs):
    *solved_refs, res_ref, own_ref = refs
    channels = res_ref.shape[1]
    lane = lax.axis_index("dir")

    def select(value):
        mine = value[:channels]
        for x in range(1, value.shape[0] // channels):
            mine = jnp.where(lane == x, value[x * channels : (x + 1) * channels], mine)
        return mine

    for c in range(8):
        res_ref[c] = select(first_ref[c])
        for (low, high), solved_ref in zip(GROUPS, solved_refs):
            for i in range(low, high):
                own_ref[i, c] = select(solved_ref[i - low, c].astype(F32))


def sweep_kernel(order_ref, counts_ref, damping_ref, *refs, low, high, tiles, factor):
    last = high == SOLVED
    hots, turned, part, begin, start_ref, res_ref, own_ref = refs[:7]
    targets, refs = refs[7:9], refs[9:]
    pair, refs = refs[:2], refs[2:]
    ends, values, state, sums, m_now, k_now = refs[-6:]
    refs = refs[:-6]
    stages = [stage for stage in TARGETS if stage[1] <= low]
    earlier_moved = {m: (refs[s], m - stage[0]) for s, stage in enumerate(stages) for m in range(*stage)}
    refs = refs[len(stages) :]
    if last:
        earlier_gains = {m: (refs[s], m - stage[0]) for s, stage in enumerate(stages) for m in range(*stage)}
        start_own, gains_ref, out_ref, moved = refs[len(stages) :]
    else:
        solved_ref, moved, out_ref = refs
    chunks = hots.shape[1] // 256
    parts = start_ref.shape[1] // 8

    def rows_at(pair, row):
        stride = pair[0].shape[0] // (chunks // 2)
        return jnp.concatenate([ref[pl.ds(row, chunks // 2, stride=stride), :] for ref in pair], axis=0)

    def fetch(gain_now, only=None):
        step = min(8, chunks) if only is None else only
        for end in (0, 1):
            for first in range(0, chunks if only is None else only, step):
                at = pl.ds((end * chunks + first) * 128, step * 128)
                out = fetch_columns(gain_now, parts, hots, part, at)
                for t in range(step):
                    ends[end, (first + t) * 8 : (first + t) * 8 + 8, :] = out[:, t * 128 : t * 128 + 128]

    def gain_at(ref):
        return [as_matrix([ref[end, pl.ds(c, chunks, stride=8), :] for c in range(8)]) for end in (0, 1)]

    def load_m():
        return [[(m_now[(u * 4 + v) * 2], m_now[(u * 4 + v) * 2 + 1]) for v in range(4)] for u in range(4)]

    def load_k():
        row = 0
        gram = {}
        for u, v in GRAM:
            if u == v:
                gram[u, v] = (k_now[row], None)
                row += 1
            else:
                gram[u, v] = (k_now[row], k_now[row + 1])
                gram[v, u] = conj(gram[u, v])
                row += 2
        return gram

    def prepare(i):
        for row in range(K_ROWS):
            k_now[row] = rows_at(pair, i * K_ROWS + row)
        for w in range(4):
            value = []
            for out in range(4):
                row = (i - low) * M_ROWS + (out * 4 + w) * 2
                value.append((rows_at(targets, row), rows_at(targets, row + 1)))
            for m in range(i):
                base = SOLVED * K_ROWS + pair_list(0, SOLVED).index((m, i)) * M_ROWS
                ref, place = (moved, m - low) if m >= low else earlier_moved[m]
                for uv in range(4):
                    at = base + (uv * 4 + w) * 2
                    cross = (rows_at(pair, at), rows_at(pair, at + 1))
                    for out in range(4):
                        row = (out * 4 + uv) * 2
                        value[out] = add(value[out], mul((ref[place, row], ref[place, row + 1]), cross))
            for out in range(4):
                m_now[(out * 4 + w) * 2] = value[out][0]
                m_now[(out * 4 + w) * 2 + 1] = value[out][1]

    def hermitian(gain):
        a = gain[0][0] ** 2 + gain[0][1] ** 2 + gain[2][0] ** 2 + gain[2][1] ** 2
        d = gain[1][0] ** 2 + gain[1][1] ** 2 + gain[3][0] ** 2 + gain[3][1] ** 2
        cross = add(mul_conj(gain[1], gain[0]), mul_conj(gain[3], gain[2]))
        return a, d, cross

    def normal_terms():
        gain_p, gain_q = gain_at(ends)
        m = load_m()
        k = load_k()
        for end, gain, other in ((0, gain_q, False), (1, gain_p, True)):
            row = 0
            for r in (0, 1):
                for c in (0, 1):
                    if other:
                        terms = [mul_conj(gain[2 * a + b], m[2 * a + r][2 * b + c]) for a in (0, 1) for b in (0, 1)]
                    else:
                        terms = [mul(gain[2 * a + b], m[2 * r + a][2 * c + b]) for a in (0, 1) for b in (0, 1)]
                    value = total(terms)
                    values[end, pl.ds(row, chunks, stride=16), :] = value[0]
                    values[end, pl.ds(row + 1, chunks, stride=16), :] = value[1]
                    row += 2
            a, d, cross = hermitian(gain)
            for r, c in ((0, 0), (1, 1), (0, 1)):
                if other:
                    kk = [[k[2 * x + r, 2 * y + c] for y in (0, 1)] for x in (0, 1)]
                    kk = [[(z[0], None if z[1] is None else -z[1]) for z in line] for line in kk]
                else:
                    kk = [[k[2 * r + x, 2 * c + y] for y in (0, 1)] for x in (0, 1)]
                real = a * kk[0][0][0] + d * kk[1][1][0]
                real += cross[0] * (kk[0][1][0] + kk[1][0][0])
                minus = None
                if kk[0][1][1] is not None:
                    minus = kk[1][0][1] - kk[0][1][1]
                    real += cross[1] * minus
                values[end, pl.ds(row, chunks, stride=16), :] = real
                row += 1
                if r != c:
                    imag = cross[1] * (kk[0][1][0] - kk[1][0][0])
                    if kk[0][0][1] is not None:
                        imag += a * kk[0][0][1]
                    if kk[1][1][1] is not None:
                        imag += d * kk[1][1][1]
                    if kk[0][1][1] is not None:
                        imag += cross[0] * kk[0][1][1]
                    if kk[1][0][1] is not None:
                        imag += cross[0] * kk[1][0][1]
                    values[end, pl.ds(row, chunks, stride=16), :] = imag
                    row += 1

    def station_sums():
        rows = jnp.concatenate([values[end, at * 16 : at * 16 + 16, :] for end in (0, 1) for at in range(chunks)], axis=1)
        which = jnp.concatenate([part[...]] * 2, axis=0)
        wide = [split_rows(jnp.where(which == w, rows, jnp.zeros_like(rows))) for w in range(parts)]
        acc = jnp.dot(jnp.concatenate(wide, axis=0), turned[...], preferred_element_type=F32)
        for w in range(parts):
            sums[w * 16 : w * 16 + 16, :] = acc[w * 32 : w * 32 + 16] + acc[w * 32 + 16 : w * 32 + 32]

    def solve(damp):
        total_rows = [sums[pl.ds(c, parts, stride=16), :] for c in range(12)]
        now = [state[pl.ds(c, parts, stride=8), :] for c in range(8)]
        numer = as_matrix([total_rows[c] + damp * now[c] for c in range(8)])
        diag_a = total_rows[8] + damp
        diag_d = total_rows[9] + damp
        cross_r, cross_i = total_rows[10:]
        scale = 1.0 / (diag_a * diag_d - cross_r * cross_r - cross_i * cross_i)
        rows = []
        for r in (0, 1):
            x, y = numer[2 * r], numer[2 * r + 1]
            low = mul(y, (cross_r, -cross_i))
            high = mul(x, (cross_r, cross_i))
            rows += [x[0] * diag_d - low[0], x[1] * diag_d - low[1]]
            rows += [y[0] * diag_a - high[0], y[1] * diag_a - high[1]]
        for c in range(8):
            state[pl.ds(c, parts, stride=8), :] = rows[c] * scale

    def add_change(i):
        for tile in range(tiles):
            at = pl.ds(tile * 128, 128)
            coher = as_matrix([own_ref[i, c, :, at] for c in range(8)])
            rows = [tile * 8 + c for c in range(8)]
            one = [as_matrix([begin[i, end, row : row + 1, :] for row in rows]) for end in (0, 1)]
            two = [as_matrix([ends[end, row : row + 1, :] for row in rows]) for end in (0, 1)]
            before, now = apply_gains(one[0], coher, one[1]), apply_gains(two[0], coher, two[1])
            for e in range(4):
                change = sub(before[e], now[e])
                out_ref[2 * e, :, at] += change[0]
                out_ref[2 * e + 1, :, at] += change[1]

    out_ref[...] = res_ref[...]
    if last:
        width = start_own.shape[2]
        gains_ref[...] = start_own[...]
        for i in range(low):
            ref, place = earlier_gains[i]
            gains_ref[order_ref[i]] = ref[place, :8, :width]
    values[...] = jnp.zeros(values.shape, F32)
    for i in range(low, high):
        which = order_ref[i]
        damp = damping_ref[which].astype(F32) * factor
        state[...] = start_ref[i]
        ends[...] = begin[i]
        prepare(i)

        def one_round():
            normal_terms()
            station_sums()
            solve(damp)

        def more(r, carry):
            one_round()
            fetch(state[...])
            return carry

        lax.fori_loop(0, jnp.minimum(counts_ref[which], LM_ITERS) - 1, more, jnp.int32(0))
        one_round()
        fetch(state[...], tiles if i + 1 == SOLVED else None)
        if last:
            gains_ref[which] = state[:8, :width]
        else:
            solved_ref[i - low] = state[...]
        add_change(i)
        if i + 1 == SOLVED:
            break
        p0, q0 = gain_at(begin.at[i])
        p1, q1 = gain_at(ends)
        for a in (0, 1):
            for b in (0, 1):
                for u in (0, 1):
                    for v in (0, 1):
                        delta = sub(mul_conj(p0[2 * a + u], q0[2 * b + v]), mul_conj(p1[2 * a + u], q1[2 * b + v]))
                        row = ((2 * a + b) * 4 + 2 * u + v) * 2
                        moved[i - low, row] = delta[0]
                        moved[i - low, row + 1] = delta[1]


def exchange(block, axis, mask):
    return lax.ppermute(block, axis, [(i, i ^ mask) for i in range(lax.axis_size(axis))])


def butterfly_sums(value, axis):
    sums = [value]
    while 1 << (len(sums) - 1) < lax.axis_size(axis):
        sums.append(sums[-1] + exchange(sums[-1], axis, 1 << (len(sums) - 1)))
    return sums


def chip_blocks(block, axis, parts_out=False):
    chips = lax.axis_size(axis) // 2
    if chips <= 4:
        blocks = [block] + [exchange(block, axis, 2 * j) for j in range(1, chips)]
        return (jnp.stack(blocks), blocks[1]) if parts_out else jnp.stack(blocks)
    parts = block[None]
    while parts.shape[0] < chips:
        parts = jnp.concatenate([parts, exchange(parts, axis, 2 * parts.shape[0])], axis=0)
    return (parts, parts) if parts_out else parts


def on_device(visibilities, coherencies, gain_offsets, stations, solve_order, counts, damping):
    groups = lax.axis_size("bl")
    owned, _, channel_count, baselines = coherencies.shape
    channels = visibilities.shape[1]
    width = gain_offsets.shape[2]
    count = groups * width
    tiles = baselines // 128
    params = pltpu.CompilerParams(vmem_limit_bytes=VMEM_BYTES)

    def call(kernel, name, shapes, scalars, arrays, scratch=(), after=(), **static):
        first, skip = len(scalars) + len(arrays), len(after)

        def body(*refs):
            kernel(*refs[:first], *refs[first + skip :], **static)

        return pl.pallas_call(
            body,
            out_shape=[jax.ShapeDtypeStruct(*shape) for shape in shapes],
            in_specs=[pl.BlockSpec(memory_space=pltpu.SMEM)] * len(scalars)
            + [pl.BlockSpec(memory_space=pltpu.VMEM)] * len(arrays)
            + [pl.BlockSpec(memory_space=pl.ANY)] * skip,
            out_specs=[pl.BlockSpec(memory_space=pltpu.VMEM)] * len(shapes),
            scratch_shapes=[pltpu.VMEM(*shape) for shape in scratch],
            compiler_params=params,
            name=name,
        )(*scalars, *arrays, *after)

    per = 128 // width
    part_rows = -(-(owned + SOLVED) // per) * 8
    block = coherencies.shape[1:]
    whole = lambda shape: pl.BlockSpec(shape, lambda g, order: (0,) * len(shape))
    picked = lambda i: pl.BlockSpec((1,) + block, lambda g, order: (order[i] % owned, 0, 0, 0))
    shapes = [(part_rows + 8, 128)] + [(high - low,) + block for low, high in GROUPS]
    packed, *chosen = pl.pallas_call(
        functools.partial(prep_kernel, owned=owned, per=per),
        out_shape=[jax.ShapeDtypeStruct(shape, dtype) for shape, dtype in zip(shapes, [F32] + [BF16] * len(GROUPS))],
        grid_spec=pltpu.PrefetchScalarGridSpec(
            num_scalar_prefetch=1,
            grid=(1,),
            in_specs=[whole(stations.shape), whole(gain_offsets.shape)] + [picked(i) for i in range(SOLVED)],
            out_specs=[whole(shape) for shape in shapes],
        ),
        compiler_params=pltpu.CompilerParams(vmem_limit_bytes=MOST_VMEM_BYTES),
        name="prepare",
    )(solve_order, stations, gain_offsets, *[coherencies] * SOLVED)

    near = chip_blocks(packed, "bl")
    blocks = [near, exchange(near, "bl", 1)]
    shared = [butterfly_sums(value, "dir")[-1] for value in chosen]

    table = ((part_rows * per, count), F32)
    part, begin = call(
        model_kernel,
        "first_model",
        [((8, channel_count, baselines), F32), ((SOLVED * 8, 2 * baselines), F32)],
        [],
        blocks + [coherencies, visibilities],
        [table, ((part_rows * per, 2 * baselines), F32)],
        width=width,
    )
    chunks = groups * tiles
    hots, turned, hot_part, ends, start, start_own = call(
        lookup_kernel,
        "lookup",
        [
            ((128, 256 * chunks), BF16),
            ((256 * chunks, 128), BF16),
            ((8, 256 * chunks), jnp.int32),
            ((SOLVED, 2, chunks * 8, 128), F32),
            ((SOLVED, count // 16, 128), F32),
            (gain_offsets.shape, F32),
        ],
        [solve_order, counts, damping],
        [gain_offsets] + blocks,
        [table],
        width=width,
        owned=owned,
        tiles=tiles,
        after=[part],
    )
    partials = butterfly_sums(part, "dir")
    first = partials[-1]
    res, own = call(
        own_kernel,
        "own_channels",
        [(visibilities.shape, F32), ((SOLVED, 8, channels, baselines), F32)],
        [],
        [first, *shared],
    )
    moved, solved = [], []
    flat = lambda near: [near.reshape(-1, 128), exchange(near, "bl", 1).reshape(-1, 128)]
    rows = SOLVED * K_ROWS + len(pair_list(0, SOLVED)) * M_ROWS
    [value] = call(
        product_kernel, "products", [((tiles, rows, 128), F32)], [], shared, after=[part], low=0, high=SOLVED
    )
    kx_near = chip_blocks(value, "bl")
    for low, high in TARGETS:
        [plus] = call(
            own_target_kernel,
            "own_targets",
            [((tiles, (high - low) * M_ROWS, 128), F32)],
            [],
            [begin] + shared,
            low=low,
            high=high,
            after=[value],
        )
        [value] = call(
            target_kernel,
            "targets",
            [((tiles, (high - low) * M_ROWS, 128), F32)],
            [],
            [first, plus] + shared,
            low=low,
            high=high,
            after=[value, hots],
        )
        near, near_x = chip_blocks(value, "bl", True)
        count_pieces = min(2, kx_near.shape[0])
        shape = (kx_near.shape[0] // count_pieces,) + kx_near.shape[1:]
        kept = call(keep_kernel, "keep", [(shape, F32)] * count_pieces, [], [kx_near], after=[value])
        crossed = jnp.concatenate([exchange(piece, "bl", 1) for piece in kept], axis=0)
        products = [kx_near.reshape(-1, 128), crossed.reshape(-1, 128)]
        targets = flat(near)
        last = high == SOLVED
        moved_shape = ((high - low, M_ROWS, chunks, 128), F32)
        outs = call(
            sweep_kernel,
            "sweep",
            [(gain_offsets.shape, F32), (visibilities.shape, F32)]
            if last
            else [((high - low, count // 16, 128), F32), moved_shape, (visibilities.shape, F32)],
            [solve_order, counts, damping],
            [hots, turned, hot_part, ends, start, res, own]
            + targets
            + products
            + moved
            + (solved + [start_own] if last else []),
            ([moved_shape] if last else [])
            + [
                ((2, chunks * 8, 128), F32),
                ((2, chunks * 16, 128), F32),
                ((count // 16, 128), F32),
                ((count // 8, 128), F32),
                ((M_ROWS, chunks, 128), F32),
                ((K_ROWS, chunks, 128), F32),
            ],
            low=low,
            high=high,
            tiles=tiles,
            factor=baselines * groups * channel_count / count,
        )
        if not last:
            solved.append(outs[0])
            moved.append(outs[1])
            res = outs[2]
    return outs[0], outs[1]


def solution(mesh):
    return jax.shard_map(
        on_device,
        mesh=mesh,
        in_specs=(
            P(None, "dir", "bl"),
            P("dir", None, None, "bl"),
            P(None, None, "bl"),
            P(None, "bl"),
            P(),
            P(),
            P(),
        ),
        out_specs=(P(None, None, "bl"), P(None, "dir", "bl")),
        check_vma=False,
    )
```
